32 devices in a mesh: section: 4 (over y, core), dp: 8 (over z, x).
Axes of the slice: x: 2, y: 2, z: 4, core: 2. Of those that a mesh axis runs over, the one named last changes fastest.
Arguments:
- block_input: bfloat16 [2, 5120, 768], P(None, 'dp'), may hold values from -6 to 6
- out_cotangent: bfloat16 [2, 5120, 768], P(None, 'dp'), may hold values from -6 to 6
- segment_ids: int32 [2, 5120], P(None, 'dp'), may hold values from 0 to 2, as said below
- grid_row: int32 [2, 5120], P(None, 'dp'), may hold values from 0 to 23, as said below
- grid_col: int32 [2, 5120], P(None, 'dp'), may hold values from 0 to 23, as said below
- valid_slot: int32 [2, 5120], P(None, 'dp'), may hold values from 0 to 1, as said below
- in_master: float32 [4, 768, 3072], P('section', 'dp')
- out_master: float32 [4, 3072, 768], P('section', 'dp'), may hold values from -0.109375 to 0.109375
- in_moment: float32 [4, 768, 3072], P('section', 'dp'), may hold values from -320 to 320
- out_moment: float32 [4, 3072, 768], P('section', 'dp'), may hold values from -320 to 320
- in_average: float32 [4, 768, 3072], P('section', 'dp')
- out_average: float32 [4, 3072, 768], P('section', 'dp'), may hold values from -0.109375 to 0.109375
- small_master: float32 [4, 7, 768], P('section')
- small_moment: float32 [4, 7, 768], P('section'), may hold values from -640 to 640
- small_average: float32 [4, 7, 768], P('section')
Outputs:
- section_outputs: bfloat16 [4, 2, 5120, 768], P('section', None, 'dp')
- input_grads: bfloat16 [4, 2, 5120, 768], P('section', None, 'dp')
- in_moment_new: float32 [4, 768, 3072], P('section', 'dp')
- in_master_new: float32 [4, 768, 3072], P('section', 'dp')
- in_average_new: float32 [4, 768, 3072], P('section', 'dp')
- out_moment_new: float32 [4, 3072, 768], P('section', 'dp')
- out_master_new: float32 [4, 3072, 768], P('section', 'dp')
- out_average_new: float32 [4, 3072, 768], P('section', 'dp')
- small_moment_new: float32 [4, 7, 768], P('section')
- small_master_new: float32 [4, 7, 768], P('section')
- small_average_new: float32 [4, 7, 768], P('section')
- branch_bias_grads: float32 [4, 768], P('section')
The draws below stay inside these ranges and needn't reach their ends.
Inputs may be any that keep to these rules, and one draw needn't show every extreme that they name: `segment_ids`: each packed sequence of 640 slots holds whole images of 14, 20 or 24 patches a side, one after another; segment ids number them 0, 1, 2, ... in order; padding slots come last and carry the last image's id. `grid_row`: the patch's row in its image, row-major order; 0 on padding. `grid_col`: the patch's column in its image; 0 on padding. `valid_slot`: every sequence holds at least one image.
All inputs are finite; a program needn't handle non-finite values.
Results may differ from the reference program's by a relative error of at most 0.015.
Values may be sent and summed in bfloat16 or wider, within the bound.
No kernel may reach another device: no remote copies, remote signals or barrier semaphores. Data moves between devices by JAX's collectives and lax.ppermute only.
A program may use at most 512 MiB of HBM per device.

```python
import math
import jax
import jax.numpy as jnp
from jax import lax

D = 768
H = 12
HD = 64
FF = 3072
SEQ = 640
SMALL_SIDE = 14
MID_SIDE = 20
BIG_SIDE = 24
MB = 2
SEQS = 1
ROWS = 5120
N_SECTION = 4
N_DP = 8


def pack_layout(key):
    sequences = MB * N_DP * SEQS
    candidate_count = SEQ // (SMALL_SIDE * SMALL_SIDE) + 1
    side_table = jnp.array([SMALL_SIDE, MID_SIDE, BIG_SIDE], jnp.int32)
    image_kind = jax.random.randint(jax.random.fold_in(key, 7), (sequences, candidate_count), 0, 3)
    image_kind = image_kind.at[1].set(0)
    image_kind = image_kind.at[0, 0].set(2)
    side_len = side_table[image_kind]
    lengths = side_len * side_len

    def place(filled, length):
        accepted = filled + length <= SEQ
        return (filled + jnp.where(accepted, length, 0), (filled, accepted))
    leftover, (starts, accepted) = lax.scan(place, jnp.zeros((sequences,), jnp.int32), lengths.T)
    position = jnp.arange(SEQ, dtype=jnp.int32)
    ends = starts + lengths.T
    inside = accepted[:, :, None] & (position[None, None, :] >= starts[:, :, None]) & (position[None, None, :] < ends[:, :, None])
    image_order = jnp.cumsum(accepted.astype(jnp.int32), axis=0) - 1
    last_image = jnp.sum(accepted.astype(jnp.int32), axis=0) - 1
    covered = jnp.any(inside, axis=0)
    segment_ids = jnp.where(covered, jnp.sum(jnp.where(inside, image_order[:, :, None], 0), axis=0), last_image[:, None])
    within = jnp.sum(jnp.where(inside, position[None, None, :] - starts[:, :, None], 0), axis=0)
    side_here = jnp.maximum(jnp.sum(jnp.where(inside, side_len.T[:, :, None], 0), axis=0), 1)
    grid_row = jnp.where(covered, within // side_here, 0)
    grid_col = jnp.where(covered, within % side_here, 0)
    valid_slot = covered.astype(jnp.int32)
    shape_out = (MB, N_DP * SEQS * SEQ)
    return tuple((member.reshape(shape_out).astype(jnp.int32) for member in (segment_ids, grid_row, grid_col, valid_slot)))


def draw_segment_ids(key, part):
    return pack_layout(key)[0]


def draw_grid_row(key, part):
    return pack_layout(key)[1]


def draw_grid_col(key, part):
    return pack_layout(key)[2]


def draw_valid_slot(key, part):
    return pack_layout(key)[3]


def projection_law(key):
    full_shape = (N_SECTION, D, FF)
    base_values = jax.random.normal(key, full_shape, jnp.float32)
    section_of = lax.broadcasted_iota(jnp.int32, full_shape, 0)
    column = lax.broadcasted_iota(jnp.int32, full_shape, 2)
    boost_factor = jnp.where((section_of % 2 == 0) & (column >= 3 * D), 8.0, 1.0)
    return base_values * boost_factor * D ** (-0.5)


def draw_in_master(key, part):
    return projection_law(jax.random.fold_in(key, 1))


def draw_in_average(key, part):
    return projection_law(jax.random.fold_in(key, 2))


def small_law(key):
    full_shape = (N_SECTION, 7, D)
    row_of = lax.broadcasted_iota(jnp.int32, full_shape, 1)
    gains = jax.random.uniform(jax.random.fold_in(key, 1), full_shape, jnp.float32, 0.5, 1.5)
    offsets = 0.3 * jax.random.normal(jax.random.fold_in(key, 2), full_shape, jnp.float32)
    frequency = jax.random.uniform(jax.random.fold_in(key, 3), full_shape, jnp.float32, -1.0, 1.0)
    return jnp.where(row_of == 0, gains, jnp.where(row_of == 6, frequency, offsets))


def draw_small_master(key, part):
    return small_law(jax.random.fold_in(key, 3))


def draw_small_average(key, part):
    return small_law(jax.random.fold_in(key, 4))


def level_of(rng, extent, pieces, low, top_value):
    def one(dim, parts):
        draws = jax.random.uniform(jax.random.fold_in(jax.random.fold_in(rng, 6), dim), (parts,), jnp.float32, low / len(pieces), top_value / len(pieces))
        return jnp.repeat(jnp.exp(draws), extent[dim] // parts).reshape((-1,) + (1,) * (len(extent) - dim - 1))

    level = one(*pieces[0])
    for cut in pieces[1:]:
        level = level * one(*cut)
    return level


def centred(stream_key, extent, width, most, split=(), kind=jnp.bfloat16):
    values = jax.random.normal(stream_key, extent, jnp.float32) * width
    if len(split) > 0:
        values = level_of(stream_key, extent, split, -0.22, 0.18) * values
    return jnp.clip(values, min=-most, max=most).astype(kind)


def setup_inputs(seed: int = 0) -> dict:
    key_of = jax.random.split(jax.random.key(seed), 16)
    return {
        "block_input": centred(key_of[0], (MB, ROWS, D), 1.0, 6.0, ((1, 8),)),
        "out_cotangent": centred(key_of[1], (MB, ROWS, D), 1.0, 6.0, ((1, 8),)),
        "segment_ids": draw_segment_ids(jax.random.fold_in(key_of[15], 71), 0),
        "grid_row": draw_grid_row(jax.random.fold_in(key_of[15], 71), 0),
        "grid_col": draw_grid_col(jax.random.fold_in(key_of[15], 71), 0),
        "valid_slot": draw_valid_slot(jax.random.fold_in(key_of[15], 71), 0),
        "in_master": draw_in_master(jax.random.fold_in(key_of[15], 71), 0),
        "out_master": centred(key_of[7], (N_SECTION, FF, D), FF ** -0.5, 0.109375, ((0, 4), (1, 8)), jnp.float32),
        "in_moment": centred(key_of[8], (N_SECTION, D, FF), (0.5 * (N_DP * MB * SEQS * SEQ) ** 0.5), 320.0, ((0, 4), (1, 8)), jnp.float32),
        "out_moment": centred(key_of[9], (N_SECTION, FF, D), (0.5 * (N_DP * MB * SEQS * SEQ) ** 0.5), 320.0, ((0, 4), (1, 8)), jnp.float32),
        "in_average": draw_in_average(jax.random.fold_in(key_of[15], 71), 0),
        "out_average": centred(key_of[11], (N_SECTION, FF, D), FF ** -0.5, 0.109375, ((0, 4), (1, 8)), jnp.float32),
        "small_master": draw_small_master(jax.random.fold_in(key_of[15], 71), 0),
        "small_moment": centred(key_of[13], (N_SECTION, 7, D), ((N_DP * MB * SEQS * SEQ) ** 0.5), 640.0, ((0, 4),), jnp.float32),
        "small_average": draw_small_average(jax.random.fold_in(key_of[15], 71), 0),
    }


@jax.custom_vjp
def low(v):
    return lax.optimization_barrier(v.astype(jnp.bfloat16)).astype(jnp.float32)

@jax.custom_vjp
def low_back(v):
    return v

def low_keep(v):
    return (low(v), None)

def low_pass(kept, grad):
    return (grad,)

def back_keep(v):
    return (v, None)

def back_low(kept, grad):
    return (low(grad),)
low.defvjp(low_keep, low_pass)
low_back.defvjp(back_keep, back_low)
NORM_EPS = 1e-06
MOMENTUM = 0.9
DECAY = 0.0001
AVERAGE = 0.8
RATE = 0.03
MASKED = -1e+30

def matmul(left_side, right_side):
    return jnp.dot(left_side, right_side, precision=lax.Precision.HIGHEST, preferred_element_type=jnp.float32)

def layer_norm(stream, norm_gain, norm_shift):
    row_mean = lax.optimization_barrier(jnp.mean(stream, axis=-1, keepdims=True))
    centered = stream - row_mean
    spread = lax.optimization_barrier(jnp.mean(centered * centered, axis=-1, keepdims=True))
    return centered * lax.rsqrt(spread + NORM_EPS) * norm_gain + norm_shift

def rotate(vectors, cosine, sine_part):
    half_width = vectors.shape[-1] // 2
    first_half = vectors[..., :half_width]
    second_half = vectors[..., half_width:]
    return jnp.concatenate([first_half * cosine - second_half * sine_part, first_half * sine_part + second_half * cosine], axis=-1)

def attention_section(stream, weight_in, small_params, segment_ids, grid_row, grid_col, valid_slot):
    length = stream.shape[0]
    lowered = low(layer_norm(stream, small_params[0], small_params[1]))
    bias_rows = small_params[2:6].reshape(-1)
    projected = low_back(matmul(lowered, weight_in[:, :3 * D]) + bias_rows[:3 * D])
    queries = projected[:, :D].reshape(length, H, HD)
    keys_plain = projected[:, D:2 * D].reshape(length, H, HD)
    values = low(projected[:, 2 * D:].reshape(length, H, HD))
    frequency = small_params[6].reshape(H, 2, HD // 2)
    angles = grid_col.astype(jnp.float32)[:, None, None] * frequency[None, :, 0] + grid_row.astype(jnp.float32)[:, None, None] * frequency[None, :, 1]
    cosine = jnp.cos(angles)
    sine_part = jnp.sin(angles)
    query_rot = low(rotate(queries, cosine, sine_part))
    key_rot = low(rotate(keys_plain, cosine, sine_part))
    scores = low_back(jnp.einsum('qhd,khd->hqk', query_rot, key_rot, precision=lax.Precision.HIGHEST) * HD ** (-0.5))
    allowed = (segment_ids[:, None] == segment_ids[None, :]) & (valid_slot[None, :] > 0)
    scores = jnp.where(allowed[None], scores, MASKED)
    attend_weights = low(jax.nn.softmax(scores, axis=-1))
    mixture = low_back(jnp.einsum('hqk,khd->qhd', attend_weights, values, precision=lax.Precision.HIGHEST))
    mixture = low(mixture.reshape(length, D))
    branch = low_back(matmul(mixture, weight_in[:, 3 * D:]) + bias_rows[3 * D:])
    return stream + branch

def mlp_section(stream, weight_in, weight_out, small_params):
    lowered = low(layer_norm(stream, small_params[0], small_params[1]))
    gate_pre = low_back(matmul(lowered, weight_in) + small_params[2:6].reshape(-1))
    activation = low(jax.nn.gelu(gate_pre, approximate=False))
    branch = low_back(matmul(activation, weight_out) + small_params[6])
    return stream + branch

def run_sequence(weights_in, weights_out, small_params, inputs, deltas, segment_ids, grid_row, grid_col, valid_slot):
    stream = low_back(inputs + deltas[0])
    produced = []
    for section_index in range(N_SECTION):
        if section_index % 2 == 0:
            result = attention_section(stream, weights_in[section_index], small_params[section_index], segment_ids, grid_row, grid_col, valid_slot)
        else:
            result = mlp_section(stream, weights_in[section_index], weights_out[section_index], small_params[section_index])
        produced.append(result)
        if section_index + 1 < N_SECTION:
            stream = low_back(low(result) + deltas[section_index + 1])
    return (result, jnp.stack(produced))

def advance(master, moment, average, gradient, step_rate):
    gradient = gradient + DECAY * master
    moment = MOMENTUM * moment + gradient
    master = master - step_rate * (gradient + MOMENTUM * moment)
    average = AVERAGE * average + (1 - AVERAGE) * master
    return (moment, master, average)

def reference(block_input, out_cotangent, segment_ids, grid_row, grid_col, valid_slot, in_master, out_master, in_moment, out_moment, in_average, out_average, small_master, small_moment, small_average):
    sequences = MB * N_DP * SEQS
    inputs = block_input.astype(jnp.float32).reshape(sequences, SEQ, D)
    layout = tuple((member.reshape(sequences, SEQ) for member in (segment_ids, grid_row, grid_col, valid_slot)))
    deltas = jnp.zeros((sequences, N_SECTION, SEQ, D), jnp.float32)

    def forward(in_weights, out_weights, small_params, inputs, deltas):
        weights_in = low(in_weights)
        weights_out = low(out_weights)

        def one_sequence(sequence_item):
            return run_sequence(weights_in, weights_out, small_params, *sequence_item)
        return lax.map(jax.checkpoint(one_sequence), (inputs, deltas) + layout)
    final_rows, pullback, sectioned = jax.vjp(forward, in_master, out_master, small_master, inputs, deltas, has_aux=True)
    masked_cotangent = (out_cotangent.astype(jnp.float32) * valid_slot.astype(jnp.float32)[..., None]).reshape(sequences, SEQ, D)
    grad_in, grad_out, grad_small, grad_inputs, grad_deltas = pullback(masked_cotangent)

    def arrange(per_sequence):
        shaped = per_sequence.reshape(MB, N_DP * SEQS, N_SECTION, SEQ, D)
        return jnp.transpose(shaped, (2, 0, 1, 3, 4)).reshape(N_SECTION, MB, N_DP * SEQS * SEQ, D).astype(jnp.bfloat16)
    section_outputs = arrange(sectioned)
    input_grads = arrange(grad_deltas)
    branch_bias_grads = jnp.stack([grad_small[section_index, 5] if section_index % 2 == 0 else grad_small[section_index, 6] for section_index in range(N_SECTION)])
    step_rate = RATE / math.sqrt(N_DP * MB * SEQS * SEQ)
    in_moment_new, in_master_new, in_average_new = advance(in_master, in_moment, in_average, grad_in, step_rate)
    out_moment_new, out_master_new, out_average_new = advance(out_master, out_moment, out_average, grad_out, step_rate)
    small_moment_new, small_master_new, small_average_new = advance(small_master, small_moment, small_average, grad_small, step_rate)
    return (section_outputs, input_grads, in_moment_new, in_master_new, in_average_new, out_moment_new, out_master_new, out_average_new, small_moment_new, small_master_new, small_average_new, branch_bias_grads)
```

```python
import functools
import math

import jax
import jax.numpy as jnp
from jax import lax
from jax.experimental import pallas as pl
from jax.experimental.pallas import tpu as pltpu
from jax.sharding import PartitionSpec as P

F32 = jnp.float32
BF16 = jnp.bfloat16
HD = 64
NORM_EPS = 1e-06
SQRT_HALF = 0.7071067811865476
INV_ROOT_TAU = 0.3989422804014327
LOG2E = 1.4426950408889634
VMEM_LIMIT = 56 * 1024 * 1024


def dot(lhs, rhs):
    return jnp.dot(lhs, rhs, preferred_element_type=F32)


def dot_t(lhs, rhs):
    return lax.dot_general(lhs, rhs, (((1,), (1,)), ((), ())), preferred_element_type=F32)


def tdot(lhs, rhs):
    return lax.dot_general(lhs, rhs, (((0,), (0,)), ((), ())), preferred_element_type=F32)


def normalize(stream):
    mean = jnp.mean(stream, axis=-1, keepdims=True)
    centered = stream - mean
    inverse = lax.rsqrt(jnp.mean(centered * centered, axis=-1, keepdims=True) + NORM_EPS)
    return centered * inverse, inverse


def lane_index(width):
    return lax.broadcasted_iota(jnp.int32, (1, width), 1)


def swap_halves(value):
    width = value.shape[1]
    first = (lane_index(width) % HD) < HD // 2
    return jnp.where(
        first, pltpu.roll(value, width - HD // 2, 1), pltpu.roll(value, HD // 2, 1)
    )


def attn_fwd_kernel(
    save, x_ref, small_ref, wq_ref, wk_ref, wv_ref, wo_ref, cos_ref, sin_ref, qe_ref, ke_ref, bq_ref, bk_ref, bv_ref, y_ref, *rest
):
    if save:
        q_out, k_out, v_out, e_out, linv_out, o_out, u_s, acc = rest
    else:
        u_s, acc = rest
    step = pl.program_id(0)
    last = pl.num_programs(0) - 1

    @pl.when(step == 0)
    def _():
        stream = x_ref[...].astype(F32)
        normed, _ = normalize(stream)
        u_s[...] = (normed * small_ref[0:1] + small_ref[1:2]).astype(BF16)
        acc[...] = stream + small_ref[5:6]

    lowered = u_s[...]
    cosine, sine = cos_ref[...], sin_ref[...]

    def turn(value):
        return (value * cosine + swap_halves(value) * sine).astype(BF16)

    q = turn(dot(lowered, wq_ref[...]) + bq_ref[...])
    k = turn(dot(lowered, wk_ref[...]) + bk_ref[...])
    v = (dot(lowered, wv_ref[...]) + bv_ref[...]).astype(BF16)
    if save:
        q_out[...] = q
        k_out[...] = k
        v_out[...] = v
    low_lane = lane_index(2 * HD) < HD
    scale = HD ** (-0.5) * LOG2E
    qe, ke = qe_ref[...], ke_ref[...]
    for pair in range(q.shape[1] // (2 * HD)):
        lanes = slice(pair * 2 * HD, (pair + 1) * 2 * HD)
        qp, kp, vp = q[:, lanes], k[:, lanes], v[:, lanes]
        qcat = jnp.concatenate([qp, qe], axis=1)
        sums = []
        for half in range(2):
            mine = low_lane if half == 0 else jnp.logical_not(low_lane)
            kcat = jnp.concatenate([jnp.where(mine, kp, jnp.zeros_like(kp)), ke], axis=1)
            scores = dot_t(qcat, kcat)
            top = jnp.max(scores, axis=-1, keepdims=True)
            e = jnp.exp2((scores - top) * scale).astype(BF16)
            if save:
                e_out[pair * 2 + half] = e
            sums.append(dot(e, jnp.where(mine, vp, jnp.ones_like(vp))))
        value = jnp.where(low_lane, sums[0], sums[1])
        total = pltpu.roll(jnp.where(low_lane, sums[1], sums[0]), HD, 1)
        inverse = 1.0 / total
        o = value * inverse
        if save:
            linv_out[:, lanes] = inverse
            o_out[:, lanes] = o
        acc[...] += dot(o.astype(BF16), wo_ref[lanes, :])

    @pl.when(step == last)
    def _():
        y_ref[...] = acc[...].astype(BF16)


def attn_fwd(save, x, small, w, cos, sin, qe, ke):
    rows, width = x.shape
    group = 4 * HD
    steps = width // group
    whole = pl.BlockSpec((rows, width), lambda g: (0, 0))
    part = pl.BlockSpec((rows, group), lambda g: (0, g))
    enc = pl.BlockSpec((rows, 128), lambda g: (0, 0))

    def wcol(base):
        return pl.BlockSpec(
            (None, width, group), lambda g, base=base: (base // 2, 0, base % 2 * steps + g)
        )

    def bias(row):
        return pl.BlockSpec((1, group), lambda g, row=row: (0, row * steps + g))

    flat = small[2:6].reshape(1, 4 * width)
    heads = width // HD
    out_shape = [jax.ShapeDtypeStruct((rows, width), BF16)]
    out_specs = [whole]
    if save:
        out_shape += [jax.ShapeDtypeStruct((rows, width), BF16)] * 3
        out_shape += [jax.ShapeDtypeStruct((heads, rows, rows), BF16)]
        out_shape += [jax.ShapeDtypeStruct((rows, width), F32)] * 2
        out_specs += [part] * 3 + [pl.BlockSpec((4, rows, rows), lambda g: (g, 0, 0))] + [part] * 2
    return pl.pallas_call(
        functools.partial(attn_fwd_kernel, save),
        grid=(steps,),
        in_specs=[
            whole,
            pl.BlockSpec((7, width), lambda g: (0, 0)),
            wcol(0), wcol(1), wcol(2),
            pl.BlockSpec((None, group, width), lambda g: (1, g, 1)),
            part, part, enc, enc,
            bias(0), bias(1), bias(2),
        ],
        out_specs=out_specs,
        out_shape=out_shape,
        scratch_shapes=[pltpu.VMEM((rows, width), BF16), pltpu.VMEM((rows, width), F32)],
        compiler_params=pltpu.CompilerParams(vmem_limit_bytes=VMEM_LIMIT),
        cost_estimate=pl.CostEstimate(
            flops=2 * rows * width * 4 * width + 4 * 4 * rows * rows * width,
            bytes_accessed=8 * width * width + 4 * rows * width,
            transcendentals=heads * rows * rows,
        ),
        name="attn_fwd",
    )(x, small, w, w, w, w, cos, sin, qe, ke, flat, flat, flat)


def mlp_fwd_kernel(save, x_ref, small_ref, bias_ref, wi_ref, wo_ref, y_ref, *rest):
    if save:
        z_out, slope_out, u_s, acc = rest
    else:
        u_s, acc = rest
    step = pl.program_id(0)

    @pl.when(step == 0)
    def _():
        stream = x_ref[...].astype(F32)
        normed, _ = normalize(stream)
        u_s[...] = (normed * small_ref[0:1] + small_ref[1:2]).astype(BF16)
        acc[...] = stream + small_ref[6:7]

    a = dot(u_s[...], wi_ref[...]) + bias_ref[...]
    phi = 0.5 + 0.5 * lax.erf(a * SQRT_HALF)
    z = (a * phi).astype(BF16)
    if save:
        z_out[...] = z
        slope_out[...] = (phi + a * jnp.exp2(a * a * (-0.5 * LOG2E)) * INV_ROOT_TAU).astype(BF16)
    acc[...] += dot(z, wo_ref[...])

    @pl.when(step == pl.num_programs(0) - 1)
    def _():
        y_ref[...] = acc[...].astype(BF16)


def mlp_fwd(save, x, small, wi, wo, tile=512):
    rows, width = x.shape
    hidden = 2 * wi.shape[2]
    steps = hidden // tile
    whole = pl.BlockSpec((rows, width), lambda g: (0, 0))
    part = pl.BlockSpec((rows, tile), lambda g: (0, g))
    out_shape = [jax.ShapeDtypeStruct((rows, width), BF16)]
    out_specs = [whole]
    if save:
        out_shape += [jax.ShapeDtypeStruct((rows, hidden), BF16)] * 2
        out_specs += [part] * 2
    return pl.pallas_call(
        functools.partial(mlp_fwd_kernel, save),
        grid=(steps,),
        in_specs=[
            whole,
            pl.BlockSpec((7, width), lambda g: (0, 0)),
            pl.BlockSpec((1, tile), lambda g: (0, g)),
            pl.BlockSpec((None, width, tile), lambda g: (g // (steps // 2), 0, g % (steps // 2))),
            pl.BlockSpec((tile, width), lambda g: (g, 0)),
        ],
        out_specs=out_specs,
        out_shape=out_shape,
        scratch_shapes=[pltpu.VMEM((rows, width), BF16), pltpu.VMEM((rows, width), F32)],
        compiler_params=pltpu.CompilerParams(vmem_limit_bytes=VMEM_LIMIT),
        cost_estimate=pl.CostEstimate(
            flops=4 * rows * width * hidden,
            bytes_accessed=4 * width * hidden + 4 * rows * width,
            transcendentals=2 * rows * hidden,
        ),
        name="mlp_fwd",
    )(x, small, small[2:6].reshape(1, hidden), wi, wo)


def norm_back(full, x_ref, gy_ref, small_ref, du, gx_ref, rows_ref):
    normed, inverse = normalize(x_ref[...].astype(F32))
    scaled = du * small_ref[0:1]
    inner = (
        scaled
        - jnp.mean(scaled, axis=-1, keepdims=True)
        - normed * jnp.mean(scaled * normed, axis=-1, keepdims=True)
    )
    gy = gy_ref[...].astype(F32)
    gx_ref[...] = (gy + inverse * inner).astype(BF16)
    if full:
        rows_ref[0:1] = jnp.sum(du * normed, axis=0, keepdims=True)
        rows_ref[1:2] = jnp.sum(du, axis=0, keepdims=True)
        rows_ref[2:3] = jnp.sum(gy, axis=0, keepdims=True)


def mlp_bwd_kernel(full, x_ref, gy_ref, small_ref, wi_ref, wo_ref, z_ref, slope_ref, gx_ref, *rest):
    if full:
        rows_ref, bias_ref, dwi_ref, dwo_ref, du_s, ut_s = rest
    else:
        rows_ref = None
        (du_s,) = rest
    step = pl.program_id(0)

    @pl.when(step == 0)
    def _():
        du_s[...] = jnp.zeros_like(du_s)
        if full:
            normed, _ = normalize(x_ref[...].astype(F32))
            lowered = (normed * small_ref[0:1] + small_ref[1:2]).astype(BF16)
            ut_s[...] = lowered.T

    gy = gy_ref[...]
    dz = dot_t(gy, wo_ref[...])
    da = (dz * slope_ref[...].astype(F32)).astype(BF16)
    du_s[...] += dot_t(da, wi_ref[...])
    if full:
        bias_ref[...] = jnp.sum(da.astype(F32), axis=0, keepdims=True)
        dwi_ref[...] = dot(ut_s[...], da).astype(BF16)
        dwo_ref[...] = tdot(z_ref[...], gy).astype(BF16)

    @pl.when(step == pl.num_programs(0) - 1)
    def _():
        norm_back(full, x_ref, gy_ref, small_ref, du_s[...], gx_ref, rows_ref)


def mlp_bwd(full, x, gy, small, wi, wo, z, slope, tile=512):
    rows, width = x.shape
    hidden = 2 * wi.shape[2]
    steps = hidden // tile
    whole = pl.BlockSpec((rows, width), lambda g: (0, 0))
    part = pl.BlockSpec((rows, tile), lambda g: (0, g))
    wi_spec = pl.BlockSpec((None, width, tile), lambda g: (g // (steps // 2), 0, g % (steps // 2)))
    dwi_spec = pl.BlockSpec((width, tile), lambda g: (0, g))
    wo_spec = pl.BlockSpec((tile, width), lambda g: (g, 0))
    out_shape = [jax.ShapeDtypeStruct((rows, width), BF16)]
    out_specs = [whole]
    scratch = [pltpu.VMEM((rows, width), F32)]
    if full:
        out_shape += [
            jax.ShapeDtypeStruct((8, width), F32),
            jax.ShapeDtypeStruct((1, hidden), F32),
            jax.ShapeDtypeStruct((width, hidden), BF16),
            jax.ShapeDtypeStruct((hidden, width), BF16),
        ]
        out_specs += [
            pl.BlockSpec((8, width), lambda g: (0, 0)),
            pl.BlockSpec((1, tile), lambda g: (0, g)),
            dwi_spec,
            wo_spec,
        ]
        scratch += [pltpu.VMEM((width, rows), BF16)]
    return pl.pallas_call(
        functools.partial(mlp_bwd_kernel, full),
        grid=(steps,),
        in_specs=[whole, whole, pl.BlockSpec((7, width), lambda g: (0, 0)), wi_spec, wo_spec, part, part],
        out_specs=out_specs,
        out_shape=out_shape,
        scratch_shapes=scratch,
        compiler_params=pltpu.CompilerParams(vmem_limit_bytes=VMEM_LIMIT),
        cost_estimate=pl.CostEstimate(
            flops=(8 if full else 4) * rows * width * hidden,
            bytes_accessed=(8 if full else 4) * width * hidden + 6 * rows * width + 4 * rows * hidden,
            transcendentals=0,
        ),
        name="mlp_bwd_full" if full else "mlp_bwd_act",
    )(x, gy, small, wi, wo, z, slope)


def attn_bwd_kernel(
    full, x_ref, gy_ref, small_ref, wq_ref, wk_ref, wv_ref, wo_ref, cos_ref, sin_ref,
    q_ref, k_ref, v_ref, e_ref, linv_ref, o_ref, grid_ref, gx_ref, *rest
):
    if full:
        rows_ref, bias_ref, angle_ref, dwq_ref, dwk_ref, dwv_ref, dwo_ref, du_s, ut_s = rest
    else:
        rows_ref = None
        (du_s,) = rest
    step = pl.program_id(0)

    @pl.when(step == 0)
    def _():
        du_s[...] = jnp.zeros_like(du_s)
        if full:
            normed, _ = normalize(x_ref[...].astype(F32))
            lowered = (normed * small_ref[0:1] + small_ref[1:2]).astype(BF16)
            ut_s[...] = lowered.T

    gy = gy_ref[...]
    width = q_ref.shape[1]
    scale = HD ** (-0.5)
    low_lane = lane_index(2 * HD) < HD
    do_all = dot_t(gy, wo_ref[...])
    o_all = o_ref[...]
    if full:
        dwo_ref[...] = tdot(o_all.astype(BF16), gy).astype(BF16)
    dos_all = (do_all * linv_ref[...]).astype(BF16)
    parts = []
    for pair in range(width // (2 * HD)):
        lanes = slice(pair * 2 * HD, (pair + 1) * 2 * HD)
        qp, kp, vp = q_ref[:, lanes], k_ref[:, lanes], v_ref[:, lanes]
        dos = dos_all[:, lanes]
        product = dos.astype(F32) * o_all[:, lanes]
        zero = jnp.zeros_like(qp)
        dq = dk = dv = 0.0
        for half in range(2):
            mine = low_lane if half == 0 else jnp.logical_not(low_lane)
            offset = jnp.sum(jnp.where(mine, product, 0.0), axis=-1, keepdims=True)
            dos_h = jnp.where(mine, dos, zero)
            e = e_ref[pair * 2 + half]
            dp = dot_t(dos_h, vp)
            ds = (e.astype(F32) * (dp - offset)).astype(BF16)
            dv = dv + tdot(e, dos_h)
            dq = dq + dot(ds, jnp.where(mine, kp, zero))
            dk = dk + tdot(ds, jnp.where(mine, qp, zero))
        parts.append((dq * scale, dk * scale, dv))
    dqr = jnp.concatenate([p[0] for p in parts], axis=1)
    dkr = jnp.concatenate([p[1] for p in parts], axis=1)
    dv = jnp.concatenate([p[2] for p in parts], axis=1).astype(BF16)
    cosine, sine = cos_ref[...], sin_ref[...]
    dq = (dqr * cosine - swap_halves(dqr) * sine).astype(BF16)
    dk = (dkr * cosine - swap_halves(dkr) * sine).astype(BF16)
    du_s[...] += dot_t(dq, wq_ref[...]) + dot_t(dk, wk_ref[...]) + dot_t(dv, wv_ref[...])
    if full:
        turned = dqr * swap_halves(q_ref[...].astype(F32)) + dkr * swap_halves(k_ref[...].astype(F32))
        angle_ref[0:1] = jnp.sum(turned * grid_ref[:, 0:1], axis=0, keepdims=True)
        angle_ref[1:2] = jnp.sum(turned * grid_ref[:, 1:2], axis=0, keepdims=True)
        bias_ref[0:1] = jnp.sum(dq.astype(F32), axis=0, keepdims=True)
        bias_ref[1:2] = jnp.sum(dk.astype(F32), axis=0, keepdims=True)
        bias_ref[2:3] = jnp.sum(dv.astype(F32), axis=0, keepdims=True)
        ut = ut_s[...]
        dwq_ref[...] = dot(ut, dq).astype(BF16)
        dwk_ref[...] = dot(ut, dk).astype(BF16)
        dwv_ref[...] = dot(ut, dv).astype(BF16)

    @pl.when(step == pl.num_programs(0) - 1)
    def _():
        norm_back(full, x_ref, gy_ref, small_ref, du_s[...], gx_ref, rows_ref)


def attn_bwd(full, x, gy, small, w, cos, sin, saved, grid_pos):
    rows, width = x.shape
    group = 4 * HD
    steps = width // group
    heads = width // HD
    whole = pl.BlockSpec((rows, width), lambda g: (0, 0))
    part = pl.BlockSpec((rows, group), lambda g: (0, g))

    def wcol(base):
        return pl.BlockSpec(
            (None, width, group), lambda g, base=base: (base // 2, 0, base % 2 * steps + g)
        )

    strip = pl.BlockSpec((8, group), lambda g: (0, g))
    out_shape = [jax.ShapeDtypeStruct((rows, width), BF16)]
    out_specs = [whole]
    scratch = [pltpu.VMEM((rows, width), F32)]
    if full:
        out_shape += [jax.ShapeDtypeStruct((8, width), F32)] * 3
        out_shape += [jax.ShapeDtypeStruct((width, width), BF16)] * 4
        out_specs += [pl.BlockSpec((8, width), lambda g: (0, 0)), strip, strip]
        out_specs += [pl.BlockSpec((width, group), lambda g: (0, g))] * 3
        out_specs += [pl.BlockSpec((group, width), lambda g: (g, 0))]
        scratch += [pltpu.VMEM((width, rows), BF16)]
    q, k, v, e, linv, o = saved
    return pl.pallas_call(
        functools.partial(attn_bwd_kernel, full),
        grid=(steps,),
        in_specs=[
            whole, whole,
            pl.BlockSpec((7, width), lambda g: (0, 0)),
            wcol(0), wcol(1), wcol(2),
            pl.BlockSpec((None, group, width), lambda g: (1, g, 1)),
            part, part, part, part, part,
            pl.BlockSpec((4, rows, rows), lambda g: (g, 0, 0)),
            part, part,
            pl.BlockSpec((rows, 128), lambda g: (0, 0)),
        ],
        out_specs=out_specs,
        out_shape=out_shape,
        scratch_shapes=scratch,
        compiler_params=pltpu.CompilerParams(vmem_limit_bytes=VMEM_LIMIT),
        cost_estimate=pl.CostEstimate(
            flops=(4 if full else 2) * rows * width * 4 * width + 16 * 4 * rows * rows * width,
            bytes_accessed=(16 if full else 8) * width * width + 30 * rows * width + 2 * heads * rows * rows,
            transcendentals=0,
        ),
        name="attn_bwd_full" if full else "attn_bwd_act",
    )(x, gy, small, w, w, w, w, cos, sin, q, k, v, e, linv, o, grid_pos)


NEXT_LAYER = ((0, 2), (1, 3))
PREV_LAYER = ((2, 0), (3, 1))
SIBLING = ((0, 1), (1, 0), (2, 3), (3, 2))
FROM_MLP = ((1, 0), (3, 2))
FROM_ATTN = ((0, 1), (2, 3))
MOMENTUM = 0.9
DECAY = 0.0001
AVERAGE = 0.8
RATE = 0.03
MASKED = -1e30


def sibling(value):
    return lax.ppermute(value, "section", SIBLING)


class Ring:
    def __init__(self, size):
        self.size = size
        self.order = list(range(0, size, 2)) + list(range(size - 1 - size % 2, 0, -2))
        place = [0] * size
        for at, member in enumerate(self.order):
            place[member] = at
        self.order_table = jnp.array(self.order, jnp.int32)
        self.at = jnp.array(place, jnp.int32)[lax.axis_index("dp")]
        self.right = [(self.order[i], self.order[(i + 1) % size]) for i in range(size)]
        self.left = [(b, a) for a, b in self.right]

    def member(self, offset):
        return self.order_table[(self.at + offset + 2 * self.size) % self.size]

    def to_right(self, value):
        return lax.ppermute(value, "dp", self.right)

    def to_left(self, value):
        return lax.ppermute(value, "dp", self.left)


def gather_parts(ring, shard):
    parts = [(shard, 0, None)]
    reach = ring.size // 2
    rightward = leftward = shard
    for step in range(1, reach):
        rightward = ring.to_right(rightward)
        leftward = ring.to_left(leftward)
        parts += [(rightward, -step, None), (leftward, step, None)]
    middle = shard.shape[-1] // 2
    parts.append((ring.to_right(rightward[..., :middle]), -reach, 0))
    parts.append((ring.to_left(leftward[..., middle:]), reach, 1))
    return parts


def place_kernel(layout, count, place_ref, *refs):
    sources, target, semaphores = refs[:count], refs[count], refs[count + 1]
    copies = []
    for number, (source, (side, part)) in enumerate(zip(sources, layout)):
        spot = place_ref[number]
        half = place_ref[count + side]
        if target.shape[1] == 2:
            place = target.at[spot, half]
        else:
            place = target.at[half, spot]
        if part is not None:
            length = source.shape[-1]
            place = place.at[:, pl.ds(part * length, length)]
        copies.append(pltpu.make_async_copy(source, place, semaphores.at[number]))
    for copy in copies:
        copy.start()
    for copy in copies:
        copy.wait()


def gather_weight(ring, core, shard, spot_first):
    mine = gather_parts(ring, shard)
    arrays, layout, places = [], [], []
    for value, offset, part in mine:
        for side, held in ((0, value), (1, sibling(value))):
            arrays.append(held)
            layout.append((side, part))
            places.append(ring.member(offset))
    count = len(arrays)
    table = jnp.stack(places + [core, 1 - core]).astype(jnp.int32)
    rows, columns = shard.shape
    if spot_first:
        shape = (ring.size, 2, rows, columns)
    else:
        shape = (2, ring.size, rows, columns)
    fitted = pl.pallas_call(
        functools.partial(place_kernel, tuple(layout), count),
        in_specs=[pl.BlockSpec(memory_space=pltpu.SMEM)] + [pl.BlockSpec(memory_space=pl.ANY)] * count,
        out_specs=pl.BlockSpec(memory_space=pl.ANY),
        out_shape=jax.ShapeDtypeStruct(shape, shard.dtype),
        scratch_shapes=[pltpu.SemaphoreType.DMA((count,))],
        cost_estimate=pl.CostEstimate(
            flops=0, bytes_accessed=8 * ring.size * rows * columns, transcendentals=0
        ),
        name="place_weight",
    )(table, *arrays)
    if spot_first:
        return fitted.reshape(2 * ring.size * rows, columns)
    return fitted.reshape(2, ring.size * rows, columns)


def reduce_over_ring(ring, chunks):
    reach = ring.size // 2

    def own(offset):
        return lax.dynamic_index_in_dim(chunks, ring.member(offset), 0, keepdims=False)

    middle = chunks.shape[-1] // 2
    far = own(reach)
    rightward = ring.to_right(far[..., :middle])
    leftward = ring.to_left(far[..., middle:])
    for step in range(1, reach):
        term_r, term_l = own(reach - step), own(step - reach)
        if step == 1:
            rightward = jnp.concatenate([term_r[..., :middle] + rightward, term_r[..., middle:]], axis=-1)
            leftward = jnp.concatenate([term_l[..., :middle], term_l[..., middle:] + leftward], axis=-1)
        else:
            rightward, leftward = term_r + rightward, term_l + leftward
        rightward, leftward = ring.to_right(rightward), ring.to_left(leftward)
    return own(0).astype(F32) + rightward.astype(F32) + leftward.astype(F32)


def sum_over_dp(value):
    size = lax.axis_size("dp")
    bit = 1
    while bit < size:
        value = value + lax.ppermute(value, "dp", [(i, i ^ bit) for i in range(size)])
        bit *= 2
    return value


def advance(master, moment, average, gradient, step_rate):
    gradient = gradient + DECAY * master
    moment = MOMENTUM * moment + gradient
    master = master - step_rate * (gradient + MOMENTUM * moment)
    average = AVERAGE * average + (1 - AVERAGE) * master
    return (moment, master, average)


def on_device(
    block_input, out_cotangent, segment_ids, grid_row, grid_col, valid_slot,
    in_master, out_master, in_moment, out_moment, in_average, out_average,
    small_master, small_moment, small_average,
):
    section_index = lax.axis_index("section")
    layer, core = section_index // 2, section_index % 2
    first_core = core == 0
    first_layer = layer == 0
    micro_count, row_count, width = block_input.shape
    ring = Ring(lax.axis_size("dp"))

    def mine(source):
        return lax.dynamic_index_in_dim(source, core, 0, keepdims=False)

    def by_core(if_first, if_second):
        return jnp.where(first_core, if_first, if_second)

    in_low = in_master[0].astype(BF16)
    out_low = out_master[0].astype(BF16)
    in_rows, hidden = in_low.shape
    out_rows = out_low.shape[0]
    in_half, out_half = hidden // 2, out_rows // 2
    crossed = sibling(by_core(in_low[:, in_half:], in_low[:, :in_half]))
    attn_shard = by_core(in_low[:, :in_half], crossed)
    up_shard = by_core(crossed, in_low[:, in_half:])
    down_shard = by_core(lax.ppermute(out_low[:out_half], "section", FROM_MLP), out_low[out_half:])
    small_own = small_master[0]
    small_other = sibling(small_own)
    small_attn = by_core(small_own, small_other)
    small_mlp = by_core(small_other, small_own)
    w_attn = gather_weight(ring, core, attn_shard, False)
    w_up = gather_weight(ring, core, up_shard, False)
    w_down = gather_weight(ring, core, down_shard, True)

    seg, row_at, col_at, valid = (mine(m) for m in (segment_ids, grid_row, grid_col, valid_slot))
    head_count = width // HD
    frequency = small_attn[6].reshape(head_count, 2, 1, HD // 2)
    spread = jnp.broadcast_to(frequency, (head_count, 2, 2, HD // 2))
    angle = (
        col_at.astype(F32)[:, None] * spread[:, 0].reshape(1, width)
        + row_at.astype(F32)[:, None] * spread[:, 1].reshape(1, width)
    )
    turn_sign = jnp.where(lax.broadcasted_iota(jnp.int32, (1, width), 1) % HD < HD // 2, -1.0, 1.0)
    cosine = jnp.cos(angle)
    sine = jnp.sin(angle) * turn_sign
    tag = lax.broadcasted_iota(jnp.int32, (1, 128), 1)
    same = seg[:, None] == tag
    query_tag = same.astype(BF16)
    key_tag = jnp.where(same & (valid[:, None] > 0), 0.0, MASKED).astype(BF16)
    lane = lax.broadcasted_iota(jnp.int32, (1, 128), 1)
    grid_pos = jnp.where(lane == 0, col_at.astype(F32)[:, None], row_at.astype(F32)[:, None])
    x0 = mine(block_input)
    cotangent = mine(out_cotangent) * valid.astype(BF16)[:, None]

    (mid0,) = attn_fwd(False, x0, small_attn, w_attn, cosine, sine, query_tag, key_tag)
    (top0,) = mlp_fwd(False, mid0, small_mlp, w_up, w_down)
    entering = jnp.where(first_layer, x0, lax.ppermute(top0, "section", NEXT_LAYER))

    mid, *saved = attn_fwd(True, entering, small_attn, w_attn, cosine, sine, query_tag, key_tag)
    top, z, slope = mlp_fwd(True, mid, small_mlp, w_up, w_down)

    (back_mid,) = mlp_bwd(False, mid, cotangent, small_mlp, w_up, w_down, z, slope)
    (back_in,) = attn_bwd(False, entering, back_mid, small_attn, w_attn, cosine, sine, saved, grid_pos)
    arriving = jnp.where(first_layer, lax.ppermute(back_in, "section", PREV_LAYER), cotangent)

    grad_mid, mlp_rows, up_bias, d_up, d_down = mlp_bwd(
        True, mid, arriving, small_mlp, w_up, w_down, z, slope
    )
    kept_up = by_core(d_up[:, :in_half], d_up[:, in_half:])
    sent_up = by_core(d_up[:, in_half:], d_up[:, :in_half])
    up_sum = kept_up + sibling(sent_up)
    up_share = reduce_over_ring(ring, up_sum.reshape(ring.size, in_rows, in_half))
    d_down = d_down.reshape(ring.size, 2, out_half, width)
    kept_down = by_core(d_down[:, 0], d_down[:, 1])
    sent_down = by_core(d_down[:, 1], d_down[:, 0])
    down_sum = kept_down + sibling(sent_down)
    down_share = reduce_over_ring(ring, down_sum)

    grad_in, attn_rows, attn_bias, turned, d_q, d_k, d_v, d_o = attn_bwd(
        True, entering, grad_mid, small_attn, w_attn, cosine, sine, saved, grid_pos
    )
    first_sum = by_core(d_q, d_v) + sibling(by_core(d_v, d_q))
    second_sum = by_core(d_k, d_o) + sibling(by_core(d_o, d_k))
    first_share = reduce_over_ring(ring, first_sum.reshape(ring.size, in_rows, width))
    second_share = reduce_over_ring(ring, second_sum.reshape(ring.size, in_rows, width))
    attn_share = jnp.concatenate([first_share, second_share], axis=1)

    turned = turned[:2].reshape(2, head_count, 2, HD // 2)
    grad_frequency = jnp.transpose(turned[:, :, 1] - turned[:, :, 0], (1, 0, 2)).reshape(1, width)
    attn_small = jnp.concatenate([attn_rows[:2], attn_bias[:3], attn_rows[2:3], grad_frequency], axis=0)
    mlp_small = jnp.concatenate([mlp_rows[:2], up_bias.reshape(4, width), mlp_rows[2:3]], axis=0)
    small_grad = sum_over_dp(by_core(attn_small, mlp_small) + sibling(by_core(mlp_small, attn_small)))

    crossed = sibling(by_core(up_share, attn_share).astype(BF16)).astype(F32)
    share_in = jnp.concatenate([by_core(attn_share, crossed), by_core(crossed, up_share)], axis=1)
    crossed = lax.ppermute(down_share.astype(BF16), "section", FROM_ATTN).astype(F32)
    share_out = jnp.where(first_core, 0.0, jnp.concatenate([crossed, down_share], axis=0))

    step_rate = RATE / math.sqrt(lax.axis_size("dp") * micro_count * row_count)
    in_new = advance(in_master[0], in_moment[0], in_average[0], share_in, step_rate)
    out_new = advance(out_master[0], out_moment[0], out_average[0], share_out, step_rate)
    small_new = advance(small_own, small_moment[0], small_average[0], small_grad, step_rate)
    branch_bias = by_core(small_grad[5], small_grad[6])

    def both_micro(attn_value, mlp_value):
        kept = by_core(attn_value, mlp_value)
        crossed = sibling(by_core(mlp_value, attn_value))
        return jnp.stack([by_core(kept, crossed), by_core(crossed, kept)])

    outputs = both_micro(mid, top)
    input_grads = both_micro(grad_in, grad_mid)
    return tuple(
        value[None]
        for value in (outputs, input_grads, *in_new, *out_new, *small_new, branch_bias)
    )


def solution(mesh):
    rows = P(None, "dp", None)
    slots = P(None, "dp")
    matrix = P("section", "dp", None)
    vectors = P("section", None, None)
    return jax.shard_map(
        on_device,
        mesh=mesh,
        in_specs=(rows,) * 2 + (slots,) * 4 + (matrix,) * 6 + (vectors,) * 3,
        out_specs=(P("section", None, "dp", None),) * 2 + (matrix,) * 6 + (vectors,) * 3 + (P("section", None),),
        check_vma=False,
    )
```

```python
import functools
import math

import jax
import jax.numpy as jnp
from jax import lax
from jax.experimental import pallas as pl
from jax.experimental.pallas import tpu as pltpu
from jax.sharding import PartitionSpec as P

F32 = jnp.float32
BF16 = jnp.bfloat16
HD = 64
NORM_EPS = 1e-06
SQRT_HALF = 0.7071067811865476
INV_ROOT_TAU = 0.3989422804014327
LOG2E = 1.4426950408889634
VMEM_LIMIT = 56 * 1024 * 1024


def dot(lhs, rhs):
    return jnp.dot(lhs, rhs, preferred_element_type=F32)


def dot_t(lhs, rhs):
    return lax.dot_general(lhs, rhs, (((1,), (1,)), ((), ())), preferred_element_type=F32)


def tdot(lhs, rhs):
    return lax.dot_general(lhs, rhs, (((0,), (0,)), ((), ())), preferred_element_type=F32)


def normalize(stream):
    mean = jnp.mean(stream, axis=-1, keepdims=True)
    centered = stream - mean
    inverse = lax.rsqrt(jnp.mean(centered * centered, axis=-1, keepdims=True) + NORM_EPS)
    return centered * inverse, inverse


def lane_index(width):
    return lax.broadcasted_iota(jnp.int32, (1, width), 1)


def swap_halves(value):
    width = value.shape[1]
    first = (lane_index(width) % HD) < HD // 2
    return jnp.where(
        first, pltpu.roll(value, width - HD // 2, 1), pltpu.roll(value, HD // 2, 1)
    )


def attn_fwd_kernel(
    save, x_ref, small_ref, wq_ref, wk_ref, wv_ref, wo_ref, cos_ref, sin_ref, qe_ref, ke_ref, bq_ref, bk_ref, bv_ref, y_ref, *rest
):
    if save:
        q_out, k_out, v_out, e_out, linv_out, o_out, u_s, acc = rest
    else:
        u_s, acc = rest
    step = pl.program_id(0)
    last = pl.num_programs(0) - 1

    @pl.when(step == 0)
    def _():
        stream = x_ref[...].astype(F32)
        normed, _ = normalize(stream)
        u_s[...] = (normed * small_ref[0:1] + small_ref[1:2]).astype(BF16)
        acc[...] = stream + small_ref[5:6]

    lowered = u_s[...]
    cosine, sine = cos_ref[...], sin_ref[...]

    def turn(value):
        return (value * cosine + swap_halves(value) * sine).astype(BF16)

    q = turn(dot(lowered, wq_ref[...]) + bq_ref[...])
    k = turn(dot(lowered, wk_ref[...]) + bk_ref[...])
    v = (dot(lowered, wv_ref[...]) + bv_ref[...]).astype(BF16)
    if save:
        q_out[...] = q
        k_out[...] = k
        v_out[...] = v
    low_lane = lane_index(2 * HD) < HD
    scale = HD ** (-0.5) * LOG2E
    qe, ke = qe_ref[...], ke_ref[...]
    for pair in range(q.shape[1] // (2 * HD)):
        lanes = slice(pair * 2 * HD, (pair + 1) * 2 * HD)
        qp, kp, vp = q[:, lanes], k[:, lanes], v[:, lanes]
        qcat = jnp.concatenate([qp, qe], axis=1)
        sums = []
        for half in range(2):
            mine = low_lane if half == 0 else jnp.logical_not(low_lane)
            kcat = jnp.concatenate([jnp.where(mine, kp, jnp.zeros_like(kp)), ke], axis=1)
            scores = dot_t(qcat, kcat)
            top = jnp.max(scores, axis=-1, keepdims=True)
            e = jnp.exp2((scores - top) * scale).astype(BF16)
            if save:
                e_out[pair * 2 + half] = e
            sums.append(dot(e, jnp.where(mine, vp, jnp.ones_like(vp))))
        value = jnp.where(low_lane, sums[0], sums[1])
        total = pltpu.roll(jnp.where(low_lane, sums[1], sums[0]), HD, 1)
        inverse = 1.0 / total
        o = value * inverse
        if save:
            linv_out[:, lanes] = inverse
            o_out[:, lanes] = o
        acc[...] += dot(o.astype(BF16), wo_ref[lanes, :])

    @pl.when(step == last)
    def _():
        y_ref[...] = acc[...].astype(BF16)


def attn_fwd(save, x, small, w, cos, sin, qe, ke):
    rows, width = x.shape
    group = 4 * HD
    steps = width // group
    whole = pl.BlockSpec((rows, width), lambda g: (0, 0))
    part = pl.BlockSpec((rows, group), lambda g: (0, g))
    enc = pl.BlockSpec((rows, 128), lambda g: (0, 0))

    def wcol(base):
        return pl.BlockSpec((None, width, group), lambda g, base=base: (base, 0, g))

    def bias(row):
        return pl.BlockSpec((1, group), lambda g, row=row: (0, row * steps + g))

    flat = small[2:6].reshape(1, 4 * width)
    heads = width // HD
    out_shape = [jax.ShapeDtypeStruct((rows, width), BF16)]
    out_specs = [whole]
    if save:
        out_shape += [jax.ShapeDtypeStruct((rows, width), BF16)] * 3
        out_shape += [jax.ShapeDtypeStruct((heads, rows, rows), BF16)]
        out_shape += [jax.ShapeDtypeStruct((rows, width), F32)] * 2
        out_specs += [part] * 3 + [pl.BlockSpec((4, rows, rows), lambda g: (g, 0, 0))] + [part] * 2
    return pl.pallas_call(
        functools.partial(attn_fwd_kernel, save),
        grid=(steps,),
        in_specs=[
            whole,
            pl.BlockSpec((7, width), lambda g: (0, 0)),
            wcol(0), wcol(1), wcol(2),
            pl.BlockSpec((None, group, width), lambda g: (3, g, 0)),
            part, part, enc, enc,
            bias(0), bias(1), bias(2),
        ],
        out_specs=out_specs,
        out_shape=out_shape,
        scratch_shapes=[pltpu.VMEM((rows, width), BF16), pltpu.VMEM((rows, width), F32)],
        compiler_params=pltpu.CompilerParams(vmem_limit_bytes=VMEM_LIMIT),
        cost_estimate=pl.CostEstimate(
            flops=2 * rows * width * 4 * width + 4 * 4 * rows * rows * width,
            bytes_accessed=8 * width * width + 4 * rows * width,
            transcendentals=heads * rows * rows,
        ),
        name="attn_fwd",
    )(x, small, w, w, w, w, cos, sin, qe, ke, flat, flat, flat)


def mlp_fwd_kernel(save, x_ref, small_ref, bias_ref, wi_ref, wo_ref, y_ref, *rest):
    if save:
        z_out, slope_out, u_s, acc = rest
    else:
        u_s, acc = rest
    step = pl.program_id(0)

    @pl.when(step == 0)
    def _():
        stream = x_ref[...].astype(F32)
        normed, _ = normalize(stream)
        u_s[...] = (normed * small_ref[0:1] + small_ref[1:2]).astype(BF16)
        acc[...] = stream + small_ref[6:7]

    a = dot(u_s[...], wi_ref[...]) + bias_ref[...]
    phi = 0.5 + 0.5 * lax.erf(a * SQRT_HALF)
    z = (a * phi).astype(BF16)
    if save:
        z_out[...] = z
        slope_out[...] = (phi + a * jnp.exp2(a * a * (-0.5 * LOG2E)) * INV_ROOT_TAU).astype(BF16)
    acc[...] += dot(z, wo_ref[...])

    @pl.when(step == pl.num_programs(0) - 1)
    def _():
        y_ref[...] = acc[...].astype(BF16)


def mlp_fwd(save, x, small, wi, wo, tile=768):
    rows, width = x.shape
    hidden = wi.shape[0] * wi.shape[2]
    per_block = width // tile
    steps = hidden // tile
    whole = pl.BlockSpec((rows, width), lambda g: (0, 0))
    part = pl.BlockSpec((rows, tile), lambda g: (0, g))
    out_shape = [jax.ShapeDtypeStruct((rows, width), BF16)]
    out_specs = [whole]
    if save:
        out_shape += [jax.ShapeDtypeStruct((rows, hidden), BF16)] * 2
        out_specs += [part] * 2
    return pl.pallas_call(
        functools.partial(mlp_fwd_kernel, save),
        grid=(steps,),
        in_specs=[
            whole,
            pl.BlockSpec((7, width), lambda g: (0, 0)),
            pl.BlockSpec((1, tile), lambda g: (0, g)),
            pl.BlockSpec((None, width, tile), lambda g: (g // per_block, 0, g % per_block)),
            pl.BlockSpec((tile, width), lambda g: (g, 0)),
        ],
        out_specs=out_specs,
        out_shape=out_shape,
        scratch_shapes=[pltpu.VMEM((rows, width), BF16), pltpu.VMEM((rows, width), F32)],
        compiler_params=pltpu.CompilerParams(vmem_limit_bytes=VMEM_LIMIT),
        cost_estimate=pl.CostEstimate(
            flops=4 * rows * width * hidden,
            bytes_accessed=4 * width * hidden + 4 * rows * width,
            transcendentals=2 * rows * hidden,
        ),
        name="mlp_fwd",
    )(x, small, small[2:6].reshape(1, hidden), wi, wo)


def norm_back(full, x_ref, gy_ref, small_ref, du, gx_ref, rows_ref):
    normed, inverse = normalize(x_ref[...].astype(F32))
    scaled = du * small_ref[0:1]
    inner = (
        scaled
        - jnp.mean(scaled, axis=-1, keepdims=True)
        - normed * jnp.mean(scaled * normed, axis=-1, keepdims=True)
    )
    gy = gy_ref[...].astype(F32)
    gx_ref[...] = (gy + inverse * inner).astype(BF16)
    if full:
        rows_ref[0:1] = jnp.sum(du * normed, axis=0, keepdims=True)
        rows_ref[1:2] = jnp.sum(du, axis=0, keepdims=True)
        rows_ref[2:3] = jnp.sum(gy, axis=0, keepdims=True)


def turn_kernel(x_ref, small_ref, mid_ref, small_mid_ref, o_ref, z_ref, ut_ref, ut_mid_ref, ot_ref, zt_ref):
    for source, small, target in ((x_ref, small_ref, ut_ref), (mid_ref, small_mid_ref, ut_mid_ref)):
        normed, _ = normalize(source[...].astype(F32))
        target[...] = (normed * small[0:1] + small[1:2]).astype(BF16).T
    ot_ref[...] = o_ref[...].astype(BF16).T
    width = x_ref.shape[1]
    for block in range(z_ref.shape[1] // width):
        zt_ref[block * width : (block + 1) * width, :] = z_ref[:, block * width : (block + 1) * width].T


def turned_factors(x, small, mid, small_mid, o, z):
    rows, width = x.shape
    vmem = pl.BlockSpec(memory_space=pltpu.VMEM)
    return pl.pallas_call(
        turn_kernel,
        in_specs=[vmem] * 6,
        out_specs=[vmem] * 4,
        out_shape=[jax.ShapeDtypeStruct((width, rows), BF16)] * 3
        + [jax.ShapeDtypeStruct((z.shape[1], rows), BF16)],
        compiler_params=pltpu.CompilerParams(vmem_limit_bytes=VMEM_LIMIT),
        cost_estimate=pl.CostEstimate(
            flops=40 * rows * width, bytes_accessed=40 * rows * width, transcendentals=0
        ),
        name="turned_factors",
    )(x, small, mid, small_mid, o, z)


def mlp_bwd_kernel(
    full, core_ref, x_ref, gy_ref, small_ref, wi_ref, wo_ref, slope_ref, *rest
):
    if full:
        ut_ref, zt_ref, gx_ref, rows_ref, bias_ref, up_kept, up_sent, down_kept, down_sent, du_s = rest
    else:
        gx_ref, du_s = rest
        rows_ref = None
    step = pl.program_id(0)

    @pl.when(step == 0)
    def _():
        du_s[...] = jnp.zeros_like(du_s)

    gy = gy_ref[...]
    dz = dot_t(gy, wo_ref[...])
    da = (dz * slope_ref[...].astype(F32)).astype(BF16)
    du_s[...] += dot_t(da, wi_ref[...])
    if full:
        first_core = core_ref[0] == 0
        bias_ref[...] = jnp.sum(da.astype(F32), axis=0, keepdims=True)
        members, share = up_kept.shape[1:3]
        d_up = dot(ut_ref[...], da).reshape(members, share, da.shape[1]).astype(BF16)

        @pl.when(step < pl.num_programs(0) // 2)
        def _():
            up_sent[0] = d_up

        @pl.when(step >= pl.num_programs(0) // 2)
        def _():
            up_kept[0] = d_up

        d_down = dot(zt_ref[...], gy)
        for member in range(down_kept.shape[0]):
            for block in range(2):
                low = (member * 4 + block) * share
                one = d_down[low : low + share]
                two = d_down[low + 2 * share : low + 3 * share]
                down_kept[member, block] = jnp.where(first_core, one, two).astype(BF16)
                down_sent[member, block] = jnp.where(first_core, two, one).astype(BF16)

    @pl.when(step == pl.num_programs(0) - 1)
    def _():
        norm_back(full, x_ref, gy_ref, small_ref, du_s[...], gx_ref, rows_ref)


def mlp_bwd(full, core, x, gy, small, wi, wo, slope, ut=None, zt=None, members=None):
    rows, width = x.shape
    blocks = wi.shape[0]
    hidden = blocks * width
    half = blocks // 2

    def block_of(g, core_ref):
        return jnp.where(g < half, (1 - core_ref[0]) * half + g, core_ref[0] * half + g - half)

    whole = pl.BlockSpec((rows, width), lambda g, c: (0, 0))
    part = pl.BlockSpec((rows, width), lambda g, c: (0, block_of(g, c)))
    in_specs = [
        whole, whole,
        pl.BlockSpec((7, width), lambda g, c: (0, 0)),
        pl.BlockSpec((None, width, width), lambda g, c: (block_of(g, c), 0, 0)),
        pl.BlockSpec((width, width), lambda g, c: (block_of(g, c), 0)),
        part,
    ]
    operands = [x, gy, small, wi, wo, slope]
    out_shape = [jax.ShapeDtypeStruct((rows, width), BF16)]
    out_specs = [whole]
    if full:
        share = width // members
        operands += [ut, zt]
        in_specs += [
            pl.BlockSpec((width, rows), lambda g, c: (0, 0)),
            pl.BlockSpec((width, rows), lambda g, c: (block_of(g, c), 0)),
        ]
        out_shape += [
            jax.ShapeDtypeStruct((8, width), F32),
            jax.ShapeDtypeStruct((1, hidden), F32),
        ]
        out_shape += [jax.ShapeDtypeStruct((2, members, share, width), BF16)] * 2
        out_shape += [jax.ShapeDtypeStruct((members, 2, share, width), BF16)] * 2
        up_block = (1, members, share, width)
        down = pl.BlockSpec(
            (members // blocks, 2, share, width), lambda g, c: (block_of(g, c), 0, 0, 0)
        )
        out_specs += [
            pl.BlockSpec((8, width), lambda g, c: (0, 0)),
            pl.BlockSpec((1, width), lambda g, c: (0, block_of(g, c))),
            pl.BlockSpec(up_block, lambda g, c: (jnp.maximum(g - half, 0), 0, 0, 0)),
            pl.BlockSpec(up_block, lambda g, c: (jnp.minimum(g, half - 1), 0, 0, 0)),
            down, down,
        ]
    return pl.pallas_call(
        functools.partial(mlp_bwd_kernel, full),
        grid_spec=pltpu.PrefetchScalarGridSpec(
            num_scalar_prefetch=1,
            grid=(blocks,),
            in_specs=in_specs,
            out_specs=out_specs,
            scratch_shapes=[pltpu.VMEM((rows, width), F32)],
        ),
        out_shape=out_shape,
        compiler_params=pltpu.CompilerParams(vmem_limit_bytes=VMEM_LIMIT),
        cost_estimate=pl.CostEstimate(
            flops=(8 if full else 4) * rows * width * hidden,
            bytes_accessed=(8 if full else 4) * width * hidden + 6 * rows * width + 4 * rows * hidden,
            transcendentals=0,
        ),
        name="mlp_bwd_full" if full else "mlp_bwd_act",
    )(core, *operands)


def norm_kernel(x_ref, gy_ref, small_ref, du_ref, gx_ref, rows_ref):
    norm_back(True, x_ref, gy_ref, small_ref, du_ref[...], gx_ref, rows_ref)


def norm_bwd(x, gy, small, du):
    rows, width = x.shape
    vmem = pl.BlockSpec(memory_space=pltpu.VMEM)
    return pl.pallas_call(
        norm_kernel,
        in_specs=[vmem] * 4,
        out_specs=[vmem] * 2,
        out_shape=[
            jax.ShapeDtypeStruct((rows, width), BF16),
            jax.ShapeDtypeStruct((8, width), F32),
        ],
        compiler_params=pltpu.CompilerParams(vmem_limit_bytes=VMEM_LIMIT),
        cost_estimate=pl.CostEstimate(flops=30 * rows * width, bytes_accessed=10 * rows * width, transcendentals=0),
        name="norm_bwd",
    )(x, gy, small, du)


def attn_bwd_kernel(
    full, first, final, x_ref, gy_ref, small_ref, wq_ref, wk_ref, wv_ref, wo_ref, cos_ref, sin_ref,
    q_ref, k_ref, v_ref, e_ref, linv_ref, o_ref, *rest
):
    if full:
        core_ref, gy_part_ref, ut_ref, ot_ref, grid_ref = rest[:5]
        rest = rest[5:]
    if not first:
        before_ref, rest = rest[0], rest[1:]
        if full:
            rest = rest[4:]
    out_ref, rest = rest[0], rest[1:]
    rows_ref = None
    if full:
        bias_ref, angle_ref, kept_ref, sent_ref = rest[:4]
        rest = rest[4:]
        if final:
            rows_ref, rest = rest[0], rest[1:]
    (du_s,) = rest
    step = pl.program_id(0)

    @pl.when(step == 0)
    def _():
        du_s[...] = jnp.zeros_like(du_s) if first else before_ref[...]

    gy = gy_ref[...]
    width = q_ref.shape[1]
    scale = HD ** (-0.5)
    low_lane = lane_index(2 * HD) < HD
    do_all = dot_t(gy, wo_ref[...])
    o_all = o_ref[...]
    dos_all = (do_all * linv_ref[...]).astype(BF16)
    parts = []
    for pair in range(width // (2 * HD)):
        lanes = slice(pair * 2 * HD, (pair + 1) * 2 * HD)
        qp, kp, vp = q_ref[:, lanes], k_ref[:, lanes], v_ref[:, lanes]
        dos = dos_all[:, lanes]
        product = dos.astype(F32) * o_all[:, lanes]
        zero = jnp.zeros_like(qp)
        dq = dk = dv = 0.0
        for half in range(2):
            mine = low_lane if half == 0 else jnp.logical_not(low_lane)
            offset = jnp.sum(jnp.where(mine, product, 0.0), axis=-1, keepdims=True)
            dos_h = jnp.where(mine, dos, zero)
            e = e_ref[pair * 2 + half]
            dp = dot_t(dos_h, vp)
            ds = (e.astype(F32) * (dp - offset)).astype(BF16)
            dv = dv + tdot(e, dos_h)
            dq = dq + dot(ds, jnp.where(mine, kp, zero))
            dk = dk + tdot(ds, jnp.where(mine, qp, zero))
        parts.append((dq * scale, dk * scale, dv))
    dqr = jnp.concatenate([p[0] for p in parts], axis=1)
    dkr = jnp.concatenate([p[1] for p in parts], axis=1)
    dv = jnp.concatenate([p[2] for p in parts], axis=1).astype(BF16)
    cosine, sine = cos_ref[...], sin_ref[...]
    dq = (dqr * cosine - swap_halves(dqr) * sine).astype(BF16)
    dk = (dkr * cosine - swap_halves(dkr) * sine).astype(BF16)
    du_s[...] += dot_t(dq, wq_ref[...]) + dot_t(dk, wk_ref[...]) + dot_t(dv, wv_ref[...])
    if full:
        turned = dqr * swap_halves(q_ref[...].astype(F32)) + dkr * swap_halves(k_ref[...].astype(F32))
        angle_ref[0:1] = jnp.sum(turned * grid_ref[:, 0:1], axis=0, keepdims=True)
        angle_ref[1:2] = jnp.sum(turned * grid_ref[:, 1:2], axis=0, keepdims=True)
        bias_ref[0:1] = jnp.sum(dq.astype(F32), axis=0, keepdims=True)
        bias_ref[1:2] = jnp.sum(dk.astype(F32), axis=0, keepdims=True)
        bias_ref[2:3] = jnp.sum(dv.astype(F32), axis=0, keepdims=True)
        first_core = core_ref[0] == 0
        members, share = kept_ref.shape[1:3]
        ut = ut_ref[...]
        pairs = (
            (dot(ut, dq), dot(ut, dv)),
            (dot(ut, dk), dot(ot_ref[...], gy_part_ref[...])),
        )
        for block, (one, two) in enumerate(pairs):
            one = one.reshape(members, share, width)
            two = two.reshape(members, share, width)
            kept_ref[block] = jnp.where(first_core, one, two).astype(BF16)
            sent_ref[block] = jnp.where(first_core, two, one).astype(BF16)

    @pl.when(step == pl.num_programs(0) - 1)
    def _():
        if final:
            norm_back(full, x_ref, gy_ref, small_ref, du_s[...], out_ref, rows_ref)
        else:
            out_ref[...] = du_s[...]


def attn_bwd(full, x, gy, small, w, cos, sin, saved, extra=None, members=None, low=0, high=None, before=None, close=True):
    rows, width = x.shape
    group = 4 * HD
    groups = width // group
    high = groups if high is None else high
    first, final = low == 0, close and high == groups
    heads = width // HD
    whole = pl.BlockSpec((rows, width), lambda g: (0, 0))
    part = pl.BlockSpec((rows, group), lambda g: (0, low + g))

    def wcol(base):
        return pl.BlockSpec((None, width, group), lambda g, base=base: (base, 0, low + g))

    strip = pl.BlockSpec((8, group), lambda g: (0, low + g))
    out_shape = [jax.ShapeDtypeStruct((rows, width), BF16 if final else F32)]
    out_specs = [whole]
    q, k, v, e, linv, o = saved
    operands = [x, gy, small, w, w, w, w, cos, sin, q, k, v, e, linv, o]
    in_specs = [
        whole, whole,
        pl.BlockSpec((7, width), lambda g: (0, 0)),
        wcol(0), wcol(1), wcol(2),
        pl.BlockSpec((None, group, width), lambda g: (3, low + g, 0)),
        part, part, part, part, part,
        pl.BlockSpec((4, rows, rows), lambda g: (low + g, 0, 0)),
        part, part,
    ]
    if full:
        core, ut, ot, grid_pos = extra
        operands += [core, gy, ut, ot, grid_pos]
        across = pl.BlockSpec((width, rows), lambda g: (0, 0))
        in_specs += [
            pl.BlockSpec(memory_space=pltpu.SMEM), part, across, across,
            pl.BlockSpec((rows, 128), lambda g: (0, 0)),
        ]
        share = width // members
        out_shape += [jax.ShapeDtypeStruct((8, width), F32)] * 2
        out_shape += [jax.ShapeDtypeStruct((2, members, share, width), BF16)] * 2
        out_specs += [strip, strip]
        out_specs += [pl.BlockSpec((2, members, share, group), lambda g: (0, 0, 0, low + g))] * 2
        if final:
            out_shape += [jax.ShapeDtypeStruct((8, width), F32)]
            out_specs += [pl.BlockSpec((8, width), lambda g: (0, 0))]
    aliases = {}
    if not first:
        if full:
            aliases = {len(operands) + 1 + i: 1 + i for i in range(4)}
        operands += list(before[: 5 if full else 1])
        in_specs += [whole] + [pl.BlockSpec(memory_space=pl.ANY)] * (4 if full else 0)
    portion = (high - low) / groups
    return pl.pallas_call(
        functools.partial(attn_bwd_kernel, full, first, final),
        grid=(high - low,),
        in_specs=in_specs,
        out_specs=out_specs,
        out_shape=out_shape,
        scratch_shapes=[pltpu.VMEM((rows, width), F32)],
        input_output_aliases=aliases,
        compiler_params=pltpu.CompilerParams(vmem_limit_bytes=VMEM_LIMIT),
        cost_estimate=pl.CostEstimate(
            flops=int(portion * ((16 if full else 8) * rows * width * width + 64 * rows * rows * width)),
            bytes_accessed=int(portion * ((16 if full else 8) * width * width + 30 * rows * width + 2 * heads * rows * rows)),
            transcendentals=0,
        ),
        name="attn_bwd_full" if full else "attn_bwd_act",
    )(*operands)


def ring_term(refs, first_dims):
    blocks = []
    for (kept, met), first in zip(refs, first_dims):
        for block in range(2):
            at = (block, 0) if first else (0, block)
            blocks.append(kept[at].astype(F32) + met[at].astype(F32))
    return blocks


def ring_sum_kernel(kind, first_dims, members_ref, *refs):
    pairs = len(first_dims)
    sides = 2 if kind in ("second", "later") else 1
    terms = []
    for _ in range(sides):
        group = [(refs[2 * i], refs[2 * i + 1]) for i in range(pairs)]
        terms.append(ring_term(group, first_dims))
        refs = refs[2 * pairs :]
    middle = pairs
    if kind == "open":
        right_ref, left_ref = refs
        for block in range(middle):
            right_ref[block] = terms[0][block].astype(BF16)
            left_ref[block] = terms[0][middle + block].astype(BF16)
        return
    came_right, came_left = refs[:2]
    if kind == "close":
        for block, term in enumerate(terms[0]):
            refs[2][block] = term + came_right[block].astype(F32) + came_left[block].astype(F32)
        return
    for side, (came, out) in enumerate(((came_right, refs[2]), (came_left, refs[3]))):
        for block, term in enumerate(terms[side]):
            if kind == "later":
                term = term + came[block].astype(F32)
            elif (block < middle) == (side == 0):
                term = term + came[block % middle].astype(F32)
            out[block] = term.astype(BF16)


class RingSum:
    def __init__(self, ring, terms):
        self.ring, self.terms = ring, terms
        self.reach = ring.size // 2
        self.share, self.width = terms[0][0].shape[2:]
        self.done = 0
        self.going = self.call("open", (self.reach,))

    def call(self, kind, offsets, *came):
        operands, in_specs = [], []
        for offset in offsets:
            at = offset % self.ring.size
            for kept, met, first in self.terms:
                if first:
                    spec = pl.BlockSpec((2, 1, self.share, self.width), lambda g, m, at=at: (0, m[at], 0, 0))
                else:
                    spec = pl.BlockSpec((1, 2, self.share, self.width), lambda g, m, at=at: (m[at], 0, 0, 0))
                operands += [kept, met]
                in_specs += [spec, spec]
        for value in came:
            operands.append(value)
            in_specs.append(pl.BlockSpec(value.shape, lambda g, m: (0, 0, 0)))
        blocks = 2 * len(self.terms)
        full = (blocks, self.share, self.width)
        if kind == "open":
            shapes = [jax.ShapeDtypeStruct((blocks // 2,) + full[1:], BF16)] * 2
        elif kind == "close":
            shapes = [jax.ShapeDtypeStruct(full, F32)]
        else:
            shapes = [jax.ShapeDtypeStruct(full, BF16)] * 2
        return pl.pallas_call(
            functools.partial(ring_sum_kernel, kind, tuple(t[2] for t in self.terms)),
            grid_spec=pltpu.PrefetchScalarGridSpec(
                num_scalar_prefetch=1,
                grid=(1,),
                in_specs=in_specs,
                out_specs=[pl.BlockSpec(s.shape, lambda g, m: (0, 0, 0)) for s in shapes],
            ),
            out_shape=shapes,
            compiler_params=pltpu.CompilerParams(vmem_limit_bytes=VMEM_LIMIT),
            cost_estimate=pl.CostEstimate(
                flops=6 * blocks * self.share * self.width,
                bytes_accessed=16 * blocks * self.share * self.width,
                transcendentals=0,
            ),
            name="ring_sum_" + kind,
        )(self.ring.members, *operands)

    def hop(self):
        self.came = (self.ring.to_right(self.going[0]), self.ring.to_left(self.going[1]))
        self.done += 1
        return self.came

    def add(self, came):
        left = self.reach - self.done
        kind = "second" if self.done == 1 else "later"
        self.going = self.call(kind, (left, -left), *came)
        return tuple(self.going)

    def result(self):
        while True:
            came = self.hop()
            if self.done == self.reach:
                return self.call("close", (0,), *came)[0]
            self.add(came)


NEXT_LAYER = ((0, 2), (1, 3))
PREV_LAYER = ((2, 0), (3, 1))
SIBLING = ((0, 1), (1, 0), (2, 3), (3, 2))
FROM_MLP = ((1, 0), (3, 2))
FROM_ATTN = ((0, 1), (2, 3))
MOMENTUM = 0.9
DECAY = 0.0001
AVERAGE = 0.8
RATE = 0.03
MASKED = -1e30


def sibling(value):
    return lax.ppermute(value, "section", SIBLING)


class Ring:
    def __init__(self, size):
        self.size = size
        order = list(range(0, size, 2)) + list(range(size - 1 - size % 2, 0, -2))
        place = {member: at for at, member in enumerate(order)}
        table = [[order[(place[m] + k) % size] for k in range(size)] for m in range(size)]
        self.members = lax.dynamic_index_in_dim(
            jnp.array(table, jnp.int32), lax.axis_index("dp"), 0, keepdims=False
        )
        self.right = [(order[i], order[(i + 1) % size]) for i in range(size)]
        self.left = [(b, a) for a, b in self.right]

    def member(self, offset):
        return self.members[offset % self.size]

    def to_right(self, value):
        return lax.ppermute(value, "dp", self.right)

    def to_left(self, value):
        return lax.ppermute(value, "dp", self.left)


tied = lax.optimization_barrier


class RingWalk:
    def __init__(self, ring, shard):
        self.ring = ring
        self.found = [(shard, 0, 0)]
        self.going = (shard, shard)
        self.done = 0

    def hop(self):
        self.done += 1
        right, left = self.going
        if self.done < self.ring.size // 2:
            right, left = self.ring.to_right(right), self.ring.to_left(left)
            self.found += [(right, -self.done, 0), (left, self.done, 0)]
        else:
            middle = right.shape[0] // 2
            right, left = self.ring.to_right(right[:middle]), self.ring.to_left(left[middle:])
            self.found += [(right, -self.done, 0), (left, self.done, middle)]
        self.going = (right, left)

    def renew(self, right, left):
        self.going = (right, left)
        if self.done:
            self.found[-2:] = [(right,) + self.found[-2][1:], (left,) + self.found[-1][1:]]


def meet(walks, *others):
    count = 2 * len(walks)
    out = tied(tuple(value for walk in walks for value in walk.going) + others)
    for number, walk in enumerate(walks):
        walk.renew(*out[2 * number : 2 * number + 2])
    return out[count:]


def place_kernel(layout, count, down_from, core_ref, members_ref, *refs):
    sources, targets = refs[:count], refs[count:]
    core = core_ref[0]
    for source, (side, offset, first) in zip(sources, layout):
        member = members_ref[offset]
        half = core if side == 0 else 1 - core
        for block in range(source.shape[0]):
            at = first + block
            if at < down_from:
                targets[0][half * 2 + at, member] = source[block]
            else:
                targets[1][member, half * 2 + at - down_from] = source[block]


def place(ring, core, found, two):
    arrays, layout = [], []
    for value, offset, first in found:
        for side, held in ((0, value), (1, sibling(value))):
            arrays.append(held)
            layout.append((side, offset % ring.size, first))
    rows, width = arrays[0].shape[1:]
    count = len(arrays)
    shapes = [(4, ring.size, rows, width)] + ([(ring.size, 4, rows, width)] if two else [])
    smem = pl.BlockSpec(memory_space=pltpu.SMEM)
    vmem = pl.BlockSpec(memory_space=pltpu.VMEM)
    placed = pl.pallas_call(
        functools.partial(place_kernel, tuple(layout), count, 2),
        in_specs=[smem, smem] + [vmem] * count,
        out_specs=[vmem] * len(shapes),
        out_shape=[jax.ShapeDtypeStruct(shape, BF16) for shape in shapes],
        compiler_params=pltpu.CompilerParams(vmem_limit_bytes=VMEM_LIMIT),
        cost_estimate=pl.CostEstimate(
            flops=0, bytes_accessed=16 * len(shapes) * ring.size * rows * width, transcendentals=0
        ),
        name="place_weights",
    )(core, ring.members, *arrays)
    whole = [placed[0].reshape(4, ring.size * rows, width)]
    if two:
        whole.append(placed[1].reshape(4 * ring.size * rows, width))
    return whole


def sum_over_dp(value):
    size = lax.axis_size("dp")
    bit = 1
    while bit < size:
        value = value + lax.ppermute(value, "dp", [(i, i ^ bit) for i in range(size)])
        bit *= 2
    return value


def advance(master, moment, average, gradient, step_rate):
    gradient = gradient + DECAY * master
    moment = MOMENTUM * moment + gradient
    master = master - step_rate * (gradient + MOMENTUM * moment)
    average = AVERAGE * average + (1 - AVERAGE) * master
    return (moment, master, average)


def on_device(
    block_input, out_cotangent, segment_ids, grid_row, grid_col, valid_slot,
    in_master, out_master, in_moment, out_moment, in_average, out_average,
    small_master, small_moment, small_average,
):
    section_index = lax.axis_index("section")
    layer, core = section_index // 2, section_index % 2
    first_core = core == 0
    first_layer = layer == 0
    core_at = core.reshape(1)
    micro_count, row_count, width = block_input.shape
    ring = Ring(lax.axis_size("dp"))

    def mine(source):
        return jnp.where(first_core, source[0], source[1])

    def by_core(if_first, if_second):
        return jnp.where(first_core, if_first, if_second)

    in_rows, hidden = in_master.shape[1:]
    in_low = in_master[0].astype(BF16)
    in_blocks = jnp.stack([in_low[:, i * width : (i + 1) * width] for i in range(4)])
    down_blocks = out_master[0].astype(BF16).reshape(4, in_rows, width)
    crossed = sibling(by_core(in_blocks[2:], in_blocks[:2]))
    attn_shard = by_core(in_blocks[:2], crossed)
    up_shard = by_core(crossed, in_blocks[2:])
    down_shard = by_core(lax.ppermute(down_blocks[:2], "section", FROM_MLP), down_blocks[2:])
    small_own = small_master[0]
    small_other = sibling(small_own)
    small_attn = by_core(small_own, small_other)
    small_mlp = by_core(small_other, small_own)
    attn_walk = RingWalk(ring, attn_shard)
    mlp_walk = RingWalk(ring, jnp.concatenate([up_shard, down_shard]))
    reach = ring.size // 2
    for step in range(reach - 1):
        attn_walk.hop()
    meet((attn_walk, mlp_walk))
    attn_walk.hop()
    mlp_walk.hop()
    meet((attn_walk, mlp_walk))
    for step in range(1, reach - 2):
        mlp_walk.hop()

    seg, row_at, col_at, valid = (mine(m) for m in (segment_ids, grid_row, grid_col, valid_slot))
    head_count = width // HD
    frequency = small_attn[6].reshape(head_count, 2, 1, HD // 2)
    spread = jnp.broadcast_to(frequency, (head_count, 2, 2, HD // 2))
    angle = (
        col_at.astype(F32)[:, None] * spread[:, 0].reshape(1, width)
        + row_at.astype(F32)[:, None] * spread[:, 1].reshape(1, width)
    )
    turn_sign = jnp.where(lax.broadcasted_iota(jnp.int32, (1, width), 1) % HD < HD // 2, -1.0, 1.0)
    cosine = jnp.cos(angle)
    sine = jnp.sin(angle) * turn_sign
    tag = lax.broadcasted_iota(jnp.int32, (1, 128), 1)
    same = seg[:, None] == tag
    query_tag = same.astype(BF16)
    key_tag = jnp.where(same & (valid[:, None] > 0), 0.0, MASKED).astype(BF16)
    lane = lax.broadcasted_iota(jnp.int32, (1, 128), 1)
    grid_pos = jnp.where(lane == 0, col_at.astype(F32)[:, None], row_at.astype(F32)[:, None])
    x0 = mine(block_input)
    cotangent = mine(out_cotangent) * valid.astype(BF16)[:, None]

    (w_attn,) = place(ring, core_at, attn_walk.found, False)
    (mid0,) = attn_fwd(False, x0, small_attn, w_attn, cosine, sine, query_tag, key_tag)
    (mid0,) = meet((mlp_walk,), mid0)
    while mlp_walk.done < reach:
        mlp_walk.hop()
    w_up, w_down = place(ring, core_at, mlp_walk.found, True)
    (top0,) = mlp_fwd(False, mid0, small_mlp, w_up, w_down)
    entering = jnp.where(first_layer, x0, lax.ppermute(top0, "section", NEXT_LAYER))

    mid, *saved = attn_fwd(True, entering, small_attn, w_attn, cosine, sine, query_tag, key_tag)
    top, z, slope = mlp_fwd(True, mid, small_mlp, w_up, w_down)

    def both_micro(attn_value, mlp_value):
        kept = by_core(attn_value, mlp_value)
        crossed = sibling(by_core(mlp_value, attn_value))
        return jnp.stack([by_core(kept, crossed), by_core(crossed, kept)])

    (back_mid,) = mlp_bwd(False, core_at, mid, cotangent, small_mlp, w_up, w_down, slope)
    (back_in,) = attn_bwd(False, entering, back_mid, small_attn, w_attn, cosine, sine, saved)
    arriving = jnp.where(first_layer, lax.ppermute(back_in, "section", PREV_LAYER), cotangent)
    outputs = both_micro(mid, top)
    arriving, outputs = tied((arriving, outputs))
    ut_attn, ut_mlp, o_t, z_t = turned_factors(entering, small_attn, mid, small_mlp, saved[5], z)

    grad_mid, mlp_rows, up_bias, up_kept, up_sent, down_kept, down_sent = mlp_bwd(
        True, core_at, mid, arriving, small_mlp, w_up, w_down, slope, ut_mlp, z_t, ring.size
    )
    met = (sibling(up_sent), sibling(down_sent))
    extra = (core_at, ut_attn, o_t, grid_pos)

    def attn_group(group, before):
        return list(
            attn_bwd(
                True, entering, grad_mid, small_attn, w_attn, cosine, sine, saved, extra, ring.size,
                group, group + 1, before, False,
            )
        )

    back = attn_group(0, None)
    *met, back[0] = tied(met + (back[0],))
    mlp_sum = RingSum(ring, ((up_kept, met[0], True), (down_kept, met[1], False)))
    for group in range(1, width // (4 * HD)):
        *mlp_sum.going, back[0] = tied(tuple(mlp_sum.going) + (back[0],))
        back = attn_group(group, back)
        *came, back[0] = tied(tuple(mlp_sum.hop()) + (back[0],))
        mlp_sum.add(came)
    du, attn_bias, turned, attn_kept, attn_sent = back
    *mlp_sum.going, du, attn_sent = tied(tuple(mlp_sum.going) + (du, attn_sent))
    grad_in, attn_rows = norm_bwd(entering, grad_mid, small_attn, du)
    attn_sum = RingSum(ring, ((attn_kept, sibling(attn_sent), True),))
    mlp_share = mlp_sum.result()
    attn_share = attn_sum.result()
    up_share, down_share = mlp_share[:2], mlp_share[2:]

    turned = turned[:2].reshape(2, head_count, 2, HD // 2)
    grad_frequency = jnp.transpose(turned[:, :, 1] - turned[:, :, 0], (1, 0, 2)).reshape(1, width)
    attn_small = jnp.concatenate([attn_rows[:2], attn_bias[:3], attn_rows[2:3], grad_frequency], axis=0)
    mlp_small = jnp.concatenate([mlp_rows[:2], up_bias.reshape(4, width), mlp_rows[2:3]], axis=0)
    small_grad = sum_over_dp(by_core(attn_small, mlp_small) + sibling(by_core(mlp_small, attn_small)))

    crossed = sibling(by_core(up_share, attn_share).astype(BF16)).astype(F32)
    first_half, second_half = by_core(attn_share, crossed), by_core(crossed, up_share)
    share_in = jnp.concatenate([first_half[0], first_half[1], second_half[0], second_half[1]], axis=1)
    crossed = lax.ppermute(down_share.astype(BF16), "section", FROM_ATTN).astype(F32)
    share_out = jnp.where(first_core, 0.0, jnp.concatenate([crossed, down_share]).reshape(4 * in_rows, width))

    step_rate = RATE / math.sqrt(lax.axis_size("dp") * micro_count * row_count)
    in_new = advance(in_master[0], in_moment[0], in_average[0], share_in, step_rate)
    out_new = advance(out_master[0], out_moment[0], out_average[0], share_out, step_rate)
    small_new = advance(small_own, small_moment[0], small_average[0], small_grad, step_rate)
    branch_bias = by_core(small_grad[5], small_grad[6])

    input_grads = both_micro(grad_in, grad_mid)
    return tuple(
        value[None]
        for value in (outputs, input_grads, *in_new, *out_new, *small_new, branch_bias)
    )


def solution(mesh):
    rows = P(None, "dp", None)
    slots = P(None, "dp")
    matrix = P("section", "dp", None)
    vectors = P("section", None, None)
    return jax.shard_map(
        on_device,
        mesh=mesh,
        in_specs=(rows,) * 2 + (slots,) * 4 + (matrix,) * 6 + (vectors,) * 3,
        out_specs=(P("section", None, "dp", None),) * 2 + (matrix,) * 6 + (vectors,) * 3 + (P("section", None),),
        check_vma=False,
    )
```

```python
import functools
import math

import jax
import jax.numpy as jnp
from jax import lax
from jax.experimental import pallas as pl
from jax.experimental.pallas import tpu as pltpu
from jax.sharding import PartitionSpec as P

F32 = jnp.float32
BF16 = jnp.bfloat16
HD = 64
NORM_EPS = 1e-06
SQRT_HALF = 0.7071067811865476
INV_ROOT_TAU = 0.3989422804014327
LOG2E = 1.4426950408889634
BIG_VMEM = 56 * 1024 * 1024
MIDDLE_VMEM = 34 * 1024 * 1024
PIECE_VMEM = 56 * 1024 * 1024
SMALL_VMEM = 14 * 1024 * 1024
TERMS_VMEM = 32 * 1024 * 1024


def dot(lhs, rhs):
    return jnp.dot(lhs, rhs, preferred_element_type=F32)


def dot_t(lhs, rhs):
    return lax.dot_general(lhs, rhs, (((1,), (1,)), ((), ())), preferred_element_type=F32)


def tdot(lhs, rhs):
    return lax.dot_general(lhs, rhs, (((0,), (0,)), ((), ())), preferred_element_type=F32)


def normalize(stream):
    mean = jnp.mean(stream, axis=-1, keepdims=True)
    centered = stream - mean
    inverse = lax.rsqrt(jnp.mean(centered * centered, axis=-1, keepdims=True) + NORM_EPS)
    return centered * inverse, inverse


def lane_index(width):
    return lax.broadcasted_iota(jnp.int32, (1, width), 1)


def swap_halves(value):
    width = value.shape[1]
    first = (lane_index(width) % HD) < HD // 2
    return jnp.where(
        first, pltpu.roll(value, width - HD // 2, 1), pltpu.roll(value, HD // 2, 1)
    )


def attn_fwd_kernel(
    save, first, final, x_ref, small_ref, wq_ref, wk_ref, wv_ref, wo_ref, cos_ref, sin_ref, qe_ref, ke_ref, bq_ref, bk_ref, bv_ref, *rest
):
    if not first:
        before_ref, rest = rest[0], rest[1:]
    y_ref, rest = rest[0], rest[1:]
    if save:
        q_out, k_out, v_out, e_out, linv_out, o_out, u_s, acc = rest
    else:
        u_s, acc = rest
    step = pl.program_id(0)
    last = pl.num_programs(0) - 1

    @pl.when(step == 0)
    def _():
        stream = x_ref[...].astype(F32)
        normed, _ = normalize(stream)
        u_s[...] = (normed * small_ref[0:1] + small_ref[1:2]).astype(BF16)
        acc[...] = stream + small_ref[5:6] if first else before_ref[...]

    lowered = u_s[...]
    cosine, sine = cos_ref[...], sin_ref[...]

    def turn(value):
        return (value * cosine + swap_halves(value) * sine).astype(BF16)

    q = turn(dot(lowered, wq_ref[...]) + bq_ref[...])
    k = turn(dot(lowered, wk_ref[...]) + bk_ref[...])
    v = (dot(lowered, wv_ref[...]) + bv_ref[...]).astype(BF16)
    if save:
        q_out[...] = q
        k_out[...] = k
        v_out[...] = v
    low_lane = lane_index(2 * HD) < HD
    scale = HD ** (-0.5) * LOG2E
    qe, ke = qe_ref[...], ke_ref[...]
    for pair in range(q.shape[1] // (2 * HD)):
        lanes = slice(pair * 2 * HD, (pair + 1) * 2 * HD)
        qp, kp, vp = q[:, lanes], k[:, lanes], v[:, lanes]
        qcat = jnp.concatenate([qp, qe], axis=1)
        sums = []
        for half in range(2):
            mine = low_lane if half == 0 else jnp.logical_not(low_lane)
            kcat = jnp.concatenate([jnp.where(mine, kp, jnp.zeros_like(kp)), ke], axis=1)
            scores = dot_t(qcat, kcat)
            top = jnp.max(scores, axis=-1, keepdims=True)
            e = jnp.exp2((scores - top) * scale).astype(BF16)
            if save:
                e_out[pair * 2 + half] = e
            sums.append(dot(e, jnp.where(mine, vp, jnp.ones_like(vp))))
        value = jnp.where(low_lane, sums[0], sums[1])
        total = pltpu.roll(jnp.where(low_lane, sums[1], sums[0]), HD, 1)
        inverse = 1.0 / total
        o = value * inverse
        if save:
            linv_out[:, lanes] = inverse
            o_out[:, lanes] = o
        acc[...] += dot(o.astype(BF16), wo_ref[lanes, :])

    @pl.when(step == last)
    def _():
        y_ref[...] = acc[...].astype(y_ref.dtype)


def attn_fwd(save, x, small, w, cos, sin, qe, ke, low=0, high=None, before=None):
    rows, width = x.shape
    group = 4 * HD
    steps = width // group
    high = steps if high is None else high
    first, final = low == 0, high == steps
    whole = pl.BlockSpec((rows, width), lambda g: (0, 0))
    part = pl.BlockSpec((rows, group), lambda g: (0, low + g))
    enc = pl.BlockSpec((rows, 128), lambda g: (0, 0))

    def wcol(base):
        return pl.BlockSpec((None, width, group), lambda g, base=base: (base, 0, low + g))

    def bias(row):
        return pl.BlockSpec((1, group), lambda g, row=row: (0, row * steps + low + g))

    flat = small[2:6].reshape(1, 4 * width)
    heads = width // HD
    out_shape = [jax.ShapeDtypeStruct((rows, width), BF16 if final else F32)]
    out_specs = [whole]
    if save:
        out_shape += [jax.ShapeDtypeStruct((rows, width), BF16)] * 3
        out_shape += [jax.ShapeDtypeStruct((heads, rows, rows), BF16)]
        out_shape += [jax.ShapeDtypeStruct((rows, width), F32)] * 2
        out_specs += [part] * 3 + [pl.BlockSpec((4, rows, rows), lambda g: (g, 0, 0))] + [part] * 2
    return pl.pallas_call(
        functools.partial(attn_fwd_kernel, save, first, final),
        grid=(high - low,),
        in_specs=[
            whole,
            pl.BlockSpec((7, width), lambda g: (0, 0)),
            wcol(0), wcol(1), wcol(2),
            pl.BlockSpec((None, group, width), lambda g: (3, low + g, 0)),
            part, part, enc, enc,
            bias(0), bias(1), bias(2),
        ]
        + ([] if first else [whole]),
        out_specs=out_specs,
        out_shape=out_shape,
        scratch_shapes=[pltpu.VMEM((rows, width), BF16), pltpu.VMEM((rows, width), F32)],
        compiler_params=pltpu.CompilerParams(vmem_limit_bytes=BIG_VMEM if save else MIDDLE_VMEM),
        cost_estimate=pl.CostEstimate(
            flops=2 * rows * width * 4 * width + 4 * 4 * rows * rows * width,
            bytes_accessed=8 * width * width + 4 * rows * width,
            transcendentals=heads * rows * rows,
        ),
        name="attn_fwd",
    )(x, small, w, w, w, w, cos, sin, qe, ke, flat, flat, flat, *([] if first else [before]))


def mlp_fwd_kernel(save, x_ref, small_ref, bias_ref, wi_ref, wo_ref, y_ref, *rest):
    if save:
        z_out, slope_out, u_s, acc = rest
    else:
        u_s, acc = rest
    step = pl.program_id(0)

    @pl.when(step == 0)
    def _():
        stream = x_ref[...].astype(F32)
        normed, _ = normalize(stream)
        u_s[...] = (normed * small_ref[0:1] + small_ref[1:2]).astype(BF16)
        acc[...] = stream + small_ref[6:7]

    a = dot(u_s[...], wi_ref[...]) + bias_ref[...]
    phi = 0.5 + 0.5 * lax.erf(a * SQRT_HALF)
    z = (a * phi).astype(BF16)
    if save:
        z_out[...] = z
        slope_out[...] = (phi + a * jnp.exp2(a * a * (-0.5 * LOG2E)) * INV_ROOT_TAU).astype(BF16)
    acc[...] += dot(z, wo_ref[...])

    @pl.when(step == pl.num_programs(0) - 1)
    def _():
        y_ref[...] = acc[...].astype(BF16)


def mlp_fwd(save, x, small, wi, wo, tile=768):
    rows, width = x.shape
    hidden = wi.shape[0] * wi.shape[2]
    per_block = width // tile
    steps = hidden // tile
    whole = pl.BlockSpec((rows, width), lambda g: (0, 0))
    part = pl.BlockSpec((rows, tile), lambda g: (0, g))
    out_shape = [jax.ShapeDtypeStruct((rows, width), BF16)]
    out_specs = [whole]
    if save:
        out_shape += [jax.ShapeDtypeStruct((rows, hidden), BF16)] * 2
        out_specs += [part] * 2
    return pl.pallas_call(
        functools.partial(mlp_fwd_kernel, save),
        grid=(steps,),
        in_specs=[
            whole,
            pl.BlockSpec((7, width), lambda g: (0, 0)),
            pl.BlockSpec((1, tile), lambda g: (0, g)),
            pl.BlockSpec((None, width, tile), lambda g: (g // per_block, 0, g % per_block)),
            pl.BlockSpec((tile, width), lambda g: (g, 0)),
        ],
        out_specs=out_specs,
        out_shape=out_shape,
        scratch_shapes=[pltpu.VMEM((rows, width), BF16), pltpu.VMEM((rows, width), F32)],
        compiler_params=pltpu.CompilerParams(vmem_limit_bytes=BIG_VMEM if save else MIDDLE_VMEM),
        cost_estimate=pl.CostEstimate(
            flops=4 * rows * width * hidden,
            bytes_accessed=4 * width * hidden + 4 * rows * width,
            transcendentals=2 * rows * hidden,
        ),
        name="mlp_fwd",
    )(x, small, small[2:6].reshape(1, hidden), wi, wo)


def norm_back(full, x_ref, gy_ref, small_ref, du, gx_ref, rows_ref):
    normed, inverse = normalize(x_ref[...].astype(F32))
    scaled = du * small_ref[0:1]
    inner = (
        scaled
        - jnp.mean(scaled, axis=-1, keepdims=True)
        - normed * jnp.mean(scaled * normed, axis=-1, keepdims=True)
    )
    gy = gy_ref[...].astype(F32)
    gx_ref[...] = (gy + inverse * inner).astype(BF16)
    if full:
        rows_ref[0:1] = jnp.sum(du * normed, axis=0, keepdims=True)
        rows_ref[1:2] = jnp.sum(du, axis=0, keepdims=True)
        rows_ref[2:3] = jnp.sum(gy, axis=0, keepdims=True)


def turn_kernel(x_ref, small_ref, mid_ref, small_mid_ref, o_ref, z_ref, ut_ref, ut_mid_ref, ot_ref, zt_ref):
    for source, small, target in ((x_ref, small_ref, ut_ref), (mid_ref, small_mid_ref, ut_mid_ref)):
        normed, _ = normalize(source[...].astype(F32))
        target[...] = (normed * small[0:1] + small[1:2]).astype(BF16).T
    ot_ref[...] = o_ref[...].astype(BF16).T
    width = x_ref.shape[1]
    for block in range(z_ref.shape[1] // width):
        zt_ref[block * width : (block + 1) * width, :] = z_ref[:, block * width : (block + 1) * width].T


def turned_factors(x, small, mid, small_mid, o, z):
    rows, width = x.shape
    vmem = pl.BlockSpec(memory_space=pltpu.VMEM)
    return pl.pallas_call(
        turn_kernel,
        in_specs=[vmem] * 6,
        out_specs=[vmem] * 4,
        out_shape=[jax.ShapeDtypeStruct((width, rows), BF16)] * 3
        + [jax.ShapeDtypeStruct((z.shape[1], rows), BF16)],
        compiler_params=pltpu.CompilerParams(vmem_limit_bytes=SMALL_VMEM),
        cost_estimate=pl.CostEstimate(
            flops=40 * rows * width, bytes_accessed=40 * rows * width, transcendentals=0
        ),
        name="turned_factors",
    )(x, small, mid, small_mid, o, z)


def mlp_bwd_kernel(
    full, core_ref, x_ref, gy_ref, small_ref, wi_ref, wo_ref, slope_ref, *rest
):
    if full:
        ut_ref, zt_ref, gx_ref, rows_ref, bias_ref, up_kept, up_sent, down_kept, down_sent, du_s = rest
    else:
        gx_ref, du_s = rest
        rows_ref = None
    step = pl.program_id(0)

    @pl.when(step == 0)
    def _():
        du_s[...] = jnp.zeros_like(du_s)

    gy = gy_ref[...]
    dz = dot_t(gy, wo_ref[...])
    da = (dz * slope_ref[...].astype(F32)).astype(BF16)
    du_s[...] += dot_t(da, wi_ref[...])
    if full:
        first_core = core_ref[0] == 0
        bias_ref[...] = jnp.sum(da.astype(F32), axis=0, keepdims=True)
        members, share = up_kept.shape[1:3]
        d_up = dot(ut_ref[...], da).reshape(members, share, da.shape[1]).astype(BF16)

        @pl.when(step < pl.num_programs(0) // 2)
        def _():
            up_sent[0] = d_up

        @pl.when(step >= pl.num_programs(0) // 2)
        def _():
            up_kept[0] = d_up

        d_down = dot(zt_ref[...], gy)
        for member in range(down_kept.shape[0]):
            for block in range(2):
                low = (member * 4 + block) * share
                one = d_down[low : low + share]
                two = d_down[low + 2 * share : low + 3 * share]
                down_kept[member, block] = jnp.where(first_core, one, two).astype(BF16)
                down_sent[member, block] = jnp.where(first_core, two, one).astype(BF16)

    @pl.when(step == pl.num_programs(0) - 1)
    def _():
        norm_back(full, x_ref, gy_ref, small_ref, du_s[...], gx_ref, rows_ref)


def mlp_bwd(full, core, x, gy, small, wi, wo, slope, ut=None, zt=None, members=None):
    rows, width = x.shape
    blocks = wi.shape[0]
    hidden = blocks * width
    half = blocks // 2

    def block_of(g, core_ref):
        return jnp.where(g < half, (1 - core_ref[0]) * half + g, core_ref[0] * half + g - half)

    whole = pl.BlockSpec((rows, width), lambda g, c: (0, 0))
    part = pl.BlockSpec((rows, width), lambda g, c: (0, block_of(g, c)))
    in_specs = [
        whole, whole,
        pl.BlockSpec((7, width), lambda g, c: (0, 0)),
        pl.BlockSpec((None, width, width), lambda g, c: (block_of(g, c), 0, 0)),
        pl.BlockSpec((width, width), lambda g, c: (block_of(g, c), 0)),
        part,
    ]
    operands = [x, gy, small, wi, wo, slope]
    out_shape = [jax.ShapeDtypeStruct((rows, width), BF16)]
    out_specs = [whole]
    if full:
        share = width // members
        operands += [ut, zt]
        in_specs += [
            pl.BlockSpec((width, rows), lambda g, c: (0, 0)),
            pl.BlockSpec((width, rows), lambda g, c: (block_of(g, c), 0)),
        ]
        out_shape += [
            jax.ShapeDtypeStruct((8, width), F32),
            jax.ShapeDtypeStruct((1, hidden), F32),
        ]
        out_shape += [jax.ShapeDtypeStruct((2, members, share, width), BF16)] * 2
        out_shape += [jax.ShapeDtypeStruct((members, 2, share, width), BF16)] * 2
        up_block = (1, members, share, width)
        down = pl.BlockSpec(
            (members // blocks, 2, share, width), lambda g, c: (block_of(g, c), 0, 0, 0)
        )
        out_specs += [
            pl.BlockSpec((8, width), lambda g, c: (0, 0)),
            pl.BlockSpec((1, width), lambda g, c: (0, block_of(g, c))),
            pl.BlockSpec(up_block, lambda g, c: (jnp.maximum(g - half, 0), 0, 0, 0)),
            pl.BlockSpec(up_block, lambda g, c: (jnp.minimum(g, half - 1), 0, 0, 0)),
            down, down,
        ]
    return pl.pallas_call(
        functools.partial(mlp_bwd_kernel, full),
        grid_spec=pltpu.PrefetchScalarGridSpec(
            num_scalar_prefetch=1,
            grid=(blocks,),
            in_specs=in_specs,
            out_specs=out_specs,
            scratch_shapes=[pltpu.VMEM((rows, width), F32)],
        ),
        out_shape=out_shape,
        compiler_params=pltpu.CompilerParams(vmem_limit_bytes=BIG_VMEM),
        cost_estimate=pl.CostEstimate(
            flops=(8 if full else 4) * rows * width * hidden,
            bytes_accessed=(8 if full else 4) * width * hidden + 6 * rows * width + 4 * rows * hidden,
            transcendentals=0,
        ),
        name="mlp_bwd_full" if full else "mlp_bwd_act",
    )(core, *operands)


def norm_kernel(
    core_ref, x_ref, gy_ref, small_ref, du_ref, bias_ref, turned_ref, mlp_rows_ref, up_bias_ref,
    gx_ref, kept_ref, sent_ref, rows_ref
):
    norm_back(True, x_ref, gy_ref, small_ref, du_ref[...], gx_ref, rows_ref)
    width = x_ref.shape[1]
    across, along = turned_ref[0:1], turned_ref[1:2]
    first = (lane_index(width) % HD) < HD // 2
    frequency = jnp.where(
        first,
        pltpu.roll(across, width - HD // 2, 1) - across,
        along - pltpu.roll(along, HD // 2, 1),
    )
    attn = [rows_ref[0:1], rows_ref[1:2], bias_ref[0:1], bias_ref[1:2], bias_ref[2:3], rows_ref[2:3], frequency]
    mlp = [mlp_rows_ref[0:1], mlp_rows_ref[1:2]]
    mlp += [up_bias_ref[0:1, i * width : (i + 1) * width] for i in range(4)]
    mlp += [mlp_rows_ref[2:3]]
    first_core = core_ref[0] == 0
    kept_ref[7:8] = jnp.zeros_like(across)
    sent_ref[7:8] = jnp.zeros_like(across)
    for row, (one, two) in enumerate(zip(attn, mlp)):
        kept_ref[row : row + 1] = jnp.where(first_core, one, two)
        sent_ref[row : row + 1] = jnp.where(first_core, two, one)


def norm_bwd(core, x, gy, small, du, attn_bias, turned, mlp_rows, up_bias):
    rows, width = x.shape
    vmem = pl.BlockSpec(memory_space=pltpu.VMEM)
    return pl.pallas_call(
        norm_kernel,
        in_specs=[pl.BlockSpec(memory_space=pltpu.SMEM)] + [vmem] * 8,
        out_specs=[vmem] * 3,
        out_shape=[jax.ShapeDtypeStruct((rows, width), BF16)]
        + [jax.ShapeDtypeStruct((8, width), F32)] * 2,
        scratch_shapes=[pltpu.VMEM((8, width), F32)],
        compiler_params=pltpu.CompilerParams(vmem_limit_bytes=SMALL_VMEM),
        cost_estimate=pl.CostEstimate(
            flops=30 * rows * width, bytes_accessed=10 * rows * width, transcendentals=0
        ),
        name="norm_bwd",
    )(core, x, gy, small, du, attn_bias, turned, mlp_rows, up_bias)


def attn_bwd_kernel(
    full, first, final, x_ref, gy_ref, small_ref, wq_ref, wk_ref, wv_ref, wo_ref, cos_ref, sin_ref,
    q_ref, k_ref, v_ref, e_ref, linv_ref, o_ref, *rest
):
    if full:
        core_ref, gy_part_ref, ut_ref, ot_ref, grid_ref = rest[:5]
        rest = rest[5:]
    if not first:
        before_ref, rest = rest[0], rest[1:]
        if full:
            rest = rest[4:]
    out_ref, rest = rest[0], rest[1:]
    rows_ref = None
    if full:
        bias_ref, angle_ref, kept_ref, sent_ref = rest[:4]
        rest = rest[4:]
        if final:
            rows_ref, rest = rest[0], rest[1:]
    (du_s,) = rest
    step = pl.program_id(0)

    @pl.when(step == 0)
    def _():
        du_s[...] = jnp.zeros_like(du_s) if first else before_ref[...]

    gy = gy_ref[...]
    width = q_ref.shape[1]
    scale = HD ** (-0.5)
    low_lane = lane_index(2 * HD) < HD
    do_all = dot_t(gy, wo_ref[...])
    o_all = o_ref[...]
    dos_all = (do_all * linv_ref[...]).astype(BF16)
    parts = []
    for pair in range(width // (2 * HD)):
        lanes = slice(pair * 2 * HD, (pair + 1) * 2 * HD)
        qp, kp, vp = q_ref[:, lanes], k_ref[:, lanes], v_ref[:, lanes]
        dos = dos_all[:, lanes]
        product = dos.astype(F32) * o_all[:, lanes]
        zero = jnp.zeros_like(qp)
        dq = dk = dv = 0.0
        for half in range(2):
            mine = low_lane if half == 0 else jnp.logical_not(low_lane)
            offset = jnp.sum(jnp.where(mine, product, 0.0), axis=-1, keepdims=True)
            dos_h = jnp.where(mine, dos, zero)
            e = e_ref[pair * 2 + half]
            dp = dot_t(dos_h, vp)
            ds = (e.astype(F32) * (dp - offset)).astype(BF16)
            dv = dv + tdot(e, dos_h)
            dq = dq + dot(ds, jnp.where(mine, kp, zero))
            dk = dk + tdot(ds, jnp.where(mine, qp, zero))
        parts.append((dq * scale, dk * scale, dv))
    dqr = jnp.concatenate([p[0] for p in parts], axis=1)
    dkr = jnp.concatenate([p[1] for p in parts], axis=1)
    dv = jnp.concatenate([p[2] for p in parts], axis=1).astype(BF16)
    cosine, sine = cos_ref[...], sin_ref[...]
    dq = (dqr * cosine - swap_halves(dqr) * sine).astype(BF16)
    dk = (dkr * cosine - swap_halves(dkr) * sine).astype(BF16)
    du_s[...] += dot_t(dq, wq_ref[...]) + dot_t(dk, wk_ref[...]) + dot_t(dv, wv_ref[...])
    if full:
        turned = dqr * swap_halves(q_ref[...].astype(F32)) + dkr * swap_halves(k_ref[...].astype(F32))
        angle_ref[0:1] = jnp.sum(turned * grid_ref[:, 0:1], axis=0, keepdims=True)
        angle_ref[1:2] = jnp.sum(turned * grid_ref[:, 1:2], axis=0, keepdims=True)
        bias_ref[0:1] = jnp.sum(dq.astype(F32), axis=0, keepdims=True)
        bias_ref[1:2] = jnp.sum(dk.astype(F32), axis=0, keepdims=True)
        bias_ref[2:3] = jnp.sum(dv.astype(F32), axis=0, keepdims=True)
        first_core = core_ref[0] == 0
        members, share = kept_ref.shape[1:3]
        ut = ut_ref[...]
        pairs = (
            (dot(ut, dq), dot(ut, dv)),
            (dot(ut, dk), dot(ot_ref[...], gy_part_ref[...])),
        )
        for block, (one, two) in enumerate(pairs):
            one = one.reshape(members, share, width)
            two = two.reshape(members, share, width)
            kept_ref[block] = jnp.where(first_core, one, two).astype(BF16)
            sent_ref[block] = jnp.where(first_core, two, one).astype(BF16)

    @pl.when(step == pl.num_programs(0) - 1)
    def _():
        if final:
            norm_back(full, x_ref, gy_ref, small_ref, du_s[...], out_ref, rows_ref)
        else:
            out_ref[...] = du_s[...]


def attn_bwd(full, x, gy, small, w, cos, sin, saved, extra=None, members=None, low=0, high=None, before=None, close=True):
    rows, width = x.shape
    group = 4 * HD
    groups = width // group
    high = groups if high is None else high
    first, final = low == 0, close and high == groups
    heads = width // HD
    whole = pl.BlockSpec((rows, width), lambda g: (0, 0))
    part = pl.BlockSpec((rows, group), lambda g: (0, low + g))

    def wcol(base):
        return pl.BlockSpec((None, width, group), lambda g, base=base: (base, 0, low + g))

    strip = pl.BlockSpec((8, group), lambda g: (0, low + g))
    out_shape = [jax.ShapeDtypeStruct((rows, width), BF16 if final else F32)]
    out_specs = [whole]
    q, k, v, e, linv, o = saved
    operands = [x, gy, small, w, w, w, w, cos, sin, q, k, v, e, linv, o]
    in_specs = [
        whole if final else pl.BlockSpec(memory_space=pl.ANY), whole,
        pl.BlockSpec((7, width), lambda g: (0, 0)),
        wcol(0), wcol(1), wcol(2),
        pl.BlockSpec((None, group, width), lambda g: (3, low + g, 0)),
        part, part, part, part, part,
        pl.BlockSpec((4, rows, rows), lambda g: (low + g, 0, 0)),
        part, part,
    ]
    if full:
        core, ut, ot, grid_pos = extra
        operands += [core, gy, ut, ot, grid_pos]
        across = pl.BlockSpec((width, rows), lambda g: (0, 0))
        in_specs += [
            pl.BlockSpec(memory_space=pltpu.SMEM), part, across, across,
            pl.BlockSpec((rows, 128), lambda g: (0, 0)),
        ]
        share = width // members
        out_shape += [jax.ShapeDtypeStruct((8, width), F32)] * 2
        out_shape += [jax.ShapeDtypeStruct((2, members, share, width), BF16)] * 2
        out_specs += [strip, strip]
        out_specs += [pl.BlockSpec((2, members, share, group), lambda g: (0, 0, 0, low + g))] * 2
        if final:
            out_shape += [jax.ShapeDtypeStruct((8, width), F32)]
            out_specs += [pl.BlockSpec((8, width), lambda g: (0, 0))]
    aliases = {}
    if not first:
        if full:
            aliases = {len(operands) + 1 + i: 1 + i for i in range(4)}
        operands += list(before[: 5 if full else 1])
        in_specs += [whole] + [pl.BlockSpec(memory_space=pl.ANY)] * (4 if full else 0)
    portion = (high - low) / groups
    return pl.pallas_call(
        functools.partial(attn_bwd_kernel, full, first, final),
        grid=(high - low,),
        in_specs=in_specs,
        out_specs=out_specs,
        out_shape=out_shape,
        scratch_shapes=[pltpu.VMEM((rows, width), F32)],
        input_output_aliases=aliases,
        compiler_params=pltpu.CompilerParams(vmem_limit_bytes=PIECE_VMEM if full else BIG_VMEM),
        cost_estimate=pl.CostEstimate(
            flops=int(portion * ((16 if full else 8) * rows * width * width + 64 * rows * rows * width)),
            bytes_accessed=int(portion * ((16 if full else 8) * width * width + 30 * rows * width + 2 * heads * rows * rows)),
            transcendentals=0,
        ),
        name="attn_bwd_full" if full else "attn_bwd_act",
    )(*operands)


SMALL_ROWS = 16


def terms_kernel(first_dims, *refs):
    out = refs[-1]
    share = refs[0].shape[2]
    for member in range(out.shape[0]):
        row = 0
        for kept, met, first in zip(refs[0:-1:2], refs[1:-1:2], first_dims):
            for block in range(2):
                at = (block, member) if first else (member, block)
                total = kept[at].astype(F32) + met[at].astype(F32)
                out[member, row : row + share] = total.astype(BF16)
                row += share


def joined_terms(sums, vmem):
    operands, in_specs = [], []
    for kept, met, first in sums:
        share, width = kept.shape[2:]
        members = kept.shape[1] if first else kept.shape[0]
        if first:
            spec = pl.BlockSpec((2, members // 2, share, width), lambda m: (0, m, 0, 0))
        else:
            spec = pl.BlockSpec((members // 2, 2, share, width), lambda m: (m, 0, 0, 0))
        operands += [kept, met]
        in_specs += [spec, spec]
    rows = 2 * len(sums) * share
    return pl.pallas_call(
        functools.partial(terms_kernel, tuple(item[2] for item in sums)),
        grid=(2,),
        in_specs=in_specs,
        out_specs=pl.BlockSpec((members // 2, rows, width), lambda m: (m, 0, 0)),
        out_shape=jax.ShapeDtypeStruct((members, rows, width), BF16),
        compiler_params=pltpu.CompilerParams(vmem_limit_bytes=vmem),
        cost_estimate=pl.CostEstimate(
            flops=members * rows * width, bytes_accessed=6 * members * rows * width, transcendentals=0
        ),
        name="joined_terms",
    )(*operands)


def unpacked(value):
    half = SMALL_ROWS // 2
    return value[:half].astype(F32) + value[half:].astype(F32)


def ring_sum_kernel(kind, extra, members_ref, *refs):
    if kind == "open":
        term, refs = refs[0], refs[1:]
        if extra:
            kept, met, right_ref, left_ref, small_out = refs
            small = kept[...] + met[...]
            small_out[...] = small
            high = small.astype(BF16)
            packed = jnp.concatenate([high.astype(F32), small - high.astype(F32)], axis=0).astype(BF16)
            right_ref[-extra:] = packed
            left_ref[-extra:] = packed
        else:
            right_ref, left_ref = refs
        middle = right_ref.shape[0] - extra
        right_ref[:middle] = term[0, :middle]
        left_ref[:middle] = term[0, middle:]
        return
    sides = 1 if kind == "close" else 2
    terms, refs = refs[:sides], refs[sides:]
    came, refs = refs[:2], refs[2:]
    if extra:
        small_in, refs = refs[0], refs[1:]
        small_out, refs = refs[-1], refs[:-1]
        small = small_in[...] + unpacked(came[0][-extra:])
        if kind != "close":
            small = small + unpacked(came[1][-extra:])
        small_out[...] = small
    rows = terms[0].shape[1]
    if kind == "close":
        refs[0][...] = terms[0][0].astype(F32) + came[0][:rows].astype(F32) + came[1][:rows].astype(F32)
        return
    middle = rows // 2
    for side in range(2):
        term, out = terms[side], refs[side]
        if kind == "later":
            out[:rows] = (term[0].astype(F32) + came[side][:rows].astype(F32)).astype(BF16)
        else:
            near = slice(0, middle) if side == 0 else slice(middle, rows)
            far = slice(middle, rows) if side == 0 else slice(0, middle)
            out[near] = (term[0, near].astype(F32) + came[side][:middle].astype(F32)).astype(BF16)
            out[far] = term[0, far]
        if extra:
            out[rows:] = came[side][-extra:]


class RingSum:
    def __init__(self, ring, terms, small=()):
        self.ring, self.terms = ring, terms
        self.reach = ring.size // 2
        self.done = 0
        self.extra = SMALL_ROWS if small else 0
        self.keep(self.call("open", (self.reach,), *small))

    def keep(self, results):
        self.going = tuple(results[:2])
        if self.extra:
            self.small = results[2]

    def call(self, kind, offsets, *values):
        rows, width = self.terms.shape[1:]
        operands, in_specs = [], []
        for offset in offsets:
            at = offset % self.ring.size
            operands.append(self.terms)
            in_specs.append(pl.BlockSpec((1, rows, width), lambda g, m, at=at: (m[at], 0, 0)))
        values = list(values)
        if self.extra and kind != "open":
            values.append(self.small)
        for value in values:
            operands.append(value)
            in_specs.append(pl.BlockSpec(value.shape, lambda g, m: (0, 0)))
        if kind == "open":
            shapes = [jax.ShapeDtypeStruct((rows // 2 + self.extra, width), BF16)] * 2
        elif kind == "close":
            shapes = [jax.ShapeDtypeStruct((rows, width), F32)]
        else:
            shapes = [jax.ShapeDtypeStruct((rows + self.extra, width), BF16)] * 2
        if self.extra:
            shapes.append(jax.ShapeDtypeStruct((SMALL_ROWS // 2, width), F32))
        return pl.pallas_call(
            functools.partial(ring_sum_kernel, kind, self.extra),
            grid_spec=pltpu.PrefetchScalarGridSpec(
                num_scalar_prefetch=1,
                grid=(1,),
                in_specs=in_specs,
                out_specs=[pl.BlockSpec(s.shape, lambda g, m: (0, 0)) for s in shapes],
            ),
            out_shape=shapes,
            compiler_params=pltpu.CompilerParams(vmem_limit_bytes=SMALL_VMEM),
            cost_estimate=pl.CostEstimate(
                flops=2 * rows * width, bytes_accessed=12 * rows * width, transcendentals=0
            ),
            name="ring_sum_" + kind,
        )(self.ring.members, *operands)

    def hop(self):
        self.came = (self.ring.to_right(self.going[0]), self.ring.to_left(self.going[1]))
        self.done += 1
        return self.came

    def add(self, came):
        left = self.reach - self.done
        self.keep(self.call("second" if self.done == 1 else "later", (left, -left), *came))

    def close(self, came):
        return self.call("close", (0,), *came)


NEXT_LAYER = ((0, 2), (1, 3))
PREV_LAYER = ((2, 0), (3, 1))
SIBLING = ((0, 1), (1, 0), (2, 3), (3, 2))
FROM_MLP = ((1, 0), (3, 2))
FROM_ATTN = ((0, 1), (2, 3))
MOMENTUM = 0.9
DECAY = 0.0001
AVERAGE = 0.8
RATE = 0.03
MASKED = -1e30


def sibling(value):
    return lax.ppermute(value, "section", SIBLING)


class Ring:
    def __init__(self, size):
        self.size = size
        order = list(range(0, size, 2)) + list(range(size - 1 - size % 2, 0, -2))
        place = {member: at for at, member in enumerate(order)}
        table = [[order[(place[m] + k) % size] for k in range(size)] for m in range(size)]
        self.members = lax.dynamic_index_in_dim(
            jnp.array(table, jnp.int32), lax.axis_index("dp"), 0, keepdims=False
        )
        self.right = [(order[i], order[(i + 1) % size]) for i in range(size)]
        self.left = [(b, a) for a, b in self.right]

    def member(self, offset):
        return self.members[offset % self.size]

    def to_right(self, value):
        return lax.ppermute(value, "dp", self.right)

    def to_left(self, value):
        return lax.ppermute(value, "dp", self.left)


tied = lax.optimization_barrier


class RingWalk:
    def __init__(self, ring, shard, split):
        self.ring = ring
        self.found = [(shard, 0, 0)]
        self.going = (shard, shard)
        self.done = 0
        self.split = split

    def hop(self):
        self.done += 1
        right, left = self.going
        if self.done < self.ring.size // 2:
            self.going = (self.ring.to_right(right), self.ring.to_left(left))
            self.found += [(self.going[0], -self.done, 0), (self.going[1], self.done, 0)]
        elif self.split:
            middle = right.shape[0] // 2
            self.going = (self.ring.to_right(right[:middle]), self.ring.to_left(left[middle:]))
            self.found += [(self.going[0], self.done, 0), (self.going[1], self.done, middle)]
        else:
            self.going = (self.ring.to_right(right),)
            self.found.append((self.going[0], self.done, 0))

    def renew(self, *going):
        self.going = going
        if self.done:
            count = len(going)
            self.found[-count:] = [(new,) + old[1:] for new, old in zip(going, self.found[-count:])]


def meet(walks, *others):
    out = tied(tuple(value for walk in walks for value in walk.going) + others)
    for walk in walks:
        count = len(walk.going)
        walk.renew(*out[:count])
        out = out[count:]
    return out


def place_spots(core, member, side, first, blocks):
    half = core if side == 0 else 1 - core
    for block in range(first, first + blocks):
        if block < 2:
            yield 0, (half * 2 + block, member)
        else:
            yield 1, (member, half * 2 + block - 2)


def place_kernel(layout, core_ref, members_ref, *refs):
    sources, targets = refs[: len(layout)], refs[len(layout) :]
    for source, (side, offset, first) in zip(sources, layout):
        spots = place_spots(core_ref[0], members_ref[offset], side, first, source.shape[0])
        for block, (matrix, spot) in enumerate(spots):
            targets[matrix][spot] = source[block]


def place_more_kernel(layout, count, core_ref, members_ref, *refs):
    sources = refs[: len(layout)]
    targets, semaphores = refs[len(layout) + count : len(layout) + 2 * count], refs[-1]
    copies = []
    for source, (side, offset, first) in zip(sources, layout):
        spots = place_spots(core_ref[0], members_ref[offset], side, first, source.shape[0])
        for block, (matrix, spot) in enumerate(spots):
            copies.append(
                pltpu.make_async_copy(
                    source.at[block], targets[matrix].at[spot], semaphores.at[len(copies)]
                )
            )
    for copy in copies:
        copy.start()
    for copy in copies:
        copy.wait()


class Matrices:
    def __init__(self, ring, core):
        self.ring, self.core = ring, core
        self.smem = pl.BlockSpec(memory_space=pltpu.SMEM)
        self.vmem = pl.BlockSpec(memory_space=pltpu.VMEM)

    def operands(self, found):
        arrays, layout = [], []
        for value, offset, first in found:
            for side, held in ((0, value), (1, sibling(value))):
                arrays.append(held)
                layout.append((side, offset % self.ring.size, first))
        return arrays, tuple(layout)

    def start(self, found):
        arrays, layout = self.operands(found)
        blocks, rows, width = arrays[0].shape
        shapes = [(4, self.ring.size, rows, width), (self.ring.size, 4, rows, width)][: blocks // 2]
        self.placed = pl.pallas_call(
            functools.partial(place_kernel, layout),
            in_specs=[self.smem] * 2 + [self.vmem] * len(arrays),
            out_specs=[self.vmem] * len(shapes),
            out_shape=[jax.ShapeDtypeStruct(shape, BF16) for shape in shapes],
            compiler_params=pltpu.CompilerParams(vmem_limit_bytes=SMALL_VMEM),
            cost_estimate=pl.CostEstimate(
                flops=0, bytes_accessed=8 * blocks * self.ring.size * rows * width, transcendentals=0
            ),
            name="place_weights",
        )(self.core, self.ring.members, *arrays)
        return tuple(self.placed)

    def finish(self, found):
        arrays, layout = self.operands(found)
        blocks, rows, width = arrays[0].shape
        count = len(self.placed)
        anywhere = pl.BlockSpec(memory_space=pl.ANY)
        first = 2 + len(arrays)
        placed = pl.pallas_call(
            functools.partial(place_more_kernel, layout, count),
            in_specs=[self.smem] * 2 + [self.vmem] * len(arrays) + [anywhere] * count,
            out_specs=[anywhere] * count,
            out_shape=[jax.ShapeDtypeStruct(value.shape, BF16) for value in self.placed],
            input_output_aliases={first + i: i for i in range(count)},
            scratch_shapes=[pltpu.SemaphoreType.DMA((sum(a.shape[0] for a in arrays),))],
            compiler_params=pltpu.CompilerParams(vmem_limit_bytes=SMALL_VMEM),
            cost_estimate=pl.CostEstimate(
                flops=0, bytes_accessed=8 * blocks * rows * width, transcendentals=0
            ),
            name="place_last",
        )(self.core, self.ring.members, *arrays, *self.placed)
        whole = [placed[0].reshape(4, self.ring.size * rows, width)]
        if count == 2:
            whole.append(placed[1].reshape(4 * self.ring.size * rows, width))
        return whole


def advance(master, moment, average, gradient, step_rate):
    gradient = gradient + DECAY * master
    moment = MOMENTUM * moment + gradient
    master = master - step_rate * (gradient + MOMENTUM * moment)
    average = AVERAGE * average + (1 - AVERAGE) * master
    return (moment, master, average)


def on_device(
    block_input, out_cotangent, segment_ids, grid_row, grid_col, valid_slot,
    in_master, out_master, in_moment, out_moment, in_average, out_average,
    small_master, small_moment, small_average,
):
    section_index = lax.axis_index("section")
    layer, core = section_index // 2, section_index % 2
    first_core = core == 0
    first_layer = layer == 0
    core_at = core.reshape(1)
    micro_count, row_count, width = block_input.shape
    ring = Ring(lax.axis_size("dp"))

    def mine(source):
        return jnp.where(first_core, source[0], source[1])

    def by_core(if_first, if_second):
        return jnp.where(first_core, if_first, if_second)

    in_rows, hidden = in_master.shape[1:]
    in_low = in_master[0].astype(BF16)
    in_blocks = jnp.stack([in_low[:, i * width : (i + 1) * width] for i in range(4)])
    down_blocks = out_master[0].astype(BF16).reshape(4, in_rows, width)
    crossed = sibling(by_core(in_blocks[2:], in_blocks[:2]))
    attn_shard = by_core(in_blocks[:2], crossed)
    up_shard = by_core(crossed, in_blocks[2:])
    down_shard = by_core(lax.ppermute(down_blocks[:2], "section", FROM_MLP), down_blocks[2:])
    small_own = small_master[0]
    small_other = sibling(small_own)
    small_attn = by_core(small_own, small_other)
    small_mlp = by_core(small_other, small_own)
    seg, row_at, col_at, valid = (mine(m) for m in (segment_ids, grid_row, grid_col, valid_slot))
    head_count = width // HD
    frequency = small_attn[6].reshape(head_count, 2, 1, HD // 2)
    spread = jnp.broadcast_to(frequency, (head_count, 2, 2, HD // 2))
    angle = (
        col_at.astype(F32)[:, None] * spread[:, 0].reshape(1, width)
        + row_at.astype(F32)[:, None] * spread[:, 1].reshape(1, width)
    )
    turn_sign = jnp.where(lax.broadcasted_iota(jnp.int32, (1, width), 1) % HD < HD // 2, -1.0, 1.0)
    cosine = jnp.cos(angle)
    sine = jnp.sin(angle) * turn_sign
    tag = lax.broadcasted_iota(jnp.int32, (1, 128), 1)
    same = seg[:, None] == tag
    query_tag = same.astype(BF16)
    key_tag = jnp.where(same & (valid[:, None] > 0), 0.0, MASKED).astype(BF16)
    lane = lax.broadcasted_iota(jnp.int32, (1, 128), 1)
    grid_pos = jnp.where(lane == 0, col_at.astype(F32)[:, None], row_at.astype(F32)[:, None])
    x0 = mine(block_input)
    cotangent = mine(out_cotangent) * valid.astype(BF16)[:, None]

    attn_walk = RingWalk(ring, attn_shard, False)
    mlp_walk = RingWalk(ring, jnp.concatenate([up_shard, down_shard]), True)
    reach = ring.size // 2
    attn_walk.hop()
    cosine, sine = meet((attn_walk,), cosine, sine)
    while attn_walk.done < reach:
        attn_walk.hop()
    attn_matrix, mlp_matrices = Matrices(ring, core_at), Matrices(ring, core_at)
    placed = attn_matrix.start(attn_walk.found[:-1])
    *attn_matrix.placed, = meet((attn_walk, mlp_walk), *placed)
    (w_attn,) = attn_matrix.finish(attn_walk.found[-1:])

    while mlp_walk.done < reach - 3:
        mlp_walk.hop()
    attn_args = (x0, small_attn, w_attn, cosine, sine, query_tag, key_tag)
    (running,) = attn_fwd(False, *attn_args, 0, 2)
    (running,) = meet((mlp_walk,), running)
    mlp_walk.hop()
    (mid0,) = attn_fwd(False, *attn_args, 2, None, running)
    (mid0,) = meet((mlp_walk,), mid0)
    mlp_walk.hop()
    meet((mlp_walk,))
    placed = mlp_matrices.start(mlp_walk.found)
    mlp_walk.hop()
    *mlp_matrices.placed, = meet((mlp_walk,), *placed)
    w_up, w_down = mlp_matrices.finish(mlp_walk.found[-2:])
    (top0,) = mlp_fwd(False, mid0, small_mlp, w_up, w_down)
    entering = jnp.where(first_layer, x0, lax.ppermute(top0, "section", NEXT_LAYER))

    mid, *saved = attn_fwd(True, entering, small_attn, w_attn, cosine, sine, query_tag, key_tag)
    top, z, slope = mlp_fwd(True, mid, small_mlp, w_up, w_down)

    def both_micro(attn_value, mlp_value):
        kept = by_core(attn_value, mlp_value)
        crossed = sibling(by_core(mlp_value, attn_value))
        return jnp.stack([by_core(kept, crossed), by_core(crossed, kept)])

    (back_mid,) = mlp_bwd(False, core_at, mid, cotangent, small_mlp, w_up, w_down, slope)
    (back_in,) = attn_bwd(False, entering, back_mid, small_attn, w_attn, cosine, sine, saved)
    arriving = jnp.where(first_layer, lax.ppermute(back_in, "section", PREV_LAYER), cotangent)
    outputs = both_micro(mid, top)
    arriving, outputs = tied((arriving, outputs))
    ut_attn, ut_mlp, o_t, z_t = turned_factors(entering, small_attn, mid, small_mlp, saved[5], z)

    grad_mid, mlp_rows, up_bias, up_kept, up_sent, down_kept, down_sent = mlp_bwd(
        True, core_at, mid, arriving, small_mlp, w_up, w_down, slope, ut_mlp, z_t, ring.size
    )
    met = (sibling(up_sent), sibling(down_sent))
    extra = (core_at, ut_attn, o_t, grid_pos)

    def attn_group(group, before):
        return list(
            attn_bwd(
                True, entering, grad_mid, small_attn, w_attn, cosine, sine, saved, extra, ring.size,
                group, group + 1, before, False,
            )
        )

    back = attn_group(0, None)
    *met, back[0] = tied(met + (back[0],))
    mlp_sum = RingSum(ring, joined_terms(((up_kept, met[0], True), (down_kept, met[1], False)), BIG_VMEM))
    for group in range(1, width // (4 * HD)):
        *mlp_sum.going, back[0] = tied(tuple(mlp_sum.going) + (back[0],))
        back = attn_group(group, back)
        *came, back[0] = tied(tuple(mlp_sum.hop()) + (back[0],))
        mlp_sum.add(came)
    du, attn_bias, turned, attn_kept, attn_sent = back
    *mlp_sum.going, attn_sent, du = tied(tuple(mlp_sum.going) + (attn_sent, du))
    grad_in, small_kept, small_sent = norm_bwd(
        core_at, entering, grad_mid, small_attn, du, attn_bias, turned, mlp_rows, up_bias
    )
    attn_met, small_met, grad_in = tied((sibling(attn_sent), sibling(small_sent), grad_in))
    attn_terms = joined_terms(((attn_kept, attn_met, True),), TERMS_VMEM)
    attn_sum = RingSum(ring, attn_terms, (small_kept, small_met))
    mlp_came = mlp_sum.hop()
    attn_came = attn_sum.hop()
    mlp_sum.add(mlp_came)
    waiting = tied(tuple(attn_came) + tuple(mlp_sum.going))
    attn_came, mlp_sum.going = waiting[:2], waiting[2:]
    mlp_came = mlp_sum.hop()
    attn_sum.add(attn_came)
    while attn_sum.done < reach:
        if mlp_sum.done < reach and attn_sum.done > 1:
            mlp_sum.add(mlp_came)
            waiting = tied(tuple(attn_came) + tuple(mlp_sum.going))
            attn_came, mlp_sum.going = waiting[:2], waiting[2:]
            mlp_came = mlp_sum.hop()
        if attn_sum.done > 1:
            attn_sum.add(attn_came)
        attn_came = attn_sum.hop()
    while mlp_sum.done < reach:
        mlp_sum.add(mlp_came)
        mlp_came = mlp_sum.hop()
    (mlp_share,) = mlp_sum.close(mlp_came)
    attn_share, small_sum = attn_sum.close(attn_came)
    mlp_share = mlp_share.reshape(4, in_rows, width)
    attn_share = attn_share.reshape(2, in_rows, width)
    small_grad = small_sum[:7]
    up_share, down_share = mlp_share[:2], mlp_share[2:]

    crossed = sibling(by_core(up_share, attn_share).astype(BF16)).astype(F32)
    first_half, second_half = by_core(attn_share, crossed), by_core(crossed, up_share)
    share_in = jnp.concatenate([first_half[0], first_half[1], second_half[0], second_half[1]], axis=1)
    crossed = lax.ppermute(down_share.astype(BF16), "section", FROM_ATTN).astype(F32)
    share_out = jnp.where(first_core, 0.0, jnp.concatenate([crossed, down_share]).reshape(4 * in_rows, width))

    step_rate = RATE / math.sqrt(lax.axis_size("dp") * micro_count * row_count)
    in_new = advance(in_master[0], in_moment[0], in_average[0], share_in, step_rate)
    out_new = advance(out_master[0], out_moment[0], out_average[0], share_out, step_rate)
    small_new = advance(small_own, small_moment[0], small_average[0], small_grad, step_rate)
    branch_bias = by_core(small_grad[5], small_grad[6])

    input_grads = both_micro(grad_in, grad_mid)
    return tuple(
        value[None]
        for value in (outputs, input_grads, *in_new, *out_new, *small_new, branch_bias)
    )


def solution(mesh):
    rows = P(None, "dp", None)
    slots = P(None, "dp")
    matrix = P("section", "dp", None)
    vectors = P("section", None, None)
    return jax.shard_map(
        on_device,
        mesh=mesh,
        in_specs=(rows,) * 2 + (slots,) * 4 + (matrix,) * 6 + (vectors,) * 3,
        out_specs=(P("section", None, "dp", None),) * 2 + (matrix,) * 6 + (vectors,) * 3 + (P("section", None),),
        check_vma=False,
    )
```

```python
import functools
import math

import jax
import jax.numpy as jnp
from jax import lax
from jax.experimental import pallas as pl
from jax.experimental.pallas import tpu as pltpu
from jax.sharding import PartitionSpec as P

F32 = jnp.float32
BF16 = jnp.bfloat16
HD = 64
NORM_EPS = 1e-06
SQRT_HALF = 0.7071067811865476
INV_ROOT_TAU = 0.3989422804014327
LOG2E = 1.4426950408889634
BIG_VMEM = 56 * 1024 * 1024
MIDDLE_VMEM = 34 * 1024 * 1024
PIECE_VMEM = 56 * 1024 * 1024
SMALL_VMEM = 14 * 1024 * 1024
TERMS_VMEM = 32 * 1024 * 1024


def dot(lhs, rhs):
    return jnp.dot(lhs, rhs, preferred_element_type=F32)


def dot_t(lhs, rhs):
    return lax.dot_general(lhs, rhs, (((1,), (1,)), ((), ())), preferred_element_type=F32)


def tdot(lhs, rhs):
    return lax.dot_general(lhs, rhs, (((0,), (0,)), ((), ())), preferred_element_type=F32)


def normalize(stream):
    mean = jnp.mean(stream, axis=-1, keepdims=True)
    centered = stream - mean
    inverse = lax.rsqrt(jnp.mean(centered * centered, axis=-1, keepdims=True) + NORM_EPS)
    return centered * inverse, inverse


def lane_index(width):
    return lax.broadcasted_iota(jnp.int32, (1, width), 1)


def swap_halves(value):
    width = value.shape[1]
    first = (lane_index(width) % HD) < HD // 2
    return jnp.where(
        first, pltpu.roll(value, width - HD // 2, 1), pltpu.roll(value, HD // 2, 1)
    )


def attn_fwd_kernel(
    save, first, final, x_ref, small_ref, wq_ref, wk_ref, wv_ref, wo_ref, cos_ref, sin_ref, qe_ref, ke_ref, bq_ref, bk_ref, bv_ref, *rest
):
    if not first:
        before_ref, rest = rest[0], rest[1:]
    y_ref, rest = rest[0], rest[1:]
    if save:
        q_out, k_out, v_out, e_out, linv_out, o_out, u_s, acc = rest
    else:
        u_s, acc = rest
    step = pl.program_id(0)
    last = pl.num_programs(0) - 1

    @pl.when(step == 0)
    def _():
        stream = x_ref[...].astype(F32)
        normed, _ = normalize(stream)
        u_s[...] = (normed * small_ref[0:1] + small_ref[1:2]).astype(BF16)
        acc[...] = stream + small_ref[5:6] if first else before_ref[...]

    lowered = u_s[...]
    cosine, sine = cos_ref[...], sin_ref[...]

    def turn(value):
        return (value * cosine + swap_halves(value) * sine).astype(BF16)

    q = turn(dot(lowered, wq_ref[...]) + bq_ref[...])
    k = turn(dot(lowered, wk_ref[...]) + bk_ref[...])
    v = (dot(lowered, wv_ref[...]) + bv_ref[...]).astype(BF16)
    if save:
        q_out[...] = q
        k_out[...] = k
        v_out[...] = v
    low_lane = lane_index(2 * HD) < HD
    scale = HD ** (-0.5) * LOG2E
    qe, ke = qe_ref[...], ke_ref[...]
    for pair in range(q.shape[1] // (2 * HD)):
        lanes = slice(pair * 2 * HD, (pair + 1) * 2 * HD)
        qp, kp, vp = q[:, lanes], k[:, lanes], v[:, lanes]
        qcat = jnp.concatenate([qp, qe], axis=1)
        sums = []
        for half in range(2):
            mine = low_lane if half == 0 else jnp.logical_not(low_lane)
            kcat = jnp.concatenate([jnp.where(mine, kp, jnp.zeros_like(kp)), ke], axis=1)
            scores = dot_t(qcat, kcat)
            top = jnp.max(scores, axis=-1, keepdims=True)
            e = jnp.exp2((scores - top) * scale).astype(BF16)
            if save:
                e_out[pair * 2 + half] = e
            sums.append(dot(e, jnp.where(mine, vp, jnp.ones_like(vp))))
        value = jnp.where(low_lane, sums[0], sums[1])
        total = pltpu.roll(jnp.where(low_lane, sums[1], sums[0]), HD, 1)
        inverse = 1.0 / total
        o = value * inverse
        if save:
            linv_out[:, lanes] = inverse
            o_out[:, lanes] = o
        acc[...] += dot(o.astype(BF16), wo_ref[lanes, :])

    @pl.when(step == last)
    def _():
        y_ref[...] = acc[...].astype(y_ref.dtype)


def attn_fwd(save, x, small, w, cos, sin, qe, ke, low=0, high=None, before=None):
    rows, width = x.shape
    group = 4 * HD
    steps = width // group
    high = steps if high is None else high
    first, final = low == 0, high == steps
    whole = pl.BlockSpec((rows, width), lambda g: (0, 0))
    part = pl.BlockSpec((rows, group), lambda g: (0, low + g))
    enc = pl.BlockSpec((rows, 128), lambda g: (0, 0))

    def wcol(base):
        return pl.BlockSpec((None, width, group), lambda g, base=base: (base, 0, low + g))

    def bias(row):
        return pl.BlockSpec((1, group), lambda g, row=row: (0, row * steps + low + g))

    flat = small[2:6].reshape(1, 4 * width)
    heads = width // HD
    out_shape = [jax.ShapeDtypeStruct((rows, width), BF16 if final else F32)]
    out_specs = [whole]
    if save:
        out_shape += [jax.ShapeDtypeStruct((rows, width), BF16)] * 3
        out_shape += [jax.ShapeDtypeStruct((heads, rows, rows), BF16)]
        out_shape += [jax.ShapeDtypeStruct((rows, width), F32)] * 2
        out_specs += [part] * 3 + [pl.BlockSpec((4, rows, rows), lambda g: (g, 0, 0))] + [part] * 2
    return pl.pallas_call(
        functools.partial(attn_fwd_kernel, save, first, final),
        grid=(high - low,),
        in_specs=[
            whole,
            pl.BlockSpec((7, width), lambda g: (0, 0)),
            wcol(0), wcol(1), wcol(2),
            pl.BlockSpec((None, group, width), lambda g: (3, low + g, 0)),
            part, part, enc, enc,
            bias(0), bias(1), bias(2),
        ]
        + ([] if first else [whole]),
        out_specs=out_specs,
        out_shape=out_shape,
        scratch_shapes=[pltpu.VMEM((rows, width), BF16), pltpu.VMEM((rows, width), F32)],
        compiler_params=pltpu.CompilerParams(vmem_limit_bytes=BIG_VMEM if save else MIDDLE_VMEM),
        cost_estimate=pl.CostEstimate(
            flops=2 * rows * width * 4 * width + 4 * 4 * rows * rows * width,
            bytes_accessed=8 * width * width + 4 * rows * width,
            transcendentals=heads * rows * rows,
        ),
        name="attn_fwd",
    )(x, small, w, w, w, w, cos, sin, qe, ke, flat, flat, flat, *([] if first else [before]))


def mlp_fwd_kernel(save, x_ref, small_ref, bias_ref, wi_ref, wo_ref, y_ref, *rest):
    if save:
        z_out, slope_out, u_s, acc = rest
    else:
        u_s, acc = rest
    step = pl.program_id(0)

    @pl.when(step == 0)
    def _():
        stream = x_ref[...].astype(F32)
        normed, _ = normalize(stream)
        u_s[...] = (normed * small_ref[0:1] + small_ref[1:2]).astype(BF16)
        acc[...] = stream + small_ref[6:7]

    a = dot(u_s[...], wi_ref[...]) + bias_ref[...]
    phi = 0.5 + 0.5 * lax.erf(a * SQRT_HALF)
    z = (a * phi).astype(BF16)
    if save:
        z_out[...] = z
        slope_out[...] = (phi + a * jnp.exp2(a * a * (-0.5 * LOG2E)) * INV_ROOT_TAU).astype(BF16)
    acc[...] += dot(z, wo_ref[...])

    @pl.when(step == pl.num_programs(0) - 1)
    def _():
        y_ref[...] = acc[...].astype(BF16)


def mlp_fwd(save, x, small, wi, wo, tile=768):
    rows, width = x.shape
    hidden = wi.shape[0] * wi.shape[2]
    per_block = width // tile
    steps = hidden // tile
    whole = pl.BlockSpec((rows, width), lambda g: (0, 0))
    part = pl.BlockSpec((rows, tile), lambda g: (0, g))
    out_shape = [jax.ShapeDtypeStruct((rows, width), BF16)]
    out_specs = [whole]
    if save:
        out_shape += [jax.ShapeDtypeStruct((rows, hidden), BF16)] * 2
        out_specs += [part] * 2
    return pl.pallas_call(
        functools.partial(mlp_fwd_kernel, save),
        grid=(steps,),
        in_specs=[
            whole,
            pl.BlockSpec((7, width), lambda g: (0, 0)),
            pl.BlockSpec((1, tile), lambda g: (0, g)),
            pl.BlockSpec((None, width, tile), lambda g: (g // per_block, 0, g % per_block)),
            pl.BlockSpec((tile, width), lambda g: (g, 0)),
        ],
        out_specs=out_specs,
        out_shape=out_shape,
        scratch_shapes=[pltpu.VMEM((rows, width), BF16), pltpu.VMEM((rows, width), F32)],
        compiler_params=pltpu.CompilerParams(vmem_limit_bytes=BIG_VMEM if save else MIDDLE_VMEM),
        cost_estimate=pl.CostEstimate(
            flops=4 * rows * width * hidden,
            bytes_accessed=4 * width * hidden + 4 * rows * width,
            transcendentals=2 * rows * hidden,
        ),
        name="mlp_fwd",
    )(x, small, small[2:6].reshape(1, hidden), wi, wo)


def norm_back(full, x_ref, gy_ref, small_ref, du, gx_ref, rows_ref):
    normed, inverse = normalize(x_ref[...].astype(F32))
    scaled = du * small_ref[0:1]
    inner = (
        scaled
        - jnp.mean(scaled, axis=-1, keepdims=True)
        - normed * jnp.mean(scaled * normed, axis=-1, keepdims=True)
    )
    gy = gy_ref[...].astype(F32)
    gx_ref[...] = (gy + inverse * inner).astype(BF16)
    if full:
        rows_ref[0:1] = jnp.sum(du * normed, axis=0, keepdims=True)
        rows_ref[1:2] = jnp.sum(du, axis=0, keepdims=True)
        rows_ref[2:3] = jnp.sum(gy, axis=0, keepdims=True)


def turn_kernel(x_ref, small_ref, mid_ref, small_mid_ref, o_ref, z_ref, ut_ref, ut_mid_ref, ot_ref, zt_ref):
    for source, small, target in ((x_ref, small_ref, ut_ref), (mid_ref, small_mid_ref, ut_mid_ref)):
        normed, _ = normalize(source[...].astype(F32))
        target[...] = (normed * small[0:1] + small[1:2]).astype(BF16).T
    ot_ref[...] = o_ref[...].astype(BF16).T
    width = x_ref.shape[1]
    for block in range(z_ref.shape[1] // width):
        zt_ref[block * width : (block + 1) * width, :] = z_ref[:, block * width : (block + 1) * width].T


def turned_factors(x, small, mid, small_mid, o, z):
    rows, width = x.shape
    vmem = pl.BlockSpec(memory_space=pltpu.VMEM)
    return pl.pallas_call(
        turn_kernel,
        in_specs=[vmem] * 6,
        out_specs=[vmem] * 4,
        out_shape=[jax.ShapeDtypeStruct((width, rows), BF16)] * 3
        + [jax.ShapeDtypeStruct((z.shape[1], rows), BF16)],
        compiler_params=pltpu.CompilerParams(vmem_limit_bytes=SMALL_VMEM),
        cost_estimate=pl.CostEstimate(
            flops=40 * rows * width, bytes_accessed=40 * rows * width, transcendentals=0
        ),
        name="turned_factors",
    )(x, small, mid, small_mid, o, z)


def mlp_bwd_kernel(
    full, core_ref, x_ref, gy_ref, small_ref, wi_ref, wo_ref, slope_ref, *rest
):
    if full:
        ut_ref, zt_ref, gx_ref, rows_ref, bias_ref, up_kept, up_sent, down_kept, down_sent, du_s = rest
    else:
        gx_ref, du_s = rest
        rows_ref = None
    step = pl.program_id(0)

    @pl.when(step == 0)
    def _():
        du_s[...] = jnp.zeros_like(du_s)

    gy = gy_ref[...]
    dz = dot_t(gy, wo_ref[...])
    da = (dz * slope_ref[...].astype(F32)).astype(BF16)
    du_s[...] += dot_t(da, wi_ref[...])
    if full:
        first_core = core_ref[0] == 0
        bias_ref[...] = jnp.sum(da.astype(F32), axis=0, keepdims=True)
        members, share = up_kept.shape[1:3]
        d_up = dot(ut_ref[...], da).reshape(members, share, da.shape[1]).astype(BF16)

        @pl.when(step < pl.num_programs(0) // 2)
        def _():
            up_sent[0] = d_up

        @pl.when(step >= pl.num_programs(0) // 2)
        def _():
            up_kept[0] = d_up

        d_down = dot(zt_ref[...], gy)
        for member in range(down_kept.shape[0]):
            for block in range(2):
                low = (member * 4 + block) * share
                one = d_down[low : low + share]
                two = d_down[low + 2 * share : low + 3 * share]
                down_kept[member, block] = jnp.where(first_core, one, two).astype(BF16)
                down_sent[member, block] = jnp.where(first_core, two, one).astype(BF16)

    @pl.when(step == pl.num_programs(0) - 1)
    def _():
        norm_back(full, x_ref, gy_ref, small_ref, du_s[...], gx_ref, rows_ref)


def mlp_bwd(full, core, x, gy, small, wi, wo, slope, ut=None, zt=None, members=None):
    rows, width = x.shape
    blocks = wi.shape[0]
    hidden = blocks * width
    half = blocks // 2

    def block_of(g, core_ref):
        return jnp.where(g < half, (1 - core_ref[0]) * half + g, core_ref[0] * half + g - half)

    whole = pl.BlockSpec((rows, width), lambda g, c: (0, 0))
    part = pl.BlockSpec((rows, width), lambda g, c: (0, block_of(g, c)))
    in_specs = [
        whole, whole,
        pl.BlockSpec((7, width), lambda g, c: (0, 0)),
        pl.BlockSpec((None, width, width), lambda g, c: (block_of(g, c), 0, 0)),
        pl.BlockSpec((width, width), lambda g, c: (block_of(g, c), 0)),
        part,
    ]
    operands = [x, gy, small, wi, wo, slope]
    out_shape = [jax.ShapeDtypeStruct((rows, width), BF16)]
    out_specs = [whole]
    if full:
        share = width // members
        operands += [ut, zt]
        in_specs += [
            pl.BlockSpec((width, rows), lambda g, c: (0, 0)),
            pl.BlockSpec((width, rows), lambda g, c: (block_of(g, c), 0)),
        ]
        out_shape += [
            jax.ShapeDtypeStruct((8, width), F32),
            jax.ShapeDtypeStruct((1, hidden), F32),
        ]
        out_shape += [jax.ShapeDtypeStruct((2, members, share, width), BF16)] * 2
        out_shape += [jax.ShapeDtypeStruct((members, 2, share, width), BF16)] * 2
        up_block = (1, members, share, width)
        down = pl.BlockSpec(
            (members // blocks, 2, share, width), lambda g, c: (block_of(g, c), 0, 0, 0)
        )
        out_specs += [
            pl.BlockSpec((8, width), lambda g, c: (0, 0)),
            pl.BlockSpec((1, width), lambda g, c: (0, block_of(g, c))),
            pl.BlockSpec(up_block, lambda g, c: (jnp.maximum(g - half, 0), 0, 0, 0)),
            pl.BlockSpec(up_block, lambda g, c: (jnp.minimum(g, half - 1), 0, 0, 0)),
            down, down,
        ]
    return pl.pallas_call(
        functools.partial(mlp_bwd_kernel, full),
        grid_spec=pltpu.PrefetchScalarGridSpec(
            num_scalar_prefetch=1,
            grid=(blocks,),
            in_specs=in_specs,
            out_specs=out_specs,
            scratch_shapes=[pltpu.VMEM((rows, width), F32)],
        ),
        out_shape=out_shape,
        compiler_params=pltpu.CompilerParams(vmem_limit_bytes=BIG_VMEM),
        cost_estimate=pl.CostEstimate(
            flops=(8 if full else 4) * rows * width * hidden,
            bytes_accessed=(8 if full else 4) * width * hidden + 6 * rows * width + 4 * rows * hidden,
            transcendentals=0,
        ),
        name="mlp_bwd_full" if full else "mlp_bwd_act",
    )(core, *operands)


def norm_kernel(
    core_ref, x_ref, gy_ref, small_ref, du_ref, bias_ref, turned_ref, mlp_rows_ref, up_bias_ref,
    gx_ref, kept_ref, sent_ref, rows_ref
):
    norm_back(True, x_ref, gy_ref, small_ref, du_ref[...], gx_ref, rows_ref)
    width = x_ref.shape[1]
    across, along = turned_ref[0:1], turned_ref[1:2]
    first = (lane_index(width) % HD) < HD // 2
    frequency = jnp.where(
        first,
        pltpu.roll(across, width - HD // 2, 1) - across,
        along - pltpu.roll(along, HD // 2, 1),
    )
    attn = [rows_ref[0:1], rows_ref[1:2], bias_ref[0:1], bias_ref[1:2], bias_ref[2:3], rows_ref[2:3], frequency]
    mlp = [mlp_rows_ref[0:1], mlp_rows_ref[1:2]]
    mlp += [up_bias_ref[0:1, i * width : (i + 1) * width] for i in range(4)]
    mlp += [mlp_rows_ref[2:3]]
    first_core = core_ref[0] == 0
    kept_ref[7:8] = jnp.zeros_like(across)
    sent_ref[7:8] = jnp.zeros_like(across)
    for row, (one, two) in enumerate(zip(attn, mlp)):
        kept_ref[row : row + 1] = jnp.where(first_core, one, two)
        sent_ref[row : row + 1] = jnp.where(first_core, two, one)


def norm_bwd(core, x, gy, small, du, attn_bias, turned, mlp_rows, up_bias):
    rows, width = x.shape
    vmem = pl.BlockSpec(memory_space=pltpu.VMEM)
    return pl.pallas_call(
        norm_kernel,
        in_specs=[pl.BlockSpec(memory_space=pltpu.SMEM)] + [vmem] * 8,
        out_specs=[vmem] * 3,
        out_shape=[jax.ShapeDtypeStruct((rows, width), BF16)]
        + [jax.ShapeDtypeStruct((8, width), F32)] * 2,
        scratch_shapes=[pltpu.VMEM((8, width), F32)],
        compiler_params=pltpu.CompilerParams(vmem_limit_bytes=SMALL_VMEM),
        cost_estimate=pl.CostEstimate(
            flops=30 * rows * width, bytes_accessed=10 * rows * width, transcendentals=0
        ),
        name="norm_bwd",
    )(core, x, gy, small, du, attn_bias, turned, mlp_rows, up_bias)


def attn_bwd_kernel(full, first, final, low, *refs):
    names = ["x", "gy", "small", "wq", "wk", "wv", "wo", "cos", "sin", "q", "k", "v", "e", "linv", "o"]
    if full:
        names += ["core", "gy_part", "ut", "ot", "grid"]
    names += [] if first else ["before"]
    ref = dict(zip(names, refs))
    rest = refs[len(names) :]
    if full and not first:
        rest = rest[4:]
    out_ref, rest = rest[0], rest[1:]
    rows_ref = None
    if full:
        bias_ref, angle_ref, kept_ref, sent_ref = rest[:4]
        rest = rest[4:]
        if final:
            rows_ref, rest = rest[0], rest[1:]
    du_s, rest = rest[0], rest[1:]
    step = pl.program_id(0)
    copies = {}
    if full:
        semaphores, scratch = rest[-1], rest[:-1]
        group = ref["gy_part"].shape[1]
        lanes = pl.ds(low * group, group)
        source = {
            "cos": ref["cos"].at[:, lanes],
            "sin": ref["sin"].at[:, lanes],
            "wq": ref["wq"].at[0, :, lanes],
            "wk": ref["wk"].at[1, :, lanes],
            "wv": ref["wv"].at[2, :, lanes],
            "ut": ref["ut"],
            "ot": ref["ot"],
        }
        if not first:
            source["before"] = ref["before"]
        number = 0
        for name, target in zip(source, scratch):
            ref[name] = target
            copies[name] = [pltpu.make_async_copy(source[name], target, semaphores.at[number])]
            number += 1
        for group_of in copies.values():
            for copy in group_of:
                copy.start()

    def held(name, head=None):
        if name in copies:
            waiting = copies[name] if head is None else copies[name][head : head + 1]
            for copy in waiting:
                copy.wait()
            if head is None:
                del copies[name]
        return ref[name] if head is None else ref[name][head]

    if not full:

        @pl.when(step == 0)
        def _():
            du_s[...] = jnp.zeros_like(du_s) if first else ref["before"][...]

    gy = ref["gy"][...]
    width = ref["gy_part"].shape[1] if full else ref["q"].shape[1]
    scale = HD ** (-0.5)
    low_lane = lane_index(2 * HD) < HD
    do_all = dot_t(gy, ref["wo"][...])
    o_all = held("o")[...]
    dos_all = (do_all * held("linv")[...]).astype(BF16)
    q_all, k_all, v_all = held("q")[...], held("k")[...], held("v")[...]
    parts = []
    for pair in range(width // (2 * HD)):
        lanes = slice(pair * 2 * HD, (pair + 1) * 2 * HD)
        qp, kp, vp = q_all[:, lanes], k_all[:, lanes], v_all[:, lanes]
        dos = dos_all[:, lanes]
        product = dos.astype(F32) * o_all[:, lanes]
        zero = jnp.zeros_like(qp)
        dq = dk = dv = 0.0
        for half in range(2):
            mine = low_lane if half == 0 else jnp.logical_not(low_lane)
            offset = jnp.sum(jnp.where(mine, product, 0.0), axis=-1, keepdims=True)
            dos_h = jnp.where(mine, dos, zero)
            e = held("e", pair * 2 + half)
            dp = dot_t(dos_h, vp)
            ds = (e.astype(F32) * (dp - offset)).astype(BF16)
            dv = dv + tdot(e, dos_h)
            dq = dq + dot(ds, jnp.where(mine, kp, zero))
            dk = dk + tdot(ds, jnp.where(mine, qp, zero))
        parts.append((dq * scale, dk * scale, dv))
    dqr = jnp.concatenate([p[0] for p in parts], axis=1)
    dkr = jnp.concatenate([p[1] for p in parts], axis=1)
    dv = jnp.concatenate([p[2] for p in parts], axis=1).astype(BF16)
    for name in list(copies):
        held(name)
    cosine, sine = held("cos")[...], held("sin")[...]
    dq = (dqr * cosine - swap_halves(dqr) * sine).astype(BF16)
    dk = (dkr * cosine - swap_halves(dkr) * sine).astype(BF16)
    du = dot_t(dq, held("wq")[...]) + dot_t(dk, held("wk")[...]) + dot_t(dv, held("wv")[...])
    if not full:
        du_s[...] += du
    elif first:
        du_s[...] = du
    else:
        du_s[...] = held("before")[...] + du
    if full:
        turned = dqr * swap_halves(q_all.astype(F32)) + dkr * swap_halves(k_all.astype(F32))
        angle_ref[0:1] = jnp.sum(turned * ref["grid"][:, 0:1], axis=0, keepdims=True)
        angle_ref[1:2] = jnp.sum(turned * ref["grid"][:, 1:2], axis=0, keepdims=True)
        bias_ref[0:1] = jnp.sum(dq.astype(F32), axis=0, keepdims=True)
        bias_ref[1:2] = jnp.sum(dk.astype(F32), axis=0, keepdims=True)
        bias_ref[2:3] = jnp.sum(dv.astype(F32), axis=0, keepdims=True)
        first_core = ref["core"][0] == 0
        members, share = kept_ref.shape[1:3]
        ut = held("ut")[...]
        pairs = (
            (dot(ut, dq), dot(ut, dv)),
            (dot(ut, dk), dot(held("ot")[...], ref["gy_part"][...])),
        )
        for block, (one, two) in enumerate(pairs):
            one = one.reshape(members, share, width)
            two = two.reshape(members, share, width)
            kept_ref[block] = jnp.where(first_core, one, two).astype(BF16)
            sent_ref[block] = jnp.where(first_core, two, one).astype(BF16)

    @pl.when(step == pl.num_programs(0) - 1)
    def _():
        if final:
            norm_back(full, ref["x"], ref["gy"], ref["small"], du_s[...], out_ref, rows_ref)
        else:
            out_ref[...] = du_s[...]


def attn_bwd(full, x, gy, small, w, cos, sin, saved, extra=None, members=None, low=0, high=None, before=None, close=True):
    rows, width = x.shape
    group = 4 * HD
    groups = width // group
    high = groups if high is None else high
    first, final = low == 0, close and high == groups
    heads = width // HD
    whole = pl.BlockSpec((rows, width), lambda g: (0, 0))
    part = pl.BlockSpec((rows, group), lambda g: (0, low + g))

    def wcol(base):
        return pl.BlockSpec((None, width, group), lambda g, base=base: (base, 0, low + g))

    strip = pl.BlockSpec((8, group), lambda g: (0, low + g))
    out_shape = [jax.ShapeDtypeStruct((rows, width), BF16 if final else F32)]
    out_specs = [whole]
    q, k, v, e, linv, o = saved
    operands = [x, gy, small, w, w, w, w, cos, sin, q, k, v, e, linv, o]
    in_specs = [
        whole if final else pl.BlockSpec(memory_space=pl.ANY), whole,
        pl.BlockSpec((7, width), lambda g: (0, 0)),
        wcol(0), wcol(1), wcol(2),
        pl.BlockSpec((None, group, width), lambda g: (3, low + g, 0)),
        part, part, part, part, part,
        pl.BlockSpec((4, rows, rows), lambda g: (low + g, 0, 0)),
        part, part,
    ]
    if full:
        anywhere = pl.BlockSpec(memory_space=pl.ANY)
        for at in (3, 4, 5, 7, 8):
            in_specs[at] = anywhere
        core, ut, ot, grid_pos = extra
        operands += [core, gy, ut, ot, grid_pos]
        in_specs += [
            pl.BlockSpec(memory_space=pltpu.SMEM), part, anywhere, anywhere,
            pl.BlockSpec((rows, 128), lambda g: (0, 0)),
        ]
        share = width // members
        out_shape += [jax.ShapeDtypeStruct((8, width), F32)] * 2
        out_shape += [jax.ShapeDtypeStruct((2, members, share, width), BF16)] * 2
        out_specs += [strip, strip]
        out_specs += [pl.BlockSpec((2, members, share, group), lambda g: (0, 0, 0, low + g))] * 2
        if final:
            out_shape += [jax.ShapeDtypeStruct((8, width), F32)]
            out_specs += [pl.BlockSpec((8, width), lambda g: (0, 0))]
    aliases = {}
    if not first:
        if full:
            aliases = {len(operands) + 1 + i: 1 + i for i in range(4)}
        operands += list(before[: 5 if full else 1])
        in_specs += [pl.BlockSpec(memory_space=pl.ANY)] * 5 if full else [whole]
    portion = (high - low) / groups
    scratch = [pltpu.VMEM((rows, width), F32)]
    if full:
        scratch += [pltpu.VMEM((rows, group), F32)] * 2
        scratch += [pltpu.VMEM((width, group), BF16)] * 3 + [pltpu.VMEM((width, rows), BF16)] * 2
        scratch += [] if first else [pltpu.VMEM((rows, width), F32)]
        scratch += [pltpu.SemaphoreType.DMA((len(scratch) - 1,))]
    return pl.pallas_call(
        functools.partial(attn_bwd_kernel, full, first, final, low),
        grid=(high - low,),
        in_specs=in_specs,
        out_specs=out_specs,
        out_shape=out_shape,
        scratch_shapes=scratch,
        input_output_aliases=aliases,
        compiler_params=pltpu.CompilerParams(vmem_limit_bytes=PIECE_VMEM if full else BIG_VMEM),
        cost_estimate=pl.CostEstimate(
            flops=int(portion * ((16 if full else 8) * rows * width * width + 64 * rows * rows * width)),
            bytes_accessed=int(portion * ((16 if full else 8) * width * width + 30 * rows * width + 2 * heads * rows * rows)),
            transcendentals=0,
        ),
        name="attn_bwd_full" if full else "attn_bwd_act",
    )(*operands)


SMALL_ROWS = 16


def terms_kernel(first_dims, *refs):
    out = refs[-1]
    share = refs[0].shape[2]
    for member in range(out.shape[0]):
        row = 0
        for kept, met, first in zip(refs[0:-1:2], refs[1:-1:2], first_dims):
            for block in range(2):
                at = (block, member) if first else (member, block)
                total = kept[at].astype(F32) + met[at].astype(F32)
                out[member, row : row + share] = total.astype(BF16)
                row += share


def joined_terms(sums, vmem):
    operands, in_specs = [], []
    for kept, met, first in sums:
        share, width = kept.shape[2:]
        members = kept.shape[1] if first else kept.shape[0]
        if first:
            spec = pl.BlockSpec((2, members // 2, share, width), lambda m: (0, m, 0, 0))
        else:
            spec = pl.BlockSpec((members // 2, 2, share, width), lambda m: (m, 0, 0, 0))
        operands += [kept, met]
        in_specs += [spec, spec]
    rows = 2 * len(sums) * share
    return pl.pallas_call(
        functools.partial(terms_kernel, tuple(item[2] for item in sums)),
        grid=(2,),
        in_specs=in_specs,
        out_specs=pl.BlockSpec((members // 2, rows, width), lambda m: (m, 0, 0)),
        out_shape=jax.ShapeDtypeStruct((members, rows, width), BF16),
        compiler_params=pltpu.CompilerParams(vmem_limit_bytes=vmem),
        cost_estimate=pl.CostEstimate(
            flops=members * rows * width, bytes_accessed=6 * members * rows * width, transcendentals=0
        ),
        name="joined_terms",
    )(*operands)


def unpacked(value):
    half = SMALL_ROWS // 2
    return value[:half].astype(F32) + value[half:].astype(F32)


def ring_sum_kernel(kind, extra, members_ref, *refs):
    if kind == "open":
        term, refs = refs[0], refs[1:]
        if extra:
            kept, met, right_ref, left_ref, small_out = refs
            small = kept[...] + met[...]
            small_out[...] = small
            high = small.astype(BF16)
            packed = jnp.concatenate([high.astype(F32), small - high.astype(F32)], axis=0).astype(BF16)
            right_ref[-extra:] = packed
            left_ref[-extra:] = packed
        else:
            right_ref, left_ref = refs
        middle = right_ref.shape[0] - extra
        right_ref[:middle] = term[0, :middle]
        left_ref[:middle] = term[0, middle:]
        return
    sides = 1 if kind == "close" else 2
    terms, refs = refs[:sides], refs[sides:]
    came, refs = refs[:2], refs[2:]
    if extra:
        small_in, refs = refs[0], refs[1:]
        small_out, refs = refs[-1], refs[:-1]
        small = small_in[...] + unpacked(came[0][-extra:])
        if kind != "close":
            small = small + unpacked(came[1][-extra:])
        small_out[...] = small
    rows = terms[0].shape[1]
    if kind == "close":
        refs[0][...] = terms[0][0].astype(F32) + came[0][:rows].astype(F32) + came[1][:rows].astype(F32)
        return
    middle = rows // 2
    for side in range(2):
        term, out = terms[side], refs[side]
        if kind == "later":
            out[:rows] = (term[0].astype(F32) + came[side][:rows].astype(F32)).astype(BF16)
        else:
            near = slice(0, middle) if side == 0 else slice(middle, rows)
            far = slice(middle, rows) if side == 0 else slice(0, middle)
            out[near] = (term[0, near].astype(F32) + came[side][:middle].astype(F32)).astype(BF16)
            out[far] = term[0, far]
        if extra:
            out[rows:] = came[side][-extra:]


class RingSum:
    def __init__(self, ring, terms, small=()):
        self.ring, self.terms = ring, terms
        self.reach = ring.size // 2
        self.done = 0
        self.extra = SMALL_ROWS if small else 0
        self.keep(self.call("open", (self.reach,), *small))

    def keep(self, results):
        self.going = tuple(results[:2])
        if self.extra:
            self.small = results[2]

    def call(self, kind, offsets, *values):
        rows, width = self.terms.shape[1:]
        operands, in_specs = [], []
        for offset in offsets:
            at = offset % self.ring.size
            operands.append(self.terms)
            in_specs.append(pl.BlockSpec((1, rows, width), lambda g, m, at=at: (m[at], 0, 0)))
        values = list(values)
        if self.extra and kind != "open":
            values.append(self.small)
        for value in values:
            operands.append(value)
            in_specs.append(pl.BlockSpec(value.shape, lambda g, m: (0, 0)))
        if kind == "open":
            shapes = [jax.ShapeDtypeStruct((rows // 2 + self.extra, width), BF16)] * 2
        elif kind == "close":
            shapes = [jax.ShapeDtypeStruct((rows, width), F32)]
        else:
            shapes = [jax.ShapeDtypeStruct((rows + self.extra, width), BF16)] * 2
        if self.extra:
            shapes.append(jax.ShapeDtypeStruct((SMALL_ROWS // 2, width), F32))
        return pl.pallas_call(
            functools.partial(ring_sum_kernel, kind, self.extra),
            grid_spec=pltpu.PrefetchScalarGridSpec(
                num_scalar_prefetch=1,
                grid=(1,),
                in_specs=in_specs,
                out_specs=[pl.BlockSpec(s.shape, lambda g, m: (0, 0)) for s in shapes],
            ),
            out_shape=shapes,
            compiler_params=pltpu.CompilerParams(vmem_limit_bytes=SMALL_VMEM),
            cost_estimate=pl.CostEstimate(
                flops=2 * rows * width, bytes_accessed=12 * rows * width, transcendentals=0
            ),
            name="ring_sum_" + kind,
        )(self.ring.members, *operands)

    def hop(self):
        self.came = (self.ring.to_right(self.going[0]), self.ring.to_left(self.going[1]))
        self.done += 1
        return self.came

    def add(self, came):
        left = self.reach - self.done
        self.keep(self.call("second" if self.done == 1 else "later", (left, -left), *came))

    def close(self, came):
        return self.call("close", (0,), *came)


def advance_kernel(rate, core_ref, attn_ref, up_ref, crossed_ref, master_ref, moment_ref, average_ref, *outs):
    step = pl.program_id(0)
    core = core_ref[0]
    own = jnp.where(core == 0, attn_ref[...], up_ref[...])
    gradient = jnp.where(step // 2 == core, own, crossed_ref[...].astype(F32))
    for out, value in zip(outs, advance(master_ref[...], moment_ref[...], average_ref[...], gradient, rate)):
        out[...] = value


def advance_blocks(core, attn, up, crossed, master, moment, average, rate):
    rows, columns = master.shape
    width = columns // 4
    block = pl.BlockSpec((None, rows, width), lambda g: (g % 2, 0, 0))
    part = pl.BlockSpec((rows, width), lambda g: (0, g))
    return pl.pallas_call(
        functools.partial(advance_kernel, rate),
        grid=(4,),
        in_specs=[pl.BlockSpec(memory_space=pltpu.SMEM)] + [block] * 3 + [part] * 3,
        out_specs=[part] * 3,
        out_shape=[jax.ShapeDtypeStruct(master.shape, F32)] * 3,
        compiler_params=pltpu.CompilerParams(vmem_limit_bytes=SMALL_VMEM),
        cost_estimate=pl.CostEstimate(
            flops=12 * rows * columns, bytes_accessed=32 * rows * columns, transcendentals=0
        ),
        name="advance_blocks",
    )(core, attn, up, crossed, master, moment, average)


NEXT_LAYER = ((0, 2), (1, 3))
PREV_LAYER = ((2, 0), (3, 1))
SIBLING = ((0, 1), (1, 0), (2, 3), (3, 2))
FROM_MLP = ((1, 0), (3, 2))
FROM_ATTN = ((0, 1), (2, 3))
MOMENTUM = 0.9
DECAY = 0.0001
AVERAGE = 0.8
RATE = 0.03
MASKED = -1e30


def sibling(value):
    return lax.ppermute(value, "section", SIBLING)


class Ring:
    def __init__(self, size):
        self.size = size
        order = list(range(0, size, 2)) + list(range(size - 1 - size % 2, 0, -2))
        place = {member: at for at, member in enumerate(order)}
        table = [[order[(place[m] + k) % size] for k in range(size)] for m in range(size)]
        self.members = lax.dynamic_index_in_dim(
            jnp.array(table, jnp.int32), lax.axis_index("dp"), 0, keepdims=False
        )
        self.right = [(order[i], order[(i + 1) % size]) for i in range(size)]
        self.left = [(b, a) for a, b in self.right]

    def member(self, offset):
        return self.members[offset % self.size]

    def to_right(self, value):
        return lax.ppermute(value, "dp", self.right)

    def to_left(self, value):
        return lax.ppermute(value, "dp", self.left)


tied = lax.optimization_barrier


class RingWalk:
    def __init__(self, ring, shard, split):
        self.ring = ring
        self.found = [(shard, 0, 0)]
        self.going = (shard, shard)
        self.done = 0
        self.split = split

    def hop(self):
        self.done += 1
        right, left = self.going
        if self.done < self.ring.size // 2:
            self.going = (self.ring.to_right(right), self.ring.to_left(left))
            self.found += [(self.going[0], -self.done, 0), (self.going[1], self.done, 0)]
        elif self.split:
            middle = right.shape[0] // 2
            self.going = (self.ring.to_right(right[:middle]), self.ring.to_left(left[middle:]))
            self.found += [(self.going[0], self.done, 0), (self.going[1], self.done, middle)]
        else:
            self.going = (self.ring.to_right(right),)
            self.found.append((self.going[0], self.done, 0))

    def renew(self, *going):
        self.going = going
        if self.done:
            count = len(going)
            self.found[-count:] = [(new,) + old[1:] for new, old in zip(going, self.found[-count:])]


def meet(walks, *others):
    out = tied(tuple(value for walk in walks for value in walk.going) + others)
    for walk in walks:
        count = len(walk.going)
        walk.renew(*out[:count])
        out = out[count:]
    return out


def place_spots(core, member, side, first, blocks):
    half = core if side == 0 else 1 - core
    for block in range(first, first + blocks):
        if block < 2:
            yield 0, (half * 2 + block, member)
        else:
            yield 1, (member, half * 2 + block - 2)


def place_kernel(layout, core_ref, members_ref, *refs):
    sources, targets = refs[: len(layout)], refs[len(layout) :]
    for source, (side, offset, first) in zip(sources, layout):
        spots = place_spots(core_ref[0], members_ref[offset], side, first, source.shape[0])
        for block, (matrix, spot) in enumerate(spots):
            targets[matrix][spot] = source[block]


def place_more_kernel(layout, count, core_ref, members_ref, *refs):
    sources = refs[: len(layout)]
    targets, semaphores = refs[len(layout) + count : len(layout) + 2 * count], refs[-1]
    copies = []
    for source, (side, offset, first) in zip(sources, layout):
        spots = place_spots(core_ref[0], members_ref[offset], side, first, source.shape[0])
        for block, (matrix, spot) in enumerate(spots):
            copies.append(
                pltpu.make_async_copy(
                    source.at[block], targets[matrix].at[spot], semaphores.at[len(copies)]
                )
            )
    for copy in copies:
        copy.start()
    for copy in copies:
        copy.wait()


class Matrices:
    def __init__(self, ring, core):
        self.ring, self.core = ring, core
        self.smem = pl.BlockSpec(memory_space=pltpu.SMEM)
        self.vmem = pl.BlockSpec(memory_space=pltpu.VMEM)

    def operands(self, found):
        arrays, layout = [], []
        for value, offset, first in found:
            for side, held in ((0, value), (1, sibling(value))):
                arrays.append(held)
                layout.append((side, offset % self.ring.size, first))
        return arrays, tuple(layout)

    def start(self, found):
        arrays, layout = self.operands(found)
        blocks, rows, width = arrays[0].shape
        shapes = [(4, self.ring.size, rows, width), (self.ring.size, 4, rows, width)][: blocks // 2]
        self.placed = pl.pallas_call(
            functools.partial(place_kernel, layout),
            in_specs=[self.smem] * 2 + [self.vmem] * len(arrays),
            out_specs=[self.vmem] * len(shapes),
            out_shape=[jax.ShapeDtypeStruct(shape, BF16) for shape in shapes],
            compiler_params=pltpu.CompilerParams(vmem_limit_bytes=SMALL_VMEM),
            cost_estimate=pl.CostEstimate(
                flops=0, bytes_accessed=8 * blocks * self.ring.size * rows * width, transcendentals=0
            ),
            name="place_weights",
        )(self.core, self.ring.members, *arrays)
        return tuple(self.placed)

    def finish(self, found):
        arrays, layout = self.operands(found)
        blocks, rows, width = arrays[0].shape
        count = len(self.placed)
        anywhere = pl.BlockSpec(memory_space=pl.ANY)
        first = 2 + len(arrays)
        placed = pl.pallas_call(
            functools.partial(place_more_kernel, layout, count),
            in_specs=[self.smem] * 2 + [self.vmem] * len(arrays) + [anywhere] * count,
            out_specs=[anywhere] * count,
            out_shape=[jax.ShapeDtypeStruct(value.shape, BF16) for value in self.placed],
            input_output_aliases={first + i: i for i in range(count)},
            scratch_shapes=[pltpu.SemaphoreType.DMA((sum(a.shape[0] for a in arrays),))],
            compiler_params=pltpu.CompilerParams(vmem_limit_bytes=SMALL_VMEM),
            cost_estimate=pl.CostEstimate(
                flops=0, bytes_accessed=8 * blocks * rows * width, transcendentals=0
            ),
            name="place_last",
        )(self.core, self.ring.members, *arrays, *self.placed)
        whole = [placed[0].reshape(4, self.ring.size * rows, width)]
        if count == 2:
            whole.append(placed[1].reshape(4 * self.ring.size * rows, width))
        return whole


def advance(master, moment, average, gradient, step_rate):
    gradient = gradient + DECAY * master
    moment = MOMENTUM * moment + gradient
    master = master - step_rate * (gradient + MOMENTUM * moment)
    average = AVERAGE * average + (1 - AVERAGE) * master
    return (moment, master, average)


def on_device(
    block_input, out_cotangent, segment_ids, grid_row, grid_col, valid_slot,
    in_master, out_master, in_moment, out_moment, in_average, out_average,
    small_master, small_moment, small_average,
):
    section_index = lax.axis_index("section")
    layer, core = section_index // 2, section_index % 2
    first_core = core == 0
    first_layer = layer == 0
    core_at = core.reshape(1)
    micro_count, row_count, width = block_input.shape
    ring = Ring(lax.axis_size("dp"))

    def mine(source):
        return jnp.where(first_core, source[0], source[1])

    def by_core(if_first, if_second):
        return jnp.where(first_core, if_first, if_second)

    in_rows, hidden = in_master.shape[1:]
    in_low = in_master[0].astype(BF16)
    in_blocks = jnp.stack([in_low[:, i * width : (i + 1) * width] for i in range(4)])
    down_blocks = out_master[0].astype(BF16).reshape(4, in_rows, width)
    crossed = sibling(by_core(in_blocks[2:], in_blocks[:2]))
    attn_shard = by_core(in_blocks[:2], crossed)
    up_shard = by_core(crossed, in_blocks[2:])
    down_shard = by_core(lax.ppermute(down_blocks[:2], "section", FROM_MLP), down_blocks[2:])
    small_own = small_master[0]
    small_other = sibling(small_own)
    small_attn = by_core(small_own, small_other)
    small_mlp = by_core(small_other, small_own)
    seg, row_at, col_at, valid = (mine(m) for m in (segment_ids, grid_row, grid_col, valid_slot))
    head_count = width // HD
    frequency = small_attn[6].reshape(head_count, 2, 1, HD // 2)
    spread = jnp.broadcast_to(frequency, (head_count, 2, 2, HD // 2))
    angle = (
        col_at.astype(F32)[:, None] * spread[:, 0].reshape(1, width)
        + row_at.astype(F32)[:, None] * spread[:, 1].reshape(1, width)
    )
    turn_sign = jnp.where(lax.broadcasted_iota(jnp.int32, (1, width), 1) % HD < HD // 2, -1.0, 1.0)
    cosine = jnp.cos(angle)
    sine = jnp.sin(angle) * turn_sign
    tag = lax.broadcasted_iota(jnp.int32, (1, 128), 1)
    same = seg[:, None] == tag
    query_tag = same.astype(BF16)
    key_tag = jnp.where(same & (valid[:, None] > 0), 0.0, MASKED).astype(BF16)
    lane = lax.broadcasted_iota(jnp.int32, (1, 128), 1)
    grid_pos = jnp.where(lane == 0, col_at.astype(F32)[:, None], row_at.astype(F32)[:, None])
    x0 = mine(block_input)
    cotangent = mine(out_cotangent) * valid.astype(BF16)[:, None]

    attn_walk = RingWalk(ring, attn_shard, False)
    mlp_walk = RingWalk(ring, jnp.concatenate([up_shard, down_shard]), False)
    reach = ring.size // 2
    attn_walk.hop()
    cosine, sine = meet((attn_walk,), cosine, sine)
    while attn_walk.done < reach:
        attn_walk.hop()
    attn_matrix, mlp_matrices = Matrices(ring, core_at), Matrices(ring, core_at)
    placed = attn_matrix.start(attn_walk.found[:-1])
    *attn_matrix.placed, = meet((attn_walk, mlp_walk), *placed)
    (w_attn,) = attn_matrix.finish(attn_walk.found[-1:])

    while mlp_walk.done < reach - 3:
        mlp_walk.hop()
    attn_args = (x0, small_attn, w_attn, cosine, sine, query_tag, key_tag)
    (running,) = attn_fwd(False, *attn_args, 0, 2)
    (running,) = meet((mlp_walk,), running)
    mlp_walk.hop()
    (mid0,) = attn_fwd(False, *attn_args, 2, None, running)
    (mid0,) = meet((mlp_walk,), mid0)
    mlp_walk.hop()
    meet((mlp_walk,))
    placed = mlp_matrices.start(mlp_walk.found)
    mlp_walk.hop()
    *mlp_matrices.placed, = meet((mlp_walk,), *placed)
    w_up, w_down = mlp_matrices.finish(mlp_walk.found[-1:])
    arrived = []
    piece = row_count // 2
    for low in range(0, row_count, piece):
        (top0,) = mlp_fwd(False, mid0[low : low + piece], small_mlp, w_up, w_down)
        arrived.append(lax.ppermute(top0, "section", NEXT_LAYER))
    entering = jnp.where(first_layer, x0, jnp.concatenate(arrived))

    mid, *saved = attn_fwd(True, entering, small_attn, w_attn, cosine, sine, query_tag, key_tag)
    top, z, slope = mlp_fwd(True, mid, small_mlp, w_up, w_down)

    def both_micro(attn_value, mlp_value):
        kept = by_core(attn_value, mlp_value)
        crossed = sibling(by_core(mlp_value, attn_value))
        return jnp.stack([by_core(kept, crossed), by_core(crossed, kept)])

    (back_mid,) = mlp_bwd(False, core_at, mid, cotangent, small_mlp, w_up, w_down, slope)
    (back_in,) = attn_bwd(False, entering, back_mid, small_attn, w_attn, cosine, sine, saved)
    arriving = jnp.where(first_layer, lax.ppermute(back_in, "section", PREV_LAYER), cotangent)
    outputs = both_micro(mid, top)
    arriving, outputs = tied((arriving, outputs))
    ut_attn, ut_mlp, o_t, z_t = turned_factors(entering, small_attn, mid, small_mlp, saved[5], z)

    grad_mid, mlp_rows, up_bias, up_kept, up_sent, down_kept, down_sent = mlp_bwd(
        True, core_at, mid, arriving, small_mlp, w_up, w_down, slope, ut_mlp, z_t, ring.size
    )
    met = (sibling(up_sent), sibling(down_sent))
    extra = (core_at, ut_attn, o_t, grid_pos)

    def attn_group(group, before):
        return list(
            attn_bwd(
                True, entering, grad_mid, small_attn, w_attn, cosine, sine, saved, extra, ring.size,
                group, group + 1, before, False,
            )
        )

    back = attn_group(0, None)
    *met, back[0] = tied(met + (back[0],))
    mlp_sum = RingSum(ring, joined_terms(((up_kept, met[0], True), (down_kept, met[1], False)), BIG_VMEM))
    for group in range(1, width // (4 * HD)):
        *mlp_sum.going, back[0] = tied(tuple(mlp_sum.going) + (back[0],))
        back = attn_group(group, back)
        *came, back[0] = tied(tuple(mlp_sum.hop()) + (back[0],))
        mlp_sum.add(came)
    du, attn_bias, turned, attn_kept, attn_sent = back
    *mlp_sum.going, attn_sent, du = tied(tuple(mlp_sum.going) + (attn_sent, du))
    grad_in, small_kept, small_sent = norm_bwd(
        core_at, entering, grad_mid, small_attn, du, attn_bias, turned, mlp_rows, up_bias
    )
    attn_met, small_met, grad_in = tied((sibling(attn_sent), sibling(small_sent), grad_in))
    attn_terms = joined_terms(((attn_kept, attn_met, True),), TERMS_VMEM)
    attn_sum = RingSum(ring, attn_terms, (small_kept, small_met))
    mlp_came = mlp_sum.hop()
    attn_came = attn_sum.hop()
    mlp_sum.add(mlp_came)
    waiting = tied(tuple(attn_came) + tuple(mlp_sum.going))
    attn_came, mlp_sum.going = waiting[:2], waiting[2:]
    mlp_came = mlp_sum.hop()
    attn_sum.add(attn_came)
    while attn_sum.done < reach:
        if mlp_sum.done < reach and attn_sum.done > 1:
            mlp_sum.add(mlp_came)
            waiting = tied(tuple(attn_came) + tuple(mlp_sum.going))
            attn_came, mlp_sum.going = waiting[:2], waiting[2:]
            mlp_came = mlp_sum.hop()
        if attn_sum.done > 1:
            attn_sum.add(attn_came)
        attn_came = attn_sum.hop()
    while mlp_sum.done < reach:
        mlp_sum.add(mlp_came)
        mlp_came = mlp_sum.hop()
    (mlp_share,) = mlp_sum.close(mlp_came)
    attn_share, small_sum = attn_sum.close(attn_came)
    mlp_share = mlp_share.reshape(4, in_rows, width)
    attn_share = attn_share.reshape(2, in_rows, width)
    small_grad = small_sum[:7]
    up_share, down_share = mlp_share[:2], mlp_share[2:]

    step_rate = RATE / math.sqrt(lax.axis_size("dp") * micro_count * row_count)
    down_crossed = lax.ppermute(down_share.astype(BF16), "section", FROM_ATTN).astype(F32)
    share_out = jnp.where(first_core, 0.0, jnp.concatenate([down_crossed, down_share]).reshape(4 * in_rows, width))
    out_new = advance(out_master[0], out_moment[0], out_average[0], share_out, step_rate)
    crossed = sibling(by_core(up_share, attn_share).astype(BF16))
    in_new = advance_blocks(
        core_at, attn_share, up_share, crossed, in_master[0], in_moment[0], in_average[0], step_rate
    )
    small_new = advance(small_own, small_moment[0], small_average[0], small_grad, step_rate)
    branch_bias = by_core(small_grad[5], small_grad[6])

    input_grads = both_micro(grad_in, grad_mid)
    return tuple(
        value[None]
        for value in (outputs, input_grads, *in_new, *out_new, *small_new, branch_bias)
    )


def solution(mesh):
    rows = P(None, "dp", None)
    slots = P(None, "dp")
    matrix = P("section", "dp", None)
    vectors = P("section", None, None)
    return jax.shard_map(
        on_device,
        mesh=mesh,
        in_specs=(rows,) * 2 + (slots,) * 4 + (matrix,) * 6 + (vectors,) * 3,
        out_specs=(P("section", None, "dp", None),) * 2 + (matrix,) * 6 + (vectors,) * 3 + (P("section", None),),
        check_vma=False,
    )
```

```python
import functools
import math

import jax
import jax.numpy as jnp
from jax import lax
from jax.experimental import pallas as pl
from jax.experimental.pallas import tpu as pltpu
from jax.sharding import PartitionSpec as P

F32 = jnp.float32
BF16 = jnp.bfloat16
HD = 64
NORM_EPS = 1e-06
SQRT_HALF = 0.7071067811865476
INV_ROOT_TAU = 0.3989422804014327
LOG2E = 1.4426950408889634
BIG_VMEM = 50 * 1024 * 1024
MIDDLE_VMEM = 34 * 1024 * 1024
PIECE_VMEM = 50 * 1024 * 1024
SMALL_VMEM = 14 * 1024 * 1024
TERMS_VMEM = 32 * 1024 * 1024


def dot(lhs, rhs):
    return jnp.dot(lhs, rhs, preferred_element_type=F32)


def dot_t(lhs, rhs):
    return lax.dot_general(lhs, rhs, (((1,), (1,)), ((), ())), preferred_element_type=F32)


def tdot(lhs, rhs):
    return lax.dot_general(lhs, rhs, (((0,), (0,)), ((), ())), preferred_element_type=F32)


def normalize(stream):
    mean = jnp.mean(stream, axis=-1, keepdims=True)
    centered = stream - mean
    inverse = lax.rsqrt(jnp.mean(centered * centered, axis=-1, keepdims=True) + NORM_EPS)
    return centered * inverse, inverse


def lane_index(width):
    return lax.broadcasted_iota(jnp.int32, (1, width), 1)


def swap_halves(value):
    width = value.shape[1]
    first = (lane_index(width) % HD) < HD // 2
    return jnp.where(
        first, pltpu.roll(value, width - HD // 2, 1), pltpu.roll(value, HD // 2, 1)
    )


def attn_fwd_kernel(
    save, first, final, x_ref, small_ref, wq_ref, wk_ref, wv_ref, wo_ref, cos_ref, sin_ref, qe_ref, ke_ref, bq_ref, bk_ref, bv_ref, *rest
):
    if not first:
        before_ref, rest = rest[0], rest[1:]
    y_ref, rest = rest[0], rest[1:]
    if save:
        q_out, k_out, v_out, e_out, linv_out, o_out, u_s, acc = rest
    else:
        u_s, acc = rest
    step = pl.program_id(0)
    last = pl.num_programs(0) - 1

    @pl.when(step == 0)
    def _():
        stream = x_ref[...].astype(F32)
        normed, _ = normalize(stream)
        u_s[...] = (normed * small_ref[0:1] + small_ref[1:2]).astype(BF16)
        acc[...] = stream + small_ref[5:6] if first else before_ref[...]

    lowered = u_s[...]
    cosine, sine = cos_ref[...], sin_ref[...]

    def turn(value):
        return (value * cosine + swap_halves(value) * sine).astype(BF16)

    q = turn(dot(lowered, wq_ref[...]) + bq_ref[...])
    k = turn(dot(lowered, wk_ref[...]) + bk_ref[...])
    v = (dot(lowered, wv_ref[...]) + bv_ref[...]).astype(BF16)
    if save:
        q_out[...] = q
        k_out[...] = k
        v_out[...] = v
    low_lane = lane_index(2 * HD) < HD
    scale = HD ** (-0.5) * LOG2E
    qe, ke = qe_ref[...], ke_ref[...]
    mixed = []
    for pair in range(q.shape[1] // (2 * HD)):
        lanes = slice(pair * 2 * HD, (pair + 1) * 2 * HD)
        qp, kp, vp = q[:, lanes], k[:, lanes], v[:, lanes]
        qcat = jnp.concatenate([qp, qe], axis=1)
        sums = []
        for half in range(2):
            mine = low_lane if half == 0 else jnp.logical_not(low_lane)
            kcat = jnp.concatenate([jnp.where(mine, kp, jnp.zeros_like(kp)), ke], axis=1)
            scores = dot_t(qcat, kcat)
            top = jnp.max(scores, axis=-1, keepdims=True)
            e = jnp.exp2((scores - top) * scale).astype(BF16)
            if save:
                e_out[pair * 2 + half] = e
            sums.append(dot(e, jnp.where(mine, vp, jnp.ones_like(vp))))
        value = jnp.where(low_lane, sums[0], sums[1])
        total = pltpu.roll(jnp.where(low_lane, sums[1], sums[0]), HD, 1)
        inverse = 1.0 / total
        o = value * inverse
        if save:
            linv_out[:, lanes] = inverse
            o_out[:, lanes] = o
        mixed.append(o.astype(BF16))
    acc[...] += dot(jnp.concatenate(mixed, axis=1), wo_ref[...])

    @pl.when(step == last)
    def _():
        y_ref[...] = acc[...].astype(y_ref.dtype)


def attn_fwd(save, x, small, w, cos, sin, qe, ke, low=0, high=None, before=None):
    rows, width = x.shape
    group = 4 * HD
    steps = width // group
    high = steps if high is None else high
    first, final = low == 0, high == steps
    whole = pl.BlockSpec((rows, width), lambda g: (0, 0))
    part = pl.BlockSpec((rows, group), lambda g: (0, low + g))
    enc = pl.BlockSpec((rows, 128), lambda g: (0, 0))

    def wcol(base):
        return pl.BlockSpec((None, width, group), lambda g, base=base: (base, 0, low + g))

    def bias(row):
        return pl.BlockSpec((1, group), lambda g, row=row: (0, row * steps + low + g))

    flat = small[2:6].reshape(1, 4 * width)
    heads = width // HD
    out_shape = [jax.ShapeDtypeStruct((rows, width), BF16 if final else F32)]
    out_specs = [whole]
    if save:
        out_shape += [jax.ShapeDtypeStruct((rows, width), BF16)] * 3
        out_shape += [jax.ShapeDtypeStruct((heads, rows, rows), BF16)]
        out_shape += [jax.ShapeDtypeStruct((rows, width), F32)] * 2
        out_specs += [part] * 3 + [pl.BlockSpec((4, rows, rows), lambda g: (g, 0, 0))] + [part] * 2
    return pl.pallas_call(
        functools.partial(attn_fwd_kernel, save, first, final),
        grid=(high - low,),
        in_specs=[
            whole,
            pl.BlockSpec((7, width), lambda g: (0, 0)),
            wcol(0), wcol(1), wcol(2),
            pl.BlockSpec((None, group, width), lambda g: (3, low + g, 0)),
            part, part, enc, enc,
            bias(0), bias(1), bias(2),
        ]
        + ([] if first else [whole]),
        out_specs=out_specs,
        out_shape=out_shape,
        scratch_shapes=[pltpu.VMEM((rows, width), BF16), pltpu.VMEM((rows, width), F32)],
        compiler_params=pltpu.CompilerParams(vmem_limit_bytes=BIG_VMEM if save else MIDDLE_VMEM),
        cost_estimate=pl.CostEstimate(
            flops=2 * rows * width * 4 * width + 4 * 4 * rows * rows * width,
            bytes_accessed=8 * width * width + 4 * rows * width,
            transcendentals=heads * rows * rows,
        ),
        name="attn_fwd",
    )(x, small, w, w, w, w, cos, sin, qe, ke, flat, flat, flat, *([] if first else [before]))


def mlp_fwd_kernel(save, x_ref, small_ref, bias_ref, wi_ref, wo_ref, y_ref, *rest):
    if save:
        z_out, slope_out, u_s, acc = rest
    else:
        u_s, acc = rest
    step = pl.program_id(0)

    @pl.when(step == 0)
    def _():
        stream = x_ref[...].astype(F32)
        normed, _ = normalize(stream)
        u_s[...] = (normed * small_ref[0:1] + small_ref[1:2]).astype(BF16)
        acc[...] = stream + small_ref[6:7]

    a = dot(u_s[...], wi_ref[...]) + bias_ref[...]
    phi = 0.5 + 0.5 * lax.erf(a * SQRT_HALF)
    z = (a * phi).astype(BF16)
    if save:
        z_out[...] = z
        slope_out[...] = (phi + a * jnp.exp2(a * a * (-0.5 * LOG2E)) * INV_ROOT_TAU).astype(BF16)
    acc[...] += dot(z, wo_ref[...])

    @pl.when(step == pl.num_programs(0) - 1)
    def _():
        y_ref[...] = acc[...].astype(BF16)


def mlp_fwd(save, x, small, wi, wo, tile=768):
    rows, width = x.shape
    hidden = wi.shape[0] * wi.shape[2]
    per_block = width // tile
    steps = hidden // tile
    whole = pl.BlockSpec((rows, width), lambda g: (0, 0))
    part = pl.BlockSpec((rows, tile), lambda g: (0, g))
    out_shape = [jax.ShapeDtypeStruct((rows, width), BF16)]
    out_specs = [whole]
    if save:
        out_shape += [jax.ShapeDtypeStruct((rows, hidden), BF16)] * 2
        out_specs += [part] * 2
    return pl.pallas_call(
        functools.partial(mlp_fwd_kernel, save),
        grid=(steps,),
        in_specs=[
            whole,
            pl.BlockSpec((7, width), lambda g: (0, 0)),
            pl.BlockSpec((1, tile), lambda g: (0, g)),
            pl.BlockSpec((None, width, tile), lambda g: (g // per_block, 0, g % per_block)),
            pl.BlockSpec((tile, width), lambda g: (g, 0)),
        ],
        out_specs=out_specs,
        out_shape=out_shape,
        scratch_shapes=[pltpu.VMEM((rows, width), BF16), pltpu.VMEM((rows, width), F32)],
        compiler_params=pltpu.CompilerParams(vmem_limit_bytes=BIG_VMEM if save else MIDDLE_VMEM),
        cost_estimate=pl.CostEstimate(
            flops=4 * rows * width * hidden,
            bytes_accessed=4 * width * hidden + 4 * rows * width,
            transcendentals=2 * rows * hidden,
        ),
        name="mlp_fwd",
    )(x, small, small[2:6].reshape(1, hidden), wi, wo)


def norm_back(full, x_ref, gy_ref, small_ref, du, gx_ref, rows_ref):
    normed, inverse = normalize(x_ref[...].astype(F32))
    scaled = du * small_ref[0:1]
    inner = (
        scaled
        - jnp.mean(scaled, axis=-1, keepdims=True)
        - normed * jnp.mean(scaled * normed, axis=-1, keepdims=True)
    )
    gy = gy_ref[...].astype(F32)
    gx_ref[...] = (gy + inverse * inner).astype(BF16)
    if full:
        rows_ref[0:1] = jnp.sum(du * normed, axis=0, keepdims=True)
        rows_ref[1:2] = jnp.sum(du, axis=0, keepdims=True)
        rows_ref[2:3] = jnp.sum(gy, axis=0, keepdims=True)


def turn_kernel(x_ref, small_ref, mid_ref, small_mid_ref, o_ref, z_ref, ut_ref, ut_mid_ref, ot_ref, zt_ref):
    for source, small, target in ((x_ref, small_ref, ut_ref), (mid_ref, small_mid_ref, ut_mid_ref)):
        normed, _ = normalize(source[...].astype(F32))
        target[...] = (normed * small[0:1] + small[1:2]).astype(BF16).T
    ot_ref[...] = o_ref[...].astype(BF16).T
    width = x_ref.shape[1]
    for block in range(z_ref.shape[1] // width):
        zt_ref[block * width : (block + 1) * width, :] = z_ref[:, block * width : (block + 1) * width].T


def turned_factors(x, small, mid, small_mid, o, z):
    rows, width = x.shape
    vmem = pl.BlockSpec(memory_space=pltpu.VMEM)
    return pl.pallas_call(
        turn_kernel,
        in_specs=[vmem] * 6,
        out_specs=[vmem] * 4,
        out_shape=[jax.ShapeDtypeStruct((width, rows), BF16)] * 3
        + [jax.ShapeDtypeStruct((z.shape[1], rows), BF16)],
        compiler_params=pltpu.CompilerParams(vmem_limit_bytes=SMALL_VMEM),
        cost_estimate=pl.CostEstimate(
            flops=40 * rows * width, bytes_accessed=40 * rows * width, transcendentals=0
        ),
        name="turned_factors",
    )(x, small, mid, small_mid, o, z)


def mlp_bwd_kernel(
    full, core_ref, x_ref, gy_ref, small_ref, wi_ref, wo_ref, slope_ref, *rest
):
    if full:
        ut_ref, zt_ref, gx_ref, rows_ref, bias_ref, up_kept, up_sent, down_kept, down_sent, du_s = rest
    else:
        gx_ref, du_s = rest
        rows_ref = None
    step = pl.program_id(0)

    @pl.when(step == 0)
    def _():
        du_s[...] = jnp.zeros_like(du_s)

    gy = gy_ref[...]
    dz = dot_t(gy, wo_ref[...])
    da = (dz * slope_ref[...].astype(F32)).astype(BF16)
    du_s[...] += dot_t(da, wi_ref[...])
    if full:
        first_core = core_ref[0] == 0
        bias_ref[...] = jnp.sum(da.astype(F32), axis=0, keepdims=True)
        members, share = up_kept.shape[1:3]
        d_up = dot(ut_ref[...], da).reshape(members, share, da.shape[1]).astype(BF16)

        @pl.when(step < pl.num_programs(0) // 2)
        def _():
            up_sent[0] = d_up

        @pl.when(step >= pl.num_programs(0) // 2)
        def _():
            up_kept[0] = d_up

        d_down = dot(zt_ref[...], gy)
        for member in range(down_kept.shape[0]):
            for block in range(2):
                low = (member * 4 + block) * share
                one = d_down[low : low + share]
                two = d_down[low + 2 * share : low + 3 * share]
                down_kept[member, block] = jnp.where(first_core, one, two).astype(BF16)
                down_sent[member, block] = jnp.where(first_core, two, one).astype(BF16)

    @pl.when(step == pl.num_programs(0) - 1)
    def _():
        norm_back(full, x_ref, gy_ref, small_ref, du_s[...], gx_ref, rows_ref)


def mlp_bwd(full, core, x, gy, small, wi, wo, slope, ut=None, zt=None, members=None):
    rows, width = x.shape
    blocks = wi.shape[0]
    hidden = blocks * width
    half = blocks // 2

    def block_of(g, core_ref):
        return jnp.where(g < half, (1 - core_ref[0]) * half + g, core_ref[0] * half + g - half)

    whole = pl.BlockSpec((rows, width), lambda g, c: (0, 0))
    part = pl.BlockSpec((rows, width), lambda g, c: (0, block_of(g, c)))
    in_specs = [
        whole, whole,
        pl.BlockSpec((7, width), lambda g, c: (0, 0)),
        pl.BlockSpec((None, width, width), lambda g, c: (block_of(g, c), 0, 0)),
        pl.BlockSpec((width, width), lambda g, c: (block_of(g, c), 0)),
        part,
    ]
    operands = [x, gy, small, wi, wo, slope]
    out_shape = [jax.ShapeDtypeStruct((rows, width), BF16)]
    out_specs = [whole]
    if full:
        share = width // members
        operands += [ut, zt]
        in_specs += [
            pl.BlockSpec((width, rows), lambda g, c: (0, 0)),
            pl.BlockSpec((width, rows), lambda g, c: (block_of(g, c), 0)),
        ]
        out_shape += [
            jax.ShapeDtypeStruct((8, width), F32),
            jax.ShapeDtypeStruct((1, hidden), F32),
        ]
        out_shape += [jax.ShapeDtypeStruct((2, members, share, width), BF16)] * 2
        out_shape += [jax.ShapeDtypeStruct((members, 2, share, width), BF16)] * 2
        up_block = (1, members, share, width)
        down = pl.BlockSpec(
            (members // blocks, 2, share, width), lambda g, c: (block_of(g, c), 0, 0, 0)
        )
        out_specs += [
            pl.BlockSpec((8, width), lambda g, c: (0, 0)),
            pl.BlockSpec((1, width), lambda g, c: (0, block_of(g, c))),
            pl.BlockSpec(up_block, lambda g, c: (jnp.maximum(g - half, 0), 0, 0, 0)),
            pl.BlockSpec(up_block, lambda g, c: (jnp.minimum(g, half - 1), 0, 0, 0)),
            down, down,
        ]
    return pl.pallas_call(
        functools.partial(mlp_bwd_kernel, full),
        grid_spec=pltpu.PrefetchScalarGridSpec(
            num_scalar_prefetch=1,
            grid=(blocks,),
            in_specs=in_specs,
            out_specs=out_specs,
            scratch_shapes=[pltpu.VMEM((rows, width), F32)],
        ),
        out_shape=out_shape,
        compiler_params=pltpu.CompilerParams(vmem_limit_bytes=BIG_VMEM),
        cost_estimate=pl.CostEstimate(
            flops=(8 if full else 4) * rows * width * hidden,
            bytes_accessed=(8 if full else 4) * width * hidden + 6 * rows * width + 4 * rows * hidden,
            transcendentals=0,
        ),
        name="mlp_bwd_full" if full else "mlp_bwd_act",
    )(core, *operands)


def norm_kernel(
    core_ref, x_ref, gy_ref, small_ref, du_ref, bias_ref, turned_ref, mlp_rows_ref, up_bias_ref,
    gx_ref, kept_ref, sent_ref, rows_ref
):
    norm_back(True, x_ref, gy_ref, small_ref, du_ref[...], gx_ref, rows_ref)
    width = x_ref.shape[1]
    across, along = turned_ref[0:1], turned_ref[1:2]
    first = (lane_index(width) % HD) < HD // 2
    frequency = jnp.where(
        first,
        pltpu.roll(across, width - HD // 2, 1) - across,
        along - pltpu.roll(along, HD // 2, 1),
    )
    attn = [rows_ref[0:1], rows_ref[1:2], bias_ref[0:1], bias_ref[1:2], bias_ref[2:3], rows_ref[2:3], frequency]
    mlp = [mlp_rows_ref[0:1], mlp_rows_ref[1:2]]
    mlp += [up_bias_ref[0:1, i * width : (i + 1) * width] for i in range(4)]
    mlp += [mlp_rows_ref[2:3]]
    first_core = core_ref[0] == 0
    kept_ref[7:8] = jnp.zeros_like(across)
    sent_ref[7:8] = jnp.zeros_like(across)
    for row, (one, two) in enumerate(zip(attn, mlp)):
        kept_ref[row : row + 1] = jnp.where(first_core, one, two)
        sent_ref[row : row + 1] = jnp.where(first_core, two, one)


def norm_bwd(core, x, gy, small, du, attn_bias, turned, mlp_rows, up_bias):
    rows, width = x.shape
    vmem = pl.BlockSpec(memory_space=pltpu.VMEM)
    return pl.pallas_call(
        norm_kernel,
        in_specs=[pl.BlockSpec(memory_space=pltpu.SMEM)] + [vmem] * 8,
        out_specs=[vmem] * 3,
        out_shape=[jax.ShapeDtypeStruct((rows, width), BF16)]
        + [jax.ShapeDtypeStruct((8, width), F32)] * 2,
        scratch_shapes=[pltpu.VMEM((8, width), F32)],
        compiler_params=pltpu.CompilerParams(vmem_limit_bytes=SMALL_VMEM),
        cost_estimate=pl.CostEstimate(
            flops=30 * rows * width, bytes_accessed=10 * rows * width, transcendentals=0
        ),
        name="norm_bwd",
    )(core, x, gy, small, du, attn_bias, turned, mlp_rows, up_bias)


def attn_bwd_kernel(full, first, final, low, *refs):
    names = ["x", "gy", "small", "wq", "wk", "wv", "wo", "cos", "sin", "q", "k", "v", "e", "linv", "o"]
    if full:
        names += ["core", "gy_part", "ut", "ot", "grid"]
    names += [] if first else ["before"]
    ref = dict(zip(names, refs))
    rest = refs[len(names) :]
    if full and not first:
        rest = rest[4:]
    out_ref, rest = rest[0], rest[1:]
    rows_ref = None
    if full:
        bias_ref, angle_ref, kept_ref, sent_ref = rest[:4]
        rest = rest[4:]
        if final:
            rows_ref, rest = rest[0], rest[1:]
    du_s, rest = rest[0], rest[1:]
    step = pl.program_id(0)
    copies = {}
    if full:
        semaphores, scratch = rest[-1], rest[:-1]
        group = ref["gy_part"].shape[1]
        lanes = pl.ds(low * group, group)
        source = {
            "cos": ref["cos"].at[:, lanes],
            "sin": ref["sin"].at[:, lanes],
            "wq": ref["wq"].at[0, :, lanes],
            "wk": ref["wk"].at[1, :, lanes],
            "wv": ref["wv"].at[2, :, lanes],
            "ut": ref["ut"],
            "ot": ref["ot"],
        }
        if not first:
            source["before"] = ref["before"]
        number = 0
        for name, target in zip(source, scratch):
            ref[name] = target
            copies[name] = [pltpu.make_async_copy(source[name], target, semaphores.at[number])]
            number += 1
        for group_of in copies.values():
            for copy in group_of:
                copy.start()

    def held(name, head=None):
        if name in copies:
            waiting = copies[name] if head is None else copies[name][head : head + 1]
            for copy in waiting:
                copy.wait()
            if head is None:
                del copies[name]
        return ref[name] if head is None else ref[name][head]

    if not full:

        @pl.when(step == 0)
        def _():
            du_s[...] = jnp.zeros_like(du_s) if first else ref["before"][...]

    gy = ref["gy"][...]
    width = ref["gy_part"].shape[1] if full else ref["q"].shape[1]
    scale = HD ** (-0.5)
    low_lane = lane_index(2 * HD) < HD
    do_all = dot_t(gy, ref["wo"][...])
    o_all = held("o")[...]
    dos_all = (do_all * held("linv")[...]).astype(BF16)
    q_all, k_all, v_all = held("q")[...], held("k")[...], held("v")[...]
    parts = []
    for pair in range(width // (2 * HD)):
        lanes = slice(pair * 2 * HD, (pair + 1) * 2 * HD)
        qp, kp, vp = q_all[:, lanes], k_all[:, lanes], v_all[:, lanes]
        dos = dos_all[:, lanes]
        product = dos.astype(F32) * o_all[:, lanes]
        zero = jnp.zeros_like(qp)
        dq = dk = dv = 0.0
        for half in range(2):
            mine = low_lane if half == 0 else jnp.logical_not(low_lane)
            offset = jnp.sum(jnp.where(mine, product, 0.0), axis=-1, keepdims=True)
            dos_h = jnp.where(mine, dos, zero)
            e = held("e", pair * 2 + half)
            dp = dot_t(dos_h, vp)
            ds = (e.astype(F32) * (dp - offset)).astype(BF16)
            dv = dv + tdot(e, dos_h)
            dq = dq + dot(ds, jnp.where(mine, kp, zero))
            dk = dk + tdot(ds, jnp.where(mine, qp, zero))
        parts.append((dq * scale, dk * scale, dv))
    dqr = jnp.concatenate([p[0] for p in parts], axis=1)
    dkr = jnp.concatenate([p[1] for p in parts], axis=1)
    dv = jnp.concatenate([p[2] for p in parts], axis=1).astype(BF16)
    for name in list(copies):
        held(name)
    cosine, sine = held("cos")[...], held("sin")[...]
    dq = (dqr * cosine - swap_halves(dqr) * sine).astype(BF16)
    dk = (dkr * cosine - swap_halves(dkr) * sine).astype(BF16)
    du = dot_t(dq, held("wq")[...]) + dot_t(dk, held("wk")[...]) + dot_t(dv, held("wv")[...])
    if not full:
        du_s[...] += du
    elif first:
        du_s[...] = du
    else:
        du_s[...] = held("before")[...] + du
    if full:
        turned = dqr * swap_halves(q_all.astype(F32)) + dkr * swap_halves(k_all.astype(F32))
        angle_ref[0:1] = jnp.sum(turned * ref["grid"][:, 0:1], axis=0, keepdims=True)
        angle_ref[1:2] = jnp.sum(turned * ref["grid"][:, 1:2], axis=0, keepdims=True)
        bias_ref[0:1] = jnp.sum(dq.astype(F32), axis=0, keepdims=True)
        bias_ref[1:2] = jnp.sum(dk.astype(F32), axis=0, keepdims=True)
        bias_ref[2:3] = jnp.sum(dv.astype(F32), axis=0, keepdims=True)
        first_core = ref["core"][0] == 0
        members, share = kept_ref.shape[1:3]
        ut = held("ut")[...]
        pairs = (
            (dot(ut, dq), dot(ut, dv)),
            (dot(ut, dk), dot(held("ot")[...], ref["gy_part"][...])),
        )
        for block, (one, two) in enumerate(pairs):
            one = one.reshape(members, share, width)
            two = two.reshape(members, share, width)
            kept_ref[block] = jnp.where(first_core, one, two).astype(BF16)
            sent_ref[block] = jnp.where(first_core, two, one).astype(BF16)

    @pl.when(step == pl.num_programs(0) - 1)
    def _():
        if final:
            norm_back(full, ref["x"], ref["gy"], ref["small"], du_s[...], out_ref, rows_ref)
        else:
            out_ref[...] = du_s[...]


def attn_bwd(full, x, gy, small, w, cos, sin, saved, extra=None, members=None, low=0, high=None, before=None, close=True):
    rows, width = x.shape
    group = 4 * HD
    groups = width // group
    high = groups if high is None else high
    first, final = low == 0, close and high == groups
    heads = width // HD
    whole = pl.BlockSpec((rows, width), lambda g: (0, 0))
    part = pl.BlockSpec((rows, group), lambda g: (0, low + g))

    def wcol(base):
        return pl.BlockSpec((None, width, group), lambda g, base=base: (base, 0, low + g))

    strip = pl.BlockSpec((8, group), lambda g: (0, low + g))
    out_shape = [jax.ShapeDtypeStruct((rows, width), BF16 if final else F32)]
    out_specs = [whole]
    q, k, v, e, linv, o = saved
    operands = [x, gy, small, w, w, w, w, cos, sin, q, k, v, e, linv, o]
    in_specs = [
        whole if final else pl.BlockSpec(memory_space=pl.ANY), whole,
        pl.BlockSpec((7, width), lambda g: (0, 0)),
        wcol(0), wcol(1), wcol(2),
        pl.BlockSpec((None, group, width), lambda g: (3, low + g, 0)),
        part, part, part, part, part,
        pl.BlockSpec((4, rows, rows), lambda g: (low + g, 0, 0)),
        part, part,
    ]
    if full:
        anywhere = pl.BlockSpec(memory_space=pl.ANY)
        for at in (3, 4, 5, 7, 8):
            in_specs[at] = anywhere
        core, ut, ot, grid_pos = extra
        operands += [core, gy, ut, ot, grid_pos]
        in_specs += [
            pl.BlockSpec(memory_space=pltpu.SMEM), part, anywhere, anywhere,
            pl.BlockSpec((rows, 128), lambda g: (0, 0)),
        ]
        share = width // members
        out_shape += [jax.ShapeDtypeStruct((8, width), F32)] * 2
        out_shape += [jax.ShapeDtypeStruct((2, members, share, width), BF16)] * 2
        out_specs += [strip, strip]
        out_specs += [pl.BlockSpec((2, members, share, group), lambda g: (0, 0, 0, low + g))] * 2
        if final:
            out_shape += [jax.ShapeDtypeStruct((8, width), F32)]
            out_specs += [pl.BlockSpec((8, width), lambda g: (0, 0))]
    aliases = {}
    if not first:
        if full:
            aliases = {len(operands) + 1 + i: 1 + i for i in range(4)}
        operands += list(before[: 5 if full else 1])
        in_specs += [pl.BlockSpec(memory_space=pl.ANY)] * 5 if full else [whole]
    portion = (high - low) / groups
    scratch = [pltpu.VMEM((rows, width), F32)]
    if full:
        scratch += [pltpu.VMEM((rows, group), F32)] * 2
        scratch += [pltpu.VMEM((width, group), BF16)] * 3 + [pltpu.VMEM((width, rows), BF16)] * 2
        scratch += [] if first else [pltpu.VMEM((rows, width), F32)]
        scratch += [pltpu.SemaphoreType.DMA((len(scratch) - 1,))]
    return pl.pallas_call(
        functools.partial(attn_bwd_kernel, full, first, final, low),
        grid=(high - low,),
        in_specs=in_specs,
        out_specs=out_specs,
        out_shape=out_shape,
        scratch_shapes=scratch,
        input_output_aliases=aliases,
        compiler_params=pltpu.CompilerParams(vmem_limit_bytes=PIECE_VMEM if full else BIG_VMEM),
        cost_estimate=pl.CostEstimate(
            flops=int(portion * ((16 if full else 8) * rows * width * width + 64 * rows * rows * width)),
            bytes_accessed=int(portion * ((16 if full else 8) * width * width + 30 * rows * width + 2 * heads * rows * rows)),
            transcendentals=0,
        ),
        name="attn_bwd_full" if full else "attn_bwd_act",
    )(*operands)


SMALL_ROWS = 16


def terms_kernel(first_dims, *refs):
    out = refs[-1]
    share = refs[0].shape[2]
    for member in range(out.shape[0]):
        row = 0
        for kept, met, first in zip(refs[0:-1:2], refs[1:-1:2], first_dims):
            for block in range(2):
                at = (block, member) if first else (member, block)
                total = kept[at].astype(F32) + met[at].astype(F32)
                out[member, row : row + share] = total.astype(BF16)
                row += share


def joined_terms(sums, vmem):
    operands, in_specs = [], []
    for kept, met, first in sums:
        share, width = kept.shape[2:]
        members = kept.shape[1] if first else kept.shape[0]
        if first:
            spec = pl.BlockSpec((2, members // 2, share, width), lambda m: (0, m, 0, 0))
        else:
            spec = pl.BlockSpec((members // 2, 2, share, width), lambda m: (m, 0, 0, 0))
        operands += [kept, met]
        in_specs += [spec, spec]
    rows = 2 * len(sums) * share
    return pl.pallas_call(
        functools.partial(terms_kernel, tuple(item[2] for item in sums)),
        grid=(2,),
        in_specs=in_specs,
        out_specs=pl.BlockSpec((members // 2, rows, width), lambda m: (m, 0, 0)),
        out_shape=jax.ShapeDtypeStruct((members, rows, width), BF16),
        compiler_params=pltpu.CompilerParams(vmem_limit_bytes=vmem),
        cost_estimate=pl.CostEstimate(
            flops=members * rows * width, bytes_accessed=6 * members * rows * width, transcendentals=0
        ),
        name="joined_terms",
    )(*operands)


def unpacked(value):
    half = SMALL_ROWS // 2
    return value[:half].astype(F32) + value[half:].astype(F32)


def ring_sum_kernel(kind, extra, members_ref, *refs):
    if kind == "open":
        term, refs = refs[0], refs[1:]
        if extra:
            kept, met, right_ref, left_ref, small_out = refs
            small = kept[...] + met[...]
            small_out[...] = small
            high = small.astype(BF16)
            packed = jnp.concatenate([high.astype(F32), small - high.astype(F32)], axis=0).astype(BF16)
            right_ref[-extra:] = packed
            left_ref[-extra:] = packed
        else:
            right_ref, left_ref = refs
        middle = right_ref.shape[0] - extra
        right_ref[:middle] = term[0, :middle]
        left_ref[:middle] = term[0, middle:]
        return
    sides = 1 if kind == "close" else 2
    terms, refs = refs[:sides], refs[sides:]
    came, refs = refs[:2], refs[2:]
    if extra:
        small_in, refs = refs[0], refs[1:]
        small_out, refs = refs[-1], refs[:-1]
        small = small_in[...] + unpacked(came[0][-extra:])
        if kind != "close":
            small = small + unpacked(came[1][-extra:])
        small_out[...] = small
    rows = terms[0].shape[1]
    if kind == "close":
        refs[0][...] = terms[0][0].astype(F32) + came[0][:rows].astype(F32) + came[1][:rows].astype(F32)
        return
    middle = rows // 2
    for side in range(2):
        term, out = terms[side], refs[side]
        if kind == "later":
            out[:rows] = (term[0].astype(F32) + came[side][:rows].astype(F32)).astype(BF16)
        else:
            near = slice(0, middle) if side == 0 else slice(middle, rows)
            far = slice(middle, rows) if side == 0 else slice(0, middle)
            out[near] = (term[0, near].astype(F32) + came[side][:middle].astype(F32)).astype(BF16)
            out[far] = term[0, far]
        if extra:
            out[rows:] = came[side][-extra:]


class RingSum:
    def __init__(self, ring, terms, small=()):
        self.ring, self.terms = ring, terms
        self.reach = ring.size // 2
        self.done = 0
        self.extra = SMALL_ROWS if small else 0
        self.keep(self.call("open", (self.reach,), *small))

    def keep(self, results):
        self.going = tuple(results[:2])
        if self.extra:
            self.small = results[2]

    def call(self, kind, offsets, *values):
        rows, width = self.terms.shape[1:]
        operands, in_specs = [], []
        for offset in offsets:
            at = offset % self.ring.size
            operands.append(self.terms)
            in_specs.append(pl.BlockSpec((1, rows, width), lambda g, m, at=at: (m[at], 0, 0)))
        values = list(values)
        if self.extra and kind != "open":
            values.append(self.small)
        for value in values:
            operands.append(value)
            in_specs.append(pl.BlockSpec(value.shape, lambda g, m: (0, 0)))
        if kind == "open":
            shapes = [jax.ShapeDtypeStruct((rows // 2 + self.extra, width), BF16)] * 2
        elif kind == "close":
            shapes = [jax.ShapeDtypeStruct((rows, width), F32)]
        else:
            shapes = [jax.ShapeDtypeStruct((rows + self.extra, width), BF16)] * 2
        if self.extra:
            shapes.append(jax.ShapeDtypeStruct((SMALL_ROWS // 2, width), F32))
        return pl.pallas_call(
            functools.partial(ring_sum_kernel, kind, self.extra),
            grid_spec=pltpu.PrefetchScalarGridSpec(
                num_scalar_prefetch=1,
                grid=(1,),
                in_specs=in_specs,
                out_specs=[pl.BlockSpec(s.shape, lambda g, m: (0, 0)) for s in shapes],
            ),
            out_shape=shapes,
            compiler_params=pltpu.CompilerParams(vmem_limit_bytes=SMALL_VMEM),
            cost_estimate=pl.CostEstimate(
                flops=2 * rows * width, bytes_accessed=12 * rows * width, transcendentals=0
            ),
            name="ring_sum_" + kind,
        )(self.ring.members, *operands)

    def hop(self):
        self.came = (self.ring.to_right(self.going[0]), self.ring.to_left(self.going[1]))
        self.done += 1
        return self.came

    def add(self, came):
        left = self.reach - self.done
        self.keep(self.call("second" if self.done == 1 else "later", (left, -left), *came))

    def close(self, came):
        return self.call("close", (0,), *came)


def advance_kernel(rate, core_ref, attn_ref, up_ref, crossed_ref, master_ref, moment_ref, average_ref, *outs):
    step = pl.program_id(0)
    core = core_ref[0]
    own = jnp.where(core == 0, attn_ref[...], up_ref[...])
    gradient = jnp.where(step // 2 == core, own, crossed_ref[...].astype(F32))
    for out, value in zip(outs, advance(master_ref[...], moment_ref[...], average_ref[...], gradient, rate)):
        out[...] = value


def advance_blocks(core, attn, up, crossed, master, moment, average, rate):
    rows, columns = master.shape
    width = columns // 4
    block = pl.BlockSpec((None, rows, width), lambda g: (g % 2, 0, 0))
    part = pl.BlockSpec((rows, width), lambda g: (0, g))
    return pl.pallas_call(
        functools.partial(advance_kernel, rate),
        grid=(4,),
        in_specs=[pl.BlockSpec(memory_space=pltpu.SMEM)] + [block] * 3 + [part] * 3,
        out_specs=[part] * 3,
        out_shape=[jax.ShapeDtypeStruct(master.shape, F32)] * 3,
        compiler_params=pltpu.CompilerParams(vmem_limit_bytes=SMALL_VMEM),
        cost_estimate=pl.CostEstimate(
            flops=12 * rows * columns, bytes_accessed=32 * rows * columns, transcendentals=0
        ),
        name="advance_blocks",
    )(core, attn, up, crossed, master, moment, average)


NEXT_LAYER = ((0, 2), (1, 3))
PREV_LAYER = ((2, 0), (3, 1))
SIBLING = ((0, 1), (1, 0), (2, 3), (3, 2))
FROM_MLP = ((1, 0), (3, 2))
FROM_ATTN = ((0, 1), (2, 3))
MOMENTUM = 0.9
DECAY = 0.0001
AVERAGE = 0.8
RATE = 0.03
MASKED = -1e30


def sibling(value):
    return lax.ppermute(value, "section", SIBLING)


class Ring:
    def __init__(self, size):
        self.size = size
        order = list(range(0, size, 2)) + list(range(size - 1 - size % 2, 0, -2))
        place = {member: at for at, member in enumerate(order)}
        table = [[order[(place[m] + k) % size] for k in range(size)] for m in range(size)]
        self.members = lax.dynamic_index_in_dim(
            jnp.array(table, jnp.int32), lax.axis_index("dp"), 0, keepdims=False
        )
        self.right = [(order[i], order[(i + 1) % size]) for i in range(size)]
        self.left = [(b, a) for a, b in self.right]

    def member(self, offset):
        return self.members[offset % self.size]

    def to_right(self, value):
        return lax.ppermute(value, "dp", self.right)

    def to_left(self, value):
        return lax.ppermute(value, "dp", self.left)


tied = lax.optimization_barrier


class RingWalk:
    def __init__(self, ring, shard, split):
        self.ring = ring
        self.found = [(shard, 0, 0)]
        self.going = (shard, shard)
        self.done = 0
        self.split = split

    def hop(self):
        self.done += 1
        right, left = self.going
        if self.done < self.ring.size // 2:
            self.going = (self.ring.to_right(right), self.ring.to_left(left))
            self.found += [(self.going[0], -self.done, 0), (self.going[1], self.done, 0)]
        elif self.split:
            middle = right.shape[0] // 2
            self.going = (self.ring.to_right(right[:middle]), self.ring.to_left(left[middle:]))
            self.found += [(self.going[0], self.done, 0), (self.going[1], self.done, middle)]
        else:
            self.going = (self.ring.to_right(right),)
            self.found.append((self.going[0], self.done, 0))

    def renew(self, *going):
        self.going = going
        if self.done:
            count = len(going)
            self.found[-count:] = [(new,) + old[1:] for new, old in zip(going, self.found[-count:])]


def meet(walks, *others):
    out = tied(tuple(value for walk in walks for value in walk.going) + others)
    for walk in walks:
        count = len(walk.going)
        walk.renew(*out[:count])
        out = out[count:]
    return out


def place_spots(core, member, side, first, blocks):
    half = core if side == 0 else 1 - core
    for block in range(first, first + blocks):
        if block < 2:
            yield 0, (half * 2 + block, member)
        else:
            yield 1, (member, half * 2 + block - 2)


def place_kernel(layout, core_ref, members_ref, *refs):
    sources, targets = refs[: len(layout)], refs[len(layout) :]
    for source, (side, offset, first) in zip(sources, layout):
        spots = place_spots(core_ref[0], members_ref[offset], side, first, source.shape[0])
        for block, (matrix, spot) in enumerate(spots):
            targets[matrix][spot] = source[block]


def place_more_kernel(layout, count, core_ref, members_ref, *refs):
    sources = refs[: len(layout)]
    targets, semaphores = refs[len(layout) + count : len(layout) + 2 * count], refs[-1]
    copies = []
    for source, (side, offset, first) in zip(sources, layout):
        spots = place_spots(core_ref[0], members_ref[offset], side, first, source.shape[0])
        for block, (matrix, spot) in enumerate(spots):
            copies.append(
                pltpu.make_async_copy(
                    source.at[block], targets[matrix].at[spot], semaphores.at[len(copies)]
                )
            )
    for copy in copies:
        copy.start()
    for copy in copies:
        copy.wait()


class Matrices:
    def __init__(self, ring, core):
        self.ring, self.core = ring, core
        self.smem = pl.BlockSpec(memory_space=pltpu.SMEM)
        self.vmem = pl.BlockSpec(memory_space=pltpu.VMEM)

    def operands(self, found):
        arrays, layout = [], []
        for value, offset, first in found:
            for side, held in ((0, value), (1, sibling(value))):
                arrays.append(held)
                layout.append((side, offset % self.ring.size, first))
        return arrays, tuple(layout)

    def start(self, found):
        arrays, layout = self.operands(found)
        blocks, rows, width = arrays[0].shape
        shapes = [(4, self.ring.size, rows, width), (self.ring.size, 4, rows, width)][: blocks // 2]
        self.placed = pl.pallas_call(
            functools.partial(place_kernel, layout),
            in_specs=[self.smem] * 2 + [self.vmem] * len(arrays),
            out_specs=[self.vmem] * len(shapes),
            out_shape=[jax.ShapeDtypeStruct(shape, BF16) for shape in shapes],
            compiler_params=pltpu.CompilerParams(vmem_limit_bytes=SMALL_VMEM),
            cost_estimate=pl.CostEstimate(
                flops=0, bytes_accessed=8 * blocks * self.ring.size * rows * width, transcendentals=0
            ),
            name="place_weights",
        )(self.core, self.ring.members, *arrays)
        return tuple(self.placed)

    def finish(self, found):
        arrays, layout = self.operands(found)
        blocks, rows, width = arrays[0].shape
        count = len(self.placed)
        anywhere = pl.BlockSpec(memory_space=pl.ANY)
        first = 2 + len(arrays)
        placed = pl.pallas_call(
            functools.partial(place_more_kernel, layout, count),
            in_specs=[self.smem] * 2 + [self.vmem] * len(arrays) + [anywhere] * count,
            out_specs=[anywhere] * count,
            out_shape=[jax.ShapeDtypeStruct(value.shape, BF16) for value in self.placed],
            input_output_aliases={first + i: i for i in range(count)},
            scratch_shapes=[pltpu.SemaphoreType.DMA((sum(a.shape[0] for a in arrays),))],
            compiler_params=pltpu.CompilerParams(vmem_limit_bytes=SMALL_VMEM),
            cost_estimate=pl.CostEstimate(
                flops=0, bytes_accessed=8 * blocks * rows * width, transcendentals=0
            ),
            name="place_last",
        )(self.core, self.ring.members, *arrays, *self.placed)
        whole = [placed[0].reshape(4, self.ring.size * rows, width)]
        if count == 2:
            whole.append(placed[1].reshape(4 * self.ring.size * rows, width))
        return whole


def advance(master, moment, average, gradient, step_rate):
    gradient = gradient + DECAY * master
    moment = MOMENTUM * moment + gradient
    master = master - step_rate * (gradient + MOMENTUM * moment)
    average = AVERAGE * average + (1 - AVERAGE) * master
    return (moment, master, average)


def on_device(
    block_input, out_cotangent, segment_ids, grid_row, grid_col, valid_slot,
    in_master, out_master, in_moment, out_moment, in_average, out_average,
    small_master, small_moment, small_average,
):
    section_index = lax.axis_index("section")
    layer, core = section_index // 2, section_index % 2
    first_core = core == 0
    first_layer = layer == 0
    core_at = core.reshape(1)
    micro_count, row_count, width = block_input.shape
    ring = Ring(lax.axis_size("dp"))

    def mine(source):
        return jnp.where(first_core, source[0], source[1])

    def by_core(if_first, if_second):
        return jnp.where(first_core, if_first, if_second)

    in_rows, hidden = in_master.shape[1:]
    in_low = in_master[0].astype(BF16)
    in_blocks = jnp.stack([in_low[:, i * width : (i + 1) * width] for i in range(4)])
    down_blocks = out_master[0].astype(BF16).reshape(4, in_rows, width)
    crossed = sibling(by_core(in_blocks[2:], in_blocks[:2]))
    attn_shard = by_core(in_blocks[:2], crossed)
    up_shard = by_core(crossed, in_blocks[2:])
    down_shard = by_core(lax.ppermute(down_blocks[:2], "section", FROM_MLP), down_blocks[2:])
    small_own = small_master[0]
    small_other = sibling(small_own)
    small_attn = by_core(small_own, small_other)
    small_mlp = by_core(small_other, small_own)
    seg, row_at, col_at, valid = (mine(m) for m in (segment_ids, grid_row, grid_col, valid_slot))
    head_count = width // HD
    frequency = small_attn[6].reshape(head_count, 2, 1, HD // 2)
    spread = jnp.broadcast_to(frequency, (head_count, 2, 2, HD // 2))
    angle = (
        col_at.astype(F32)[:, None] * spread[:, 0].reshape(1, width)
        + row_at.astype(F32)[:, None] * spread[:, 1].reshape(1, width)
    )
    turn_sign = jnp.where(lax.broadcasted_iota(jnp.int32, (1, width), 1) % HD < HD // 2, -1.0, 1.0)
    cosine = jnp.cos(angle)
    sine = jnp.sin(angle) * turn_sign
    tag = lax.broadcasted_iota(jnp.int32, (1, 128), 1)
    same = seg[:, None] == tag
    query_tag = same.astype(BF16)
    key_tag = jnp.where(same & (valid[:, None] > 0), 0.0, MASKED).astype(BF16)
    lane = lax.broadcasted_iota(jnp.int32, (1, 128), 1)
    grid_pos = jnp.where(lane == 0, col_at.astype(F32)[:, None], row_at.astype(F32)[:, None])
    x0 = mine(block_input)
    cotangent = mine(out_cotangent) * valid.astype(BF16)[:, None]

    attn_walk = RingWalk(ring, attn_shard, False)
    mlp_walk = RingWalk(ring, jnp.concatenate([up_shard, down_shard]), False)
    reach = ring.size // 2
    attn_walk.hop()
    cosine, sine = meet((attn_walk,), cosine, sine)
    while attn_walk.done < reach:
        attn_walk.hop()
    attn_matrix, mlp_matrices = Matrices(ring, core_at), Matrices(ring, core_at)
    placed = attn_matrix.start(attn_walk.found[:-1])
    *attn_matrix.placed, = meet((attn_walk, mlp_walk), *placed)
    (w_attn,) = attn_matrix.finish(attn_walk.found[-1:])

    while mlp_walk.done < reach - 3:
        mlp_walk.hop()
    attn_args = (x0, small_attn, w_attn, cosine, sine, query_tag, key_tag)
    (running,) = attn_fwd(False, *attn_args, 0, 2)
    (running,) = meet((mlp_walk,), running)
    mlp_walk.hop()
    (mid0,) = attn_fwd(False, *attn_args, 2, None, running)
    (mid0,) = meet((mlp_walk,), mid0)
    mlp_walk.hop()
    meet((mlp_walk,))
    placed = mlp_matrices.start(mlp_walk.found)
    mlp_walk.hop()
    *mlp_matrices.placed, = meet((mlp_walk,), *placed)
    w_up, w_down = mlp_matrices.finish(mlp_walk.found[-1:])
    arrived = []
    piece = row_count // 2
    for low in range(0, row_count, piece):
        (top0,) = mlp_fwd(False, mid0[low : low + piece], small_mlp, w_up, w_down)
        arrived.append(lax.ppermute(top0, "section", NEXT_LAYER))
    entering = jnp.where(first_layer, x0, jnp.concatenate(arrived))

    mid, *saved = attn_fwd(True, entering, small_attn, w_attn, cosine, sine, query_tag, key_tag)
    top, z, slope = mlp_fwd(True, mid, small_mlp, w_up, w_down)

    def both_micro(attn_value, mlp_value):
        kept = by_core(attn_value, mlp_value)
        crossed = sibling(by_core(mlp_value, attn_value))
        return jnp.stack([by_core(kept, crossed), by_core(crossed, kept)])

    (back_mid,) = mlp_bwd(False, core_at, mid, cotangent, small_mlp, w_up, w_down, slope)
    (back_in,) = attn_bwd(False, entering, back_mid, small_attn, w_attn, cosine, sine, saved)
    arriving = jnp.where(first_layer, lax.ppermute(back_in, "section", PREV_LAYER), cotangent)
    outputs = both_micro(mid, top)
    arriving, outputs = tied((arriving, outputs))
    ut_attn, ut_mlp, o_t, z_t = turned_factors(entering, small_attn, mid, small_mlp, saved[5], z)

    grad_mid, mlp_rows, up_bias, up_kept, up_sent, down_kept, down_sent = mlp_bwd(
        True, core_at, mid, arriving, small_mlp, w_up, w_down, slope, ut_mlp, z_t, ring.size
    )
    met = (sibling(up_sent), sibling(down_sent))
    extra = (core_at, ut_attn, o_t, grid_pos)

    def attn_group(group, before):
        return list(
            attn_bwd(
                True, entering, grad_mid, small_attn, w_attn, cosine, sine, saved, extra, ring.size,
                group, group + 1, before, False,
            )
        )

    back = attn_group(0, None)
    *met, back[0] = tied(met + (back[0],))
    mlp_sum = RingSum(ring, joined_terms(((up_kept, met[0], True), (down_kept, met[1], False)), BIG_VMEM))
    for group in range(1, width // (4 * HD)):
        *mlp_sum.going, back[0] = tied(tuple(mlp_sum.going) + (back[0],))
        back = attn_group(group, back)
        *came, back[0] = tied(tuple(mlp_sum.hop()) + (back[0],))
        mlp_sum.add(came)
    du, attn_bias, turned, attn_kept, attn_sent = back
    *mlp_sum.going, attn_sent, du = tied(tuple(mlp_sum.going) + (attn_sent, du))
    grad_in, small_kept, small_sent = norm_bwd(
        core_at, entering, grad_mid, small_attn, du, attn_bias, turned, mlp_rows, up_bias
    )
    attn_met, small_met, grad_in = tied((sibling(attn_sent), sibling(small_sent), grad_in))
    attn_terms = joined_terms(((attn_kept, attn_met, True),), TERMS_VMEM)
    attn_sum = RingSum(ring, attn_terms, (small_kept, small_met))
    mlp_came = mlp_sum.hop()
    attn_came = attn_sum.hop()
    mlp_sum.add(mlp_came)
    waiting = tied(tuple(attn_came) + tuple(mlp_sum.going))
    attn_came, mlp_sum.going = waiting[:2], waiting[2:]
    mlp_came = mlp_sum.hop()
    attn_sum.add(attn_came)
    while attn_sum.done < reach:
        if mlp_sum.done < reach and attn_sum.done > 1:
            mlp_sum.add(mlp_came)
            waiting = tied(tuple(attn_came) + tuple(mlp_sum.going))
            attn_came, mlp_sum.going = waiting[:2], waiting[2:]
            mlp_came = mlp_sum.hop()
        if attn_sum.done > 1:
            attn_sum.add(attn_came)
        attn_came = attn_sum.hop()
    while mlp_sum.done < reach:
        mlp_sum.add(mlp_came)
        mlp_came = mlp_sum.hop()
    (mlp_share,) = mlp_sum.close(mlp_came)
    attn_share, small_sum = attn_sum.close(attn_came)
    mlp_share = mlp_share.reshape(4, in_rows, width)
    attn_share = attn_share.reshape(2, in_rows, width)
    small_grad = small_sum[:7]
    up_share, down_share = mlp_share[:2], mlp_share[2:]

    step_rate = RATE / math.sqrt(lax.axis_size("dp") * micro_count * row_count)
    down_crossed = lax.ppermute(down_share.astype(BF16), "section", FROM_ATTN).astype(F32)
    share_out = jnp.where(first_core, 0.0, jnp.concatenate([down_crossed, down_share]).reshape(4 * in_rows, width))
    out_new = advance(out_master[0], out_moment[0], out_average[0], share_out, step_rate)
    crossed = sibling(by_core(up_share, attn_share).astype(BF16))
    in_new = advance_blocks(
        core_at, attn_share, up_share, crossed, in_master[0], in_moment[0], in_average[0], step_rate
    )
    small_new = advance(small_own, small_moment[0], small_average[0], small_grad, step_rate)
    branch_bias = by_core(small_grad[5], small_grad[6])

    input_grads = both_micro(grad_in, grad_mid)
    return tuple(
        value[None]
        for value in (outputs, input_grads, *in_new, *out_new, *small_new, branch_bias)
    )


def solution(mesh):
    rows = P(None, "dp", None)
    slots = P(None, "dp")
    matrix = P("section", "dp", None)
    vectors = P("section", None, None)
    return jax.shard_map(
        on_device,
        mesh=mesh,
        in_specs=(rows,) * 2 + (slots,) * 4 + (matrix,) * 6 + (vectors,) * 3,
        out_specs=(P("section", None, "dp", None),) * 2 + (matrix,) * 6 + (vectors,) * 3 + (P("section", None),),
        check_vma=False,
    )
```
